32 devices in a mesh: pipe: 2 (over x), dp: 4 (over y, core), tensor: 4 (over z).
Axes of the slice: x: 2, y: 2, z: 4, core: 2. Of those that a mesh axis runs over, the one named last changes fastest.
Arguments:
- x_vit: bfloat16 [8, 576, 1024], P('dp', 'tensor'), may hold values from -6 to 6
- x_conv: bfloat16 [8, 1024, 1536], P('dp', None, 'tensor'), may hold values from -12 to 12
- positions: int32 [8, 576], P('dp'), may hold values from 0 to 575, each once within a row
- valid: int32 [8, 576], P('dp'), may hold values from 0 to 1, as said below
- qkv_weight: bfloat16 [2, 1024, 3, 1024], P('pipe', None, None, 'tensor'), may hold values from -0.1875 to 0.1875
- attn_weight: bfloat16 [2, 1024, 1024], P('pipe', 'tensor'), may hold values from -1 to 1
- fc_in: bfloat16 [2, 1024, 4096], P('pipe', None, 'tensor'), may hold values from -0.1875 to 0.1875
- fc_out: bfloat16 [2, 4096, 1024], P('pipe', 'tensor'), may hold values from -0.09375 to 0.09375
- vit_gains: float32 [2, 2, 1024], P('pipe'), may hold values from 0.5 to 1.5
- vit_shifts: float32 [2, 2, 1024], P('pipe'), may hold values from -3 to 3
- pw_in: bfloat16 [2, 1536, 6144], P('pipe', None, 'tensor'), may hold values from -0.15625 to 0.15625
- pw_out: bfloat16 [2, 6144, 1536], P('pipe', 'tensor'), may hold values from -0.078125 to 0.078125
- dw_kernel: float32 [2, 49, 1536], P('pipe', None, 'tensor'), may hold values from -0.875 to 0.875
- conv_gains: float32 [2, 2, 1536], P('pipe', None, 'tensor'), may hold values from 0.5 to 1.5
- conv_shift: float32 [2, 1536], P('pipe', 'tensor'), may hold values from -3 to 3
- proj_weight: bfloat16 [2, 1536, 1024], P('pipe'), may hold values from -0.15625 to 0.15625
- taps: float32 [2, 9, 1024], P('pipe'), may hold values from -2 to 2
- gate: float32 [2, 1024], P('pipe'), may hold values from -2 to 2
- dy_vit: bfloat16 [8, 576, 1024], P('dp', 'tensor'), may hold values from -6 to 6
- dy_conv: bfloat16 [8, 1024, 1536], P('dp', None, 'tensor'), may hold values from -6 to 6
Outputs:
- out_vit: bfloat16 [2, 8, 576, 1024], P('pipe', 'dp', 'tensor')
- out_conv: bfloat16 [2, 8, 1024, 1536], P('pipe', 'dp', None, 'tensor')
- grad_vit: float32 [2, 8, 576, 1024], P('pipe', 'dp', 'tensor')
- grad_conv: float32 [2, 8, 1024, 1536], P('pipe', 'dp', None, 'tensor')
- rms_vit: float32 [2, 8, 576], P('pipe', 'dp', 'tensor')
- rms_conv: float32 [2, 8, 1024], P('pipe', 'dp')
- grad_qkv: float32 [2, 1024, 3, 1024], P('pipe', 'dp', None, 'tensor')
- grad_attn: float32 [2, 1024, 1024], P('pipe', 'tensor', 'dp')
- grad_fc_in: float32 [2, 1024, 4096], P('pipe', 'dp', 'tensor')
- grad_fc_out: float32 [2, 4096, 1024], P('pipe', 'tensor', 'dp')
- grad_vit_gains: float32 [2, 2, 1024], P('pipe')
- grad_vit_shifts: float32 [2, 2, 1024], P('pipe')
- grad_pw_in: float32 [2, 1536, 6144], P('pipe', 'dp', 'tensor')
- grad_pw_out: float32 [2, 6144, 1536], P('pipe', 'tensor', 'dp')
- grad_dw: float32 [2, 49, 1536], P('pipe', None, 'tensor')
- grad_conv_gains: float32 [2, 2, 1536], P('pipe', None, 'tensor')
- grad_conv_shift: float32 [2, 1536], P('pipe', 'tensor')
- grad_proj: float32 [2, 1536, 1024], P('pipe', 'dp', 'tensor')
- grad_taps: float32 [2, 9, 1024], P('pipe')
- grad_gate: float32 [2, 1024], P('pipe')
The draws below stay inside these ranges and needn't reach their ends.
Inputs may be any that keep to these rules, and one draw needn't show every extreme that they name: Each row of positions names every one of the 576 grid cells once. The valid tokens of each image are a prefix of 288 tokens or more; in every draw some image has all 576 valid.
All inputs are finite; a program needn't handle non-finite values.
Results may differ from the reference program's by a relative error of at most 0.025.
Values may be sent and summed in bfloat16 or wider, within the bound.
No kernel may reach another device: no remote copies, remote signals or barrier semaphores. Data moves between devices by JAX's collectives and lax.ppermute only.
A program may use at most 320 MiB of HBM per device.

```python
import jax
import jax.numpy as jnp
from jax import lax

WIDTH = 1024
HEADS = 16
HEAD_DIM = 64
FF = 4096
CHANNELS = 1536
CONV_FF = 6144
GRID = 24
CGRID = 32
PATCHES = 576
CELLS = 1024
IMAGES = 8


def draw_valid(key, part):
    key = jax.random.fold_in(key, 11)
    length_key, full_key = jax.random.split(key)
    lengths = jax.random.randint(length_key, (IMAGES, 1), PATCHES // 2, PATCHES + 1)
    chosen = jax.random.randint(full_key, (), 0, IMAGES)
    lengths = jnp.where(jnp.arange(IMAGES)[:, None] == chosen, PATCHES, lengths)
    return (jnp.arange(PATCHES)[None, :] < lengths).astype(jnp.int32)


def draw_x_conv(key, part):
    key = jax.random.fold_in(key, 13)
    ramp = jnp.arange(CHANNELS).astype(jnp.float32) / max(CHANNELS - 1, 1)
    base = jax.random.truncated_normal(key, -4.0, 4.0, (IMAGES, CELLS, CHANNELS), jnp.float32)
    scale = 0.5 * jnp.power(6.0, ramp)
    return (base * scale[None, None, :]).astype(jnp.bfloat16)


def block_levels(stream_key, shape, pieces, smallest, top_value):
    factor_of = 1.0
    for axis_at, parts in pieces:
        heights = jax.random.uniform(jax.random.fold_in(jax.random.fold_in(stream_key, 6), axis_at), (parts,), jnp.float32, smallest / len(pieces), top_value / len(pieces))
        factor_of = factor_of * jnp.repeat(jnp.exp(heights), shape[axis_at] // parts).reshape((-1,) + (1,) * (len(shape) - 1 - axis_at))
    return factor_of


def gaussian(rng, dims, deviation, limit, shards=(), dtype=jnp.bfloat16):
    entries = deviation * jax.random.normal(rng, dims, jnp.float32)
    if shards:
        entries = entries * block_levels(rng, dims, shards, -0.22, 0.18)
    return jnp.clip(entries, -limit, limit).astype(dtype)


def setup_inputs(seed: int = 0) -> dict:
    arg_keys = jax.random.split(jax.random.key(seed), 21)
    x_vit = gaussian(arg_keys[0], (IMAGES, PATCHES, WIDTH), 1.0, 6.0, ((0, 4), (1, 4)))
    x_conv = draw_x_conv(jax.random.fold_in(arg_keys[20], 71), 0)
    positions = jax.vmap(lambda own: jax.random.permutation(own, PATCHES))(jax.random.split(arg_keys[2], IMAGES)).reshape((IMAGES, PATCHES)).astype(jnp.int32)
    valid = draw_valid(jax.random.fold_in(arg_keys[20], 71), 0)
    qkv_weight = gaussian(arg_keys[4], (2, WIDTH, 3, WIDTH), WIDTH ** -0.5, 0.1875, ((0, 2), (3, 4)))
    attn_weight = gaussian(arg_keys[5], (2, WIDTH, WIDTH), (max(WIDTH // 24, 1)) ** -0.5, 1.0, ((0, 2), (1, 4)))
    fc_in = gaussian(arg_keys[6], (2, WIDTH, FF), WIDTH ** -0.5, 0.1875, ((0, 2), (2, 4)))
    fc_out = gaussian(arg_keys[7], (2, FF, WIDTH), FF ** -0.5, 0.09375, ((0, 2), (1, 4)))
    vit_gains = jnp.clip(1.0 + 0.1 * jax.random.normal(arg_keys[8], (2, 2, WIDTH), jnp.float32), 0.5, 1.5)
    vit_shifts = gaussian(arg_keys[9], (2, 2, WIDTH), 0.5, 3.0, ((0, 2),), jnp.float32)
    pw_in = gaussian(arg_keys[10], (2, CHANNELS, CONV_FF), CHANNELS ** -0.5, 0.15625, ((0, 2), (2, 4)))
    pw_out = gaussian(arg_keys[11], (2, CONV_FF, CHANNELS), CONV_FF ** -0.5, 0.078125, ((0, 2), (1, 4)))
    dw_kernel = gaussian(arg_keys[12], (2, 49, CHANNELS), 49 ** -0.5, 0.875, ((0, 2), (2, 4)), jnp.float32)
    conv_gains = jnp.clip(1.0 + 0.1 * jax.random.normal(arg_keys[13], (2, 2, CHANNELS), jnp.float32), 0.5, 1.5)
    conv_shift = gaussian(arg_keys[14], (2, CHANNELS), 0.5, 3.0, ((0, 2), (1, 4)), jnp.float32)
    proj_weight = gaussian(arg_keys[15], (2, CHANNELS, WIDTH), CHANNELS ** -0.5, 0.15625, ((0, 2),))
    taps = gaussian(arg_keys[16], (2, 9, WIDTH), 9 ** -0.5, 2.0, ((0, 2),), jnp.float32)
    gate = jnp.clip(jax.random.uniform(arg_keys[17], (2, WIDTH), jnp.float32, -2.0, 2.0) * block_levels(arg_keys[17], (2, WIDTH), ((0, 2),), -0.4, 0.0), -2.0, 2.0)
    dy_vit = gaussian(arg_keys[18], (IMAGES, PATCHES, WIDTH), 1.0, 6.0, ((0, 4), (1, 4)))
    dy_conv = gaussian(arg_keys[19], (IMAGES, CELLS, CHANNELS), 1.0, 6.0, ((0, 4), (2, 4)))
    return dict(x_vit=x_vit, x_conv=x_conv, positions=positions, valid=valid, qkv_weight=qkv_weight, attn_weight=attn_weight, fc_in=fc_in, fc_out=fc_out, vit_gains=vit_gains, vit_shifts=vit_shifts, pw_in=pw_in, pw_out=pw_out, dw_kernel=dw_kernel, conv_gains=conv_gains, conv_shift=conv_shift, proj_weight=proj_weight, taps=taps, gate=gate, dy_vit=dy_vit, dy_conv=dy_conv)


@jax.custom_vjp
def low(v):
    return lax.optimization_barrier(v.astype(jnp.bfloat16)).astype(jnp.float32)

@jax.custom_vjp
def low_back(v):
    return v

def low_keep(v):
    return (low(v), None)

def low_pass(kept, grad):
    return (grad,)

def back_keep(v):
    return (v, None)

def back_low(kept, grad):
    return (low(grad),)
low.defvjp(low_keep, low_pass)
low_back.defvjp(back_keep, back_low)

def matmul(left, right):
    return jnp.dot(left, right, precision=lax.Precision.HIGHEST, preferred_element_type=jnp.float32)

def layer_norm(values, gains, shifts, epsilon):
    centred = values - lax.optimization_barrier(jnp.mean(values, axis=-1, keepdims=True))
    variance = lax.optimization_barrier(jnp.mean(centred * centred, axis=-1, keepdims=True))
    return centred * lax.rsqrt(variance + epsilon) * gains + shifts

def gelu_exact(values):
    return jax.nn.gelu(values, approximate=False)

def depthwise(grid, kernel, side_taps):
    half_side = side_taps // 2
    extent = grid.shape[0]
    padded = jnp.pad(grid, ((half_side, half_side), (half_side, half_side), (0, 0)))
    summed = jnp.zeros(grid.shape, jnp.float32)
    for row_tap in range(side_taps):
        for col_tap in range(side_taps):
            summed = summed + padded[row_tap:row_tap + extent, col_tap:col_tap + extent, :] * kernel[row_tap * side_taps + col_tap]
    return summed

def pool_matrix(coarse, fine):
    row_index = jnp.arange(coarse)[:, None]
    col_index = jnp.arange(fine)[None, :]
    starts = row_index * fine // coarse
    stops = -(-(row_index + 1) * fine // coarse)
    inside = (col_index >= starts) & (col_index < stops)
    return jnp.where(inside, 1.0 / (stops - starts).astype(jnp.float32), 0.0).astype(jnp.float32)

def one_layer(stream, feature, positions_one, valid_one, weights):
    qkv_w, attn_w, fc_in_w, fc_out_w, vit_gain, vit_shift, pw_in_w, pw_out_w, dw_w, conv_gain, conv_shift_w, proj_w, taps_w, gate_w = weights
    mixed = depthwise(feature.reshape(CGRID, CGRID, CHANNELS), dw_w, 7).reshape(CELLS, CHANNELS)
    normed = low(layer_norm(mixed, conv_gain[0], conv_shift_w, 1e-06))
    hidden = low(gelu_exact(low_back(matmul(normed, pw_in_w))))
    feature_out = feature + conv_gain[1] * low_back(matmul(hidden, pw_out_w))
    pooling = pool_matrix(GRID, CGRID)
    pooled = jnp.einsum('ai,bj,ijc->abc', pooling, pooling, feature_out.reshape(CGRID, CGRID, CHANNELS), precision=lax.Precision.HIGHEST)
    pooled = low(pooled.reshape(PATCHES, CHANNELS))
    adapted = low_back(matmul(pooled, proj_w))
    spread = depthwise(adapted.reshape(GRID, GRID, WIDTH), taps_w, 3).reshape(PATCHES, WIDTH)
    stream_in = stream + jnp.take(jnp.tanh(gate_w) * spread, positions_one, axis=0)
    normed_a = low(layer_norm(stream_in, vit_gain[0], vit_shift[0], 1e-05))
    project = matmul(normed_a, qkv_w.reshape(WIDTH, 3 * WIDTH)).reshape(PATCHES, 3, HEADS, HEAD_DIM)
    query = low_back(low(project[:, 0]))
    keys_all = low_back(low(project[:, 1]))
    values_all = low_back(low(project[:, 2]))
    scores = low_back(jnp.einsum('qhd,khd->hqk', query, keys_all, precision=lax.Precision.HIGHEST) * HEAD_DIM ** (-0.5))
    scores = jnp.where(valid_one[None, None, :] > 0, scores, -1000000000.0)
    probs = low(jax.nn.softmax(scores, axis=-1))
    attended = jnp.einsum('hqk,khd->qhd', probs, values_all, precision=lax.Precision.HIGHEST).reshape(PATCHES, WIDTH)
    attended = low_back(low(attended))
    stream_mid = stream_in + low_back(matmul(attended, attn_w))
    normed_b = low(layer_norm(stream_mid, vit_gain[1], vit_shift[1], 1e-05))
    hidden_b = low(gelu_exact(low_back(matmul(normed_b, fc_in_w))))
    stream_out = stream_mid + low_back(matmul(hidden_b, fc_out_w))
    return (stream_out, feature_out)

def both_layers(weights, stream, feature, bump_stream, bump_feature, positions_one, valid_one):
    stream_one, feature_one = one_layer(stream, feature, positions_one, valid_one, tuple((member[0] for member in weights)))
    stream_next = low_back(low(stream_one)) + bump_stream
    feature_next = low_back(low(feature_one)) + bump_feature
    stream_two, feature_two = one_layer(stream_next, feature_next, positions_one, valid_one, tuple((member[1] for member in weights)))
    return ((stream_two, feature_two), (stream_one, feature_one))

def row_root(values):
    return jnp.sqrt(lax.optimization_barrier(jnp.mean(values * values, axis=-1)))

def reference(x_vit, x_conv, positions, valid, qkv_weight, attn_weight, fc_in, fc_out, vit_gains, vit_shifts, pw_in, pw_out, dw_kernel, conv_gains, conv_shift, proj_weight, taps, gate, dy_vit, dy_conv):
    weights = tuple((member.astype(jnp.float32) for member in (qkv_weight, attn_weight, fc_in, fc_out, vit_gains, vit_shifts, pw_in, pw_out, dw_kernel, conv_gains, conv_shift, proj_weight, taps, gate)))

    def per_image(running, sample):
        stream, feature, positions_one, valid_one, cot_stream, cot_feature = sample

        def forward(weights_in, stream_in, feature_in, bump_stream, bump_feature):
            return both_layers(weights_in, stream_in, feature_in, bump_stream, bump_feature, positions_one, valid_one)
        outputs, pullback, firsts = jax.vjp(forward, weights, stream, feature, jnp.zeros_like(stream), jnp.zeros_like(feature), has_aux=True)
        gradients = pullback((cot_stream, cot_feature))
        running = tuple((former + latter for former, latter in zip(running, gradients[0])))
        stacked_vit = jnp.stack([firsts[0], outputs[0]]).astype(jnp.bfloat16)
        stacked_conv = jnp.stack([firsts[1], outputs[1]]).astype(jnp.bfloat16)
        stacked_grad_vit = jnp.stack([gradients[1], gradients[3]])
        stacked_grad_conv = jnp.stack([gradients[2], gradients[4]])
        measure_vit = jnp.stack([row_root(firsts[0]), row_root(outputs[0])])
        measure_conv = jnp.stack([row_root(firsts[1]), row_root(outputs[1])])
        return (running, (stacked_vit, stacked_conv, stacked_grad_vit, stacked_grad_conv, measure_vit, measure_conv))
    start_grads = tuple((jnp.zeros(member.shape, jnp.float32) for member in weights))
    totals, per_item = lax.scan(per_image, start_grads, (x_vit.astype(jnp.float32), x_conv.astype(jnp.float32), positions, valid, dy_vit.astype(jnp.float32), dy_conv.astype(jnp.float32)))
    reordered = tuple((jnp.swapaxes(member, 0, 1) for member in per_item))
    return (reordered[0], reordered[1], reordered[2], reordered[3], reordered[4], reordered[5], totals[0], totals[1], totals[2], totals[3], totals[4], totals[5], totals[6], totals[7], totals[8], totals[9], totals[10], totals[11], totals[12], totals[13])
```

```python
import math

import jax
import jax.numpy as jnp
from jax import lax
from jax.sharding import PartitionSpec as P

HEAD_DIM = 64


def for_sending(array):
    return jax.tree.map(lambda a: a.astype(jnp.bfloat16) if a.dtype == jnp.float32 else a, array)


def traded(array, axis, bit):
    return lax.ppermute(array, axis, [(i, i ^ bit) for i in range(lax.axis_size(axis))])


def bits_of(axis):
    return [1 << k for k in range((lax.axis_size(axis) - 1).bit_length())]


def total_over(values, axis):
    for bit in bits_of(axis):
        values = values + traded(values, axis, bit)
    return values


def layer_pair(own):
    flat = own.reshape((2, own.shape[0] // 2) + own.shape[1:])
    odd = lax.axis_index("dp") % 2
    sent = lax.dynamic_index_in_dim(flat, odd, 0, keepdims=False)
    got = traded(sent, "pipe", 1)
    rest = traded(got, "dp", 1)
    first_half = jnp.where(odd == 0, got, rest)
    second_half = jnp.where(odd == 0, rest, got)
    other = jnp.concatenate([first_half, second_half], 0)
    first = lax.axis_index("pipe") == 0
    return (jnp.where(first, own, other), jnp.where(first, other, own))


def gelu_and_slope(values):
    cumulative = 0.5 * (1.0 + lax.erf(values * (1.0 / math.sqrt(2.0))))
    density = jnp.exp(-0.5 * values * values) * (1.0 / math.sqrt(2.0 * math.pi))
    return (
        (values * cumulative).astype(jnp.bfloat16),
        (cumulative + values * density).astype(jnp.bfloat16),
    )


def windows(coarse, fine):
    starts = [row * fine // coarse for row in range(coarse)]
    stops = [-(-(row + 1) * fine // coarse) for row in range(coarse)]
    return (starts, stops)


def pool_axis(grid, axis, coarse):
    starts, stops = windows(coarse, grid.shape[axis])
    slabs = []
    for start, stop in zip(starts, stops):
        slab = lax.slice_in_dim(grid, start, stop, axis=axis)
        slabs.append(jnp.sum(slab, axis=axis, keepdims=True) * (1.0 / (stop - start)))
    return jnp.concatenate(slabs, axis)


def unpool_axis(grid, axis, fine):
    starts, stops = windows(grid.shape[axis], fine)
    slabs = []
    for place in range(fine):
        parts = [
            lax.slice_in_dim(grid, row, row + 1, axis=axis) * (1.0 / (stop - start))
            for row, (start, stop) in enumerate(zip(starts, stops))
            if start <= place < stop
        ]
        slabs.append(sum(parts[1:], parts[0]))
    return jnp.concatenate(slabs, axis)


def pool(grid, coarse):
    return pool_axis(pool_axis(grid, 1, coarse), 2, coarse)


def unpool(grid, fine):
    return unpool_axis(unpool_axis(grid, 2, fine), 1, fine)


def depthwise(grid, kernel, side_taps):
    half_side = side_taps // 2
    extent = grid.shape[1]
    padded = jnp.pad(grid, ((0, 0), (half_side, half_side), (half_side, half_side), (0, 0)))
    summed = jnp.zeros(grid.shape, jnp.float32)
    for row_tap in range(side_taps):
        for col_tap in range(side_taps):
            summed = (
                summed
                + padded[:, row_tap : row_tap + extent, col_tap : col_tap + extent, :]
                * kernel[row_tap * side_taps + col_tap]
            )
    return summed


def depthwise_taps(grid, upstream, side_taps):
    half_side = side_taps // 2
    extent = grid.shape[1]
    padded = jnp.pad(grid, ((0, 0), (half_side, half_side), (half_side, half_side), (0, 0)))
    rows_out = []
    for row_tap in range(side_taps):
        for col_tap in range(side_taps):
            window = padded[:, row_tap : row_tap + extent, col_tap : col_tap + extent, :]
            rows_out.append(jnp.sum(window * upstream, axis=(0, 1, 2)))
    return jnp.stack(rows_out, 0)


def norm_rows(values, epsilon):
    centred = values - jnp.mean(values, -1, keepdims=True)
    inverse = lax.rsqrt(jnp.mean(centred * centred, -1, keepdims=True) + epsilon)
    return (centred * inverse, inverse)


def norm_back(upstream, scaled, inverse, gains):
    weighted = upstream * gains
    return inverse * (
        weighted
        - jnp.mean(weighted, -1, keepdims=True)
        - scaled * jnp.mean(weighted * scaled, -1, keepdims=True)
    )


def inner(left, right):
    leading = tuple(range(left.ndim - 1))
    return lax.dot_general(
        left, right, ((leading, leading), ((), ())), preferred_element_type=jnp.float32
    )


def along(left, right):
    return lax.dot_general(
        left, right, (((left.ndim - 1,), (1,)), ((), ())), preferred_element_type=jnp.float32
    )


def own_block(values, count, axis):
    return lax.dynamic_slice_in_dim(values, lax.axis_index("tensor") * count, count, axis)


def widen(values, whole, axis):
    shape = list(values.shape)
    shape[axis] = whole
    empty = jnp.zeros(tuple(shape), jnp.float32)
    return lax.dynamic_update_slice_in_dim(
        empty, values, lax.axis_index("tensor") * values.shape[axis], axis
    )


def gather_tokens(values):
    return lax.all_gather(values, "tensor", axis=1, tiled=True)


def scatter_tokens(values):
    return lax.psum_scatter(
        values.astype(jnp.bfloat16), "tensor", scatter_dimension=1, tiled=True
    ).astype(jnp.float32)


def gather_channels(values):
    return lax.all_gather(values, "tensor", axis=1, tiled=True)


def scatter_channels(values):
    return lax.psum_scatter(
        values.astype(jnp.bfloat16), "tensor", scatter_dimension=1, tiled=True
    ).astype(jnp.float32)


def channel_total(first_part, second_part):
    both = total_over(jnp.stack([first_part, second_part]), "tensor")
    return (both[0], both[1])


def attention_scores(query, keys_all, key_mask, score_scale):
    scores = (
        jnp.einsum("bqhd,bkhd->bhqk", query, keys_all, preferred_element_type=jnp.float32)
        * score_scale
    )
    return jnp.where(key_mask[:, None, None, :] > 0, scores, -1000000000.0)


def section_forward(stream, feature, places, key_mask, params):
    (
        qkv_w,
        attn_w,
        fc_in_w,
        fc_out_w,
        vit_gain,
        vit_shift,
        pw_in_w,
        pw_out_w,
        dw_w,
        conv_gain,
        conv_shift_w,
        proj_w,
        taps_w,
        gate_w,
    ) = params
    images, local_tokens, model_width = stream.shape
    conv_cells, local_channels = (feature.shape[1], feature.shape[2])
    conv_side = math.isqrt(conv_cells)
    tokens = local_tokens * lax.axis_size("tensor")
    vit_side = math.isqrt(tokens)
    channels = local_channels * lax.axis_size("tensor")
    local_width = attn_w.shape[0]
    heads_here = local_width // HEAD_DIM
    score_scale = HEAD_DIM ** (-0.5)
    feature_grid = feature.reshape(images, conv_side, conv_side, local_channels)
    mixed = depthwise(feature_grid, dw_w, 7).reshape(images * conv_cells, local_channels)
    first_sum, second_sum = channel_total(jnp.sum(mixed, -1), jnp.sum(mixed * mixed, -1))
    centre = first_sum / channels
    inverse = lax.rsqrt(second_sum / channels - centre * centre + 1e-06)
    scaled = (mixed - centre[:, None]) * inverse[:, None]
    normed_full = gather_channels((scaled * conv_gain[0] + conv_shift_w).astype(jnp.bfloat16))
    expand = jnp.dot(normed_full, pw_in_w, preferred_element_type=jnp.float32)
    hidden, slope = gelu_and_slope(expand)
    branch = scatter_channels(jnp.dot(hidden, pw_out_w, preferred_element_type=jnp.float32))
    feature_out = feature.reshape(images * conv_cells, local_channels) + conv_gain[1] * branch
    pooled = pool(feature_out.reshape(images, conv_side, conv_side, local_channels), vit_side)
    pooled_full = lax.all_gather(
        pooled.reshape(images * tokens, local_channels).astype(jnp.bfloat16),
        "tensor",
        axis=1,
        tiled=True,
    )
    proj_cols = proj_w
    taps_cols = taps_w
    gate_cols = gate_w
    adapted = jnp.dot(pooled_full, proj_cols, preferred_element_type=jnp.float32).reshape(
        images, vit_side, vit_side, local_width
    )
    spread = depthwise(adapted, taps_cols, 3).reshape(images, tokens, local_width)
    picked = jnp.tanh(gate_cols) * jnp.take_along_axis(spread, places[:, :, None], axis=1)
    moved = lax.all_to_all(
        picked.astype(jnp.bfloat16), "tensor", split_axis=1, concat_axis=2, tiled=True
    ).astype(picked.dtype)
    stream_in = stream + moved
    scaled_a, inverse_a = norm_rows(stream_in, 1e-05)
    normed_a = gather_tokens((scaled_a * vit_gain[0] + vit_shift[0]).astype(jnp.bfloat16))
    project = jnp.dot(
        normed_a, qkv_w.reshape(model_width, 3 * local_width), preferred_element_type=jnp.float32
    )
    project = project.astype(jnp.bfloat16).reshape(images, tokens, 3, heads_here, HEAD_DIM)
    query = project[:, :, 0]
    keys_all = project[:, :, 1]
    values_all = project[:, :, 2]
    scores = attention_scores(query, keys_all, key_mask, score_scale)
    highest = jnp.max(scores, -1, keepdims=True)
    raised = jnp.exp(scores - highest)
    totals = jnp.sum(raised, -1, keepdims=True)
    probs = (raised / totals).astype(jnp.bfloat16)
    log_total = highest + jnp.log(totals)
    attended = jnp.einsum("bhqk,bkhd->bqhd", probs, values_all, preferred_element_type=jnp.float32)
    attended = attended.astype(jnp.bfloat16).reshape(images, tokens, local_width)
    stream_mid = stream_in + scatter_tokens(
        jnp.dot(attended, attn_w, preferred_element_type=jnp.float32)
    )
    scaled_b, inverse_b = norm_rows(stream_mid, 1e-05)
    normed_b = gather_tokens((scaled_b * vit_gain[1] + vit_shift[1]).astype(jnp.bfloat16))
    expand_b = jnp.dot(normed_b, fc_in_w, preferred_element_type=jnp.float32)
    hidden_b, slope_b = gelu_and_slope(expand_b)
    stream_out = stream_mid + scatter_tokens(
        jnp.dot(hidden_b, fc_out_w, preferred_element_type=jnp.float32)
    )
    vit_measure = jnp.sqrt(jnp.mean(stream_out * stream_out, -1))
    conv_rows = feature_out.reshape(images, conv_cells, local_channels)
    conv_square = total_over(jnp.sum(conv_rows * conv_rows, -1), "tensor")
    conv_measure = jnp.sqrt(conv_square / channels)
    kept_values = dict(
        feature=feature_grid,
        scaled=scaled,
        inverse=inverse,
        normed_full=normed_full,
        slope=slope,
        hidden=hidden,
        branch=branch,
        pooled_full=pooled_full,
        adapted=adapted,
        spread=spread,
        places=places,
        key_mask=key_mask,
        scaled_a=scaled_a,
        inverse_a=inverse_a,
        normed_a=normed_a,
        query=query,
        keys_all=keys_all,
        values_all=values_all,
        log_total=log_total,
        attended=attended,
        scaled_b=scaled_b,
        inverse_b=inverse_b,
        normed_b=normed_b,
        slope_b=slope_b,
        hidden_b=hidden_b,
    )
    return (stream_out, conv_rows, (vit_measure, conv_measure), kept_values)


def section_backward(grad_stream, grad_feature, kept_values, params):
    (
        qkv_w,
        attn_w,
        fc_in_w,
        fc_out_w,
        vit_gain,
        vit_shift,
        pw_in_w,
        pw_out_w,
        dw_w,
        conv_gain,
        conv_shift_w,
        proj_w,
        taps_w,
        gate_w,
    ) = params
    images, local_tokens, model_width = grad_stream.shape
    conv_cells, local_channels = (grad_feature.shape[1], grad_feature.shape[2])
    conv_side = math.isqrt(conv_cells)
    tokens = local_tokens * lax.axis_size("tensor")
    vit_side = math.isqrt(tokens)
    channels = local_channels * lax.axis_size("tensor")
    local_width = attn_w.shape[0]
    heads_here = local_width // HEAD_DIM
    score_scale = HEAD_DIM ** (-0.5)
    grad_full = gather_tokens(grad_stream.astype(jnp.bfloat16))
    grad_fc_out = inner(kept_values["hidden_b"], grad_full)
    grad_expand_b = (along(grad_full, fc_out_w) * kept_values["slope_b"].astype(jnp.float32)).astype(
        jnp.bfloat16
    )
    grad_fc_in = inner(kept_values["normed_b"], grad_expand_b)
    grad_normed_b = scatter_tokens(along(grad_expand_b, fc_in_w))
    gain_second = jnp.sum(grad_normed_b * kept_values["scaled_b"], axis=(0, 1))
    shift_second = jnp.sum(grad_normed_b, axis=(0, 1))
    grad_mid = grad_stream + norm_back(
        grad_normed_b, kept_values["scaled_b"], kept_values["inverse_b"], vit_gain[1]
    )
    grad_mid_full = gather_tokens(grad_mid.astype(jnp.bfloat16))
    grad_attn = inner(kept_values["attended"], grad_mid_full)
    grad_attended = (
        along(grad_mid_full, attn_w)
        .astype(jnp.bfloat16)
        .reshape(images, tokens, heads_here, HEAD_DIM)
    )
    query = kept_values["query"]
    keys_all = kept_values["keys_all"]
    scores = attention_scores(query, keys_all, kept_values["key_mask"], score_scale)
    exact = jnp.exp(scores - kept_values["log_total"])
    rounded = exact.astype(jnp.bfloat16)
    grad_values = jnp.einsum(
        "bhqk,bqhd->bkhd", rounded, grad_attended, preferred_element_type=jnp.float32
    )
    grad_probs = jnp.einsum(
        "bqhd,bkhd->bhqk",
        grad_attended,
        kept_values["values_all"],
        preferred_element_type=jnp.float32,
    )
    grad_scores = (exact * (grad_probs - jnp.sum(grad_probs * exact, -1, keepdims=True))).astype(
        jnp.bfloat16
    )
    grad_query = (
        jnp.einsum("bhqk,bkhd->bqhd", grad_scores, keys_all, preferred_element_type=jnp.float32)
        * score_scale
    )
    grad_keys = (
        jnp.einsum("bhqk,bqhd->bkhd", grad_scores, query, preferred_element_type=jnp.float32)
        * score_scale
    )
    grad_project = (
        jnp.stack([grad_query, grad_keys, grad_values], 2)
        .astype(jnp.bfloat16)
        .reshape(images, tokens, 3 * local_width)
    )
    grad_qkv = inner(kept_values["normed_a"], grad_project).reshape(model_width, 3, local_width)
    grad_normed_a = scatter_tokens(along(grad_project, qkv_w.reshape(model_width, 3 * local_width)))
    gain_first = jnp.sum(grad_normed_a * kept_values["scaled_a"], axis=(0, 1))
    shift_first = jnp.sum(grad_normed_a, axis=(0, 1))
    grad_in = grad_mid + norm_back(
        grad_normed_a, kept_values["scaled_a"], kept_values["inverse_a"], vit_gain[0]
    )
    grad_cols = lax.all_to_all(
        for_sending(grad_in), "tensor", split_axis=2, concat_axis=1, tiled=True
    ).astype(grad_in.dtype)
    order = jnp.argsort(kept_values["places"], axis=1)
    grad_placed = jnp.take_along_axis(grad_cols, order[:, :, None], axis=1)
    proj_cols = proj_w
    taps_cols = taps_w
    gate_value = jnp.tanh(gate_w)
    grad_gate = jnp.sum(grad_placed * kept_values["spread"], axis=(0, 1)) * (
        1.0 - gate_value * gate_value
    )
    grad_spread = (grad_placed * gate_value).reshape(images, vit_side, vit_side, local_width)
    grad_taps = depthwise_taps(kept_values["adapted"], grad_spread, 3)
    grad_adapted = (
        depthwise(grad_spread, taps_cols[::-1], 3)
        .reshape(images * tokens, local_width)
        .astype(jnp.bfloat16)
    )
    grad_proj = inner(kept_values["pooled_full"], grad_adapted)
    grad_pooled = lax.psum_scatter(
        along(grad_adapted, proj_cols).astype(jnp.bfloat16),
        "tensor",
        scatter_dimension=1,
        tiled=True,
    ).astype(jnp.float32)
    grad_pooled = grad_pooled.reshape(images, vit_side, vit_side, local_channels)
    unpooled = unpool(grad_pooled, conv_side)
    grad_out_rows = (
        grad_feature.reshape(images, conv_side, conv_side, local_channels) + unpooled
    ).reshape(images * conv_cells, local_channels)
    grad_scale = jnp.sum(grad_out_rows * kept_values["branch"], 0)
    grad_branch = gather_channels((grad_out_rows * conv_gain[1]).astype(jnp.bfloat16))
    grad_pw_out = inner(kept_values["hidden"], grad_branch)
    grad_expand = (along(grad_branch, pw_out_w) * kept_values["slope"].astype(jnp.float32)).astype(
        jnp.bfloat16
    )
    grad_pw_in = inner(kept_values["normed_full"], grad_expand)
    grad_normed = scatter_channels(along(grad_expand, pw_in_w))
    scaled = kept_values["scaled"]
    grad_gain = jnp.sum(grad_normed * scaled, 0)
    grad_shift = jnp.sum(grad_normed, 0)
    weighted = grad_normed * conv_gain[0]
    first_sum, second_sum = channel_total(jnp.sum(weighted, -1), jnp.sum(weighted * scaled, -1))
    grad_mixed = kept_values["inverse"][:, None] * (
        weighted - first_sum[:, None] / channels - scaled * (second_sum[:, None] / channels)
    )
    grad_grid = grad_mixed.reshape(images, conv_side, conv_side, local_channels)
    grad_dw = depthwise_taps(kept_values["feature"], grad_grid, 7)
    grad_feature_in = grad_out_rows + depthwise(grad_grid, dw_w[::-1], 7).reshape(
        images * conv_cells, local_channels
    )
    large_parts = (grad_qkv, grad_attn, grad_fc_in, grad_fc_out, grad_pw_in, grad_pw_out, grad_proj)
    small_parts = (
        grad_dw,
        jnp.stack([grad_gain, grad_scale]),
        grad_shift[None],
        grad_taps,
        grad_gate[None],
    )
    norm_parts = (jnp.stack([gain_first, gain_second]), jnp.stack([shift_first, shift_second]))
    return (
        grad_in,
        grad_feature_in.reshape(images, conv_cells, local_channels),
        large_parts,
        small_parts,
        norm_parts,
    )


def own_share(partial, axis, keep_layer):
    count = lax.axis_size("dp")
    index = lax.axis_index("dp")
    shape = partial.shape
    block = shape[axis] // count
    blocks = partial.reshape(shape[:axis] + (count, block) + shape[axis + 1 :])
    for bit in bits_of("dp"):
        left = blocks.shape[axis] // 2
        blocks = blocks.reshape(blocks.shape[:axis] + (left, 2) + blocks.shape[axis + 1 :])
        mine = (index // bit) % 2
        kept = lax.dynamic_index_in_dim(blocks, mine, axis + 1, keepdims=False)
        sent = lax.dynamic_index_in_dim(blocks, 1 - mine, axis + 1, keepdims=False)
        blocks = kept + traded(sent.astype(jnp.bfloat16), "dp", bit).astype(jnp.float32)
    blocks = jnp.squeeze(blocks, axis)
    arrived = lax.ppermute(blocks.astype(jnp.bfloat16), "pipe", [(1 - keep_layer, keep_layer)])
    return blocks + arrived.astype(jnp.float32)


def body(
    x_vit,
    x_conv,
    positions,
    valid,
    qkv_weight,
    attn_weight,
    fc_in,
    fc_out,
    vit_gains,
    vit_shifts,
    pw_in,
    pw_out,
    dw_kernel,
    conv_gains,
    conv_shift,
    proj_weight,
    taps,
    gate,
    dy_vit,
    dy_conv,
):
    pipe_index = lax.axis_index("pipe")
    first_section = pipe_index == 0
    here = x_vit.shape[0] // lax.axis_size("pipe")
    local_width = attn_weight.shape[1]

    def select(former, latter):
        return jnp.where(first_section, former, latter)

    def portion(source):
        return lax.dynamic_slice_in_dim(source, pipe_index * here, here, 0)

    weights = dict(
        dw=dw_kernel[0],
        gain=conv_gains[0],
        shift=conv_shift,
        pw_in=pw_in[0],
        pw_out=pw_out[0],
        proj=own_block(proj_weight[0], local_width, 1),
        taps=own_block(taps[0], local_width, 1),
        gate=own_block(gate, local_width, 1),
        vit_gain=vit_gains[0],
        vit_shift=vit_shifts[0],
        qkv=qkv_weight[0],
        attn=attn_weight[0],
        fc_in=fc_in[0],
        fc_out=fc_out[0],
    )
    small = ("dw", "gain", "shift", "taps", "gate", "vit_gain", "vit_shift")
    swapped = {}
    for name in small:
        other = traded(weights[name], "pipe", 1)
        swapped[name] = (select(weights[name], other), select(other, weights[name]))
    for name in ("pw_in", "pw_out", "proj", "qkv", "attn", "fc_in", "fc_out"):
        swapped[name] = layer_pair(weights[name])

    def params_of(layer):
        return tuple(
            swapped[name][layer][0] if name in ("shift", "gate") else swapped[name][layer]
            for name in (
                "qkv",
                "attn",
                "fc_in",
                "fc_out",
                "vit_gain",
                "vit_shift",
                "pw_in",
                "pw_out",
                "dw",
                "gain",
                "shift",
                "proj",
                "taps",
                "gate",
            )
        )

    places = portion(positions)
    key_mask = portion(valid)
    stream = portion(x_vit)
    feature = portion(x_conv)
    outs = []
    kept_list = []
    for layer in range(2):
        stream_out, feature_out, measure, kept_values = section_forward(
            stream.astype(jnp.float32), feature.astype(jnp.float32), places, key_mask, params_of(layer)
        )
        stream = stream_out.astype(jnp.bfloat16)
        feature = feature_out.astype(jnp.bfloat16)
        outs.append([stream, feature, measure[0], measure[1]])
        kept_list.append(kept_values)
    grad_stream = portion(dy_vit)
    grad_feature = portion(dy_conv)
    large = [None, None]
    small_sums = [None, None]
    norm_sums = [None, None]
    for layer in (1, 0):
        grad_stream_in, grad_feature_in, large_parts, small_parts, norm_parts = section_backward(
            grad_stream.astype(jnp.float32),
            grad_feature.astype(jnp.float32),
            kept_list[layer],
            params_of(layer),
        )
        grad_stream = grad_stream_in.astype(jnp.bfloat16)
        grad_feature = grad_feature_in.astype(jnp.bfloat16)
        outs[layer] += [grad_stream_in, grad_feature_in]
        large[layer] = [
            own_share(member, axis, layer)
            for member, axis in zip(large_parts, (0, 1, 0, 1, 0, 1, 0))
        ]
        small_sums[layer] = small_parts
        norm_sums[layer] = norm_parts

    def over_images(pair):
        kept = select(pair[0], pair[1])
        sent = select(pair[1], pair[0])
        return total_over(kept + traded(sent, "pipe", 1), "dp")

    model_width = vit_gains.shape[2]
    column_sums = over_images([jnp.concatenate([part[0], part[1], part[2]], 0) for part in small_sums])
    token_sums = over_images(
        [
            jnp.concatenate(
                [
                    widen(part[3], model_width, 1),
                    widen(part[4], model_width, 1),
                    norm[0],
                    norm[1],
                ],
                0,
            )
            for part, norm in zip(small_sums, norm_sums)
        ]
    )
    token_sums = total_over(token_sums, "tensor")
    large_own = [select(former, latter) for former, latter in zip(large[0], large[1])]
    tap_count = dw_kernel.shape[1]
    side = taps.shape[1]

    def both_images(member):
        mine, theirs = (select(outs[0][member], outs[1][member]), select(outs[1][member], outs[0][member]))
        sent = theirs if member in (2, 3) else for_sending(theirs)
        got = traded(sent, "pipe", 1).astype(mine.dtype)
        return jnp.concatenate([select(mine, got), select(got, mine)], 0)[None]

    out_vit, out_conv, rms_vit, rms_conv, grad_vit, grad_conv = (
        both_images(member) for member in range(6)
    )
    return (
        out_vit,
        out_conv,
        grad_vit,
        grad_conv,
        rms_vit,
        rms_conv,
        large_own[0][None],
        large_own[1][None],
        large_own[2][None],
        large_own[3][None],
        token_sums[side + 1 : side + 3][None],
        token_sums[side + 3 : side + 5][None],
        large_own[4][None],
        large_own[5][None],
        column_sums[:tap_count][None],
        column_sums[tap_count : tap_count + 2][None],
        column_sums[tap_count + 2 :],
        large_own[6][None],
        token_sums[:side][None],
        token_sums[side][None],
    )


def solution(mesh):
    return jax.shard_map(
        body,
        mesh=mesh,
        in_specs=(
            P("dp", "tensor", None),
            P("dp", None, "tensor"),
            P("dp", None),
            P("dp", None),
            P("pipe", None, None, "tensor"),
            P("pipe", "tensor", None),
            P("pipe", None, "tensor"),
            P("pipe", "tensor", None),
            P("pipe", None, None),
            P("pipe", None, None),
            P("pipe", None, "tensor"),
            P("pipe", "tensor", None),
            P("pipe", None, "tensor"),
            P("pipe", None, "tensor"),
            P("pipe", "tensor"),
            P("pipe", None, None),
            P("pipe", None, None),
            P("pipe", None),
            P("dp", "tensor", None),
            P("dp", None, "tensor"),
        ),
        out_specs=(
            P("pipe", "dp", "tensor", None),
            P("pipe", "dp", None, "tensor"),
            P("pipe", "dp", "tensor", None),
            P("pipe", "dp", None, "tensor"),
            P("pipe", "dp", "tensor"),
            P("pipe", "dp", None),
            P("pipe", "dp", None, "tensor"),
            P("pipe", "tensor", "dp"),
            P("pipe", "dp", "tensor"),
            P("pipe", "tensor", "dp"),
            P("pipe", None, None),
            P("pipe", None, None),
            P("pipe", "dp", "tensor"),
            P("pipe", "tensor", "dp"),
            P("pipe", None, "tensor"),
            P("pipe", None, "tensor"),
            P("pipe", "tensor"),
            P("pipe", "dp", "tensor"),
            P("pipe", None, None),
            P("pipe", None),
        ),
        check_vma=False,
    )
```

```python
import functools
import math

import jax
import jax.numpy as jnp
from jax import lax
from jax.experimental import pallas as pl
from jax.experimental.pallas import tpu as pltpu
from jax.sharding import PartitionSpec as P

HEAD_DIM = 64
LANES = 128
MARGIN = 8
BAND = 4
F32 = jnp.float32
BF16 = jnp.bfloat16


def product(left, right, left_axis, right_axis):
    return lax.dot_general(
        left, right, (((left_axis,), (right_axis,)), ((), ())), preferred_element_type=F32
    )


def settings(mebibytes):
    return pltpu.CompilerParams(vmem_limit_bytes=mebibytes << 20)


def fill_padded(padded, values):
    extent = values.shape[0]
    half = (padded.shape[0] - extent) // 2
    padded[...] = jnp.zeros_like(padded)
    padded[half : half + extent, MARGIN : MARGIN + extent, :] = values.astype(F32)


def windows_of(padded, first, side, extent):
    for col in range(side):
        start = MARGIN - side // 2 + col
        yield col, padded[pl.ds(first, BAND + side - 1), pl.ds(start, extent), :]


def mix_kernel(side, reverse, with_base, *refs):
    x_ref, kernel_ref = refs[:2]
    out_ref, padded = refs[-2:]
    extent = x_ref.shape[1]
    fill_padded(padded, x_ref[0])

    def band(step, carry):
        first = step * BAND
        if with_base:
            total = refs[2][0, pl.ds(first, BAND)]
        else:
            total = jnp.zeros((BAND, extent, x_ref.shape[3]), F32)
        for col, window in windows_of(padded, first, side, extent):
            for row in range(side):
                tap = row * side + col
                weight = kernel_ref[side * side - 1 - tap if reverse else tap]
                total = total + window[row : row + BAND] * weight
        out_ref[0, pl.ds(first, BAND)] = total.astype(out_ref.dtype)
        return carry

    lax.fori_loop(0, extent // BAND, band, 0)


def depthwise(grid, kernel, side, base=None, reverse=False, dtype=F32):
    images, extent, _, channels = grid.shape
    block = pl.BlockSpec((1, extent, extent, LANES), lambda n, c: (n, 0, 0, c))
    taps = pl.BlockSpec((side * side, LANES), lambda n, c: (0, c))
    extra = () if base is None else (base,)
    return pl.pallas_call(
        functools.partial(mix_kernel, side, reverse, base is not None),
        grid=(images, channels // LANES),
        in_specs=[block, taps] + [block] * len(extra),
        out_specs=block,
        out_shape=jax.ShapeDtypeStruct(grid.shape, dtype),
        scratch_shapes=[pltpu.VMEM((extent + side - 1, extent + 2 * MARGIN, LANES), F32)],
        compiler_params=settings(32),
    )(grid, kernel, *extra)


def taps_kernel(side, x_ref, upstream_ref, out_ref, padded, sums):
    extent = x_ref.shape[1]
    fill_padded(padded, x_ref[0])
    sums[...] = jnp.zeros_like(sums)

    def band(step, carry):
        first = step * BAND
        upstream = upstream_ref[0, pl.ds(first, BAND)]
        for col, window in windows_of(padded, first, side, extent):
            for row in range(side):
                part = window[row : row + BAND] * upstream
                sums[row * side + col] += jnp.sum(part.reshape(-1, 8, LANES), 0)
        return carry

    lax.fori_loop(0, extent // BAND, band, 0)
    out_ref[0] = jnp.sum(sums[...], 1)


def depthwise_taps(grid, upstream, side):
    images, extent, _, channels = grid.shape
    block = pl.BlockSpec((1, extent, extent, LANES), lambda n, c: (n, 0, 0, c))
    sums = pl.pallas_call(
        functools.partial(taps_kernel, side),
        grid=(images, channels // LANES),
        in_specs=[block, block],
        out_specs=pl.BlockSpec((1, side * side, LANES), lambda n, c: (n, 0, c)),
        out_shape=jax.ShapeDtypeStruct((images, side * side, channels), F32),
        scratch_shapes=[
            pltpu.VMEM((extent + side - 1, extent + 2 * MARGIN, LANES), F32),
            pltpu.VMEM((side * side, 8, LANES), F32),
        ],
        compiler_params=settings(32),
    )(grid, upstream)
    return jnp.sum(sums, 0)


def gelu_and_slope(values):
    cumulative = 0.5 * (1.0 + lax.erf(values * (1.0 / math.sqrt(2.0))))
    density = jnp.exp(-0.5 * values * values) * (1.0 / math.sqrt(2.0 * math.pi))
    return ((values * cumulative).astype(BF16), (cumulative + values * density).astype(BF16))


def store_parts(out_ref, total):
    if len(out_ref.shape) == 2:
        out_ref[...] = total.astype(BF16)
        return
    width = out_ref.shape[2]
    for part in range(out_ref.shape[0]):
        out_ref[part] = total[:, part * width : (part + 1) * width].astype(BF16)


def mlp_kernel(step, x_ref, first_ref, second_ref, hidden_ref, slope_ref, out_ref):
    x = x_ref[...]
    total = None
    for at in range(0, first_ref.shape[1], step):
        units = slice(at, at + step)
        hidden, slope = gelu_and_slope(product(x, first_ref[:, units], 1, 0))
        hidden_ref[:, units] = hidden
        slope_ref[:, units] = slope
        part = product(hidden, second_ref[units, :], 1, 0)
        total = part if total is None else total + part
    store_parts(out_ref, total)


def mlp_back_kernel(step, upstream_ref, slope_ref, first_ref, second_ref, grad_ref, out_ref):
    upstream = upstream_ref[...]
    total = None
    for at in range(0, first_ref.shape[1], step):
        units = slice(at, at + step)
        grad = product(upstream, second_ref[units, :], 1, 1) * slope_ref[:, units].astype(F32)
        grad = grad.astype(BF16)
        grad_ref[:, units] = grad
        part = product(grad, first_ref[:, units], 1, 1)
        total = part if total is None else total + part
    store_parts(out_ref, total)


def parts_spec(count, rows, width, tile):
    if count is None:
        return (
            pl.BlockSpec((tile, width), lambda i: (i, 0)),
            jax.ShapeDtypeStruct((rows, width), BF16),
        )
    return (
        pl.BlockSpec((count, tile, width // count), lambda i: (0, i, 0)),
        jax.ShapeDtypeStruct((count, rows, width // count), BF16),
    )


def largest_step(units):
    return 512 if units % 512 == 0 else units


def mlp(x, first, second, tile, count=None):
    rows, units = (x.shape[0], first.shape[1])
    whole = [pl.BlockSpec(w.shape, lambda i: (0, 0)) for w in (first, second)]
    out_spec, out_shape = parts_spec(count, rows, second.shape[1], tile)
    inside = pl.BlockSpec((tile, units), lambda i: (i, 0))
    return pl.pallas_call(
        functools.partial(mlp_kernel, largest_step(units)),
        grid=(rows // tile,),
        in_specs=[pl.BlockSpec((tile, x.shape[1]), lambda i: (i, 0))] + whole,
        out_specs=[inside, inside, out_spec],
        out_shape=[jax.ShapeDtypeStruct((rows, units), BF16)] * 2 + [out_shape],
        compiler_params=settings(56),
    )(x, first, second)


def mlp_back(upstream, slope, first, second, tile, count=None):
    rows, units = slope.shape
    whole = [pl.BlockSpec(w.shape, lambda i: (0, 0)) for w in (first, second)]
    out_spec, out_shape = parts_spec(count, rows, first.shape[0], tile)
    inside = pl.BlockSpec((tile, units), lambda i: (i, 0))
    return pl.pallas_call(
        functools.partial(mlp_back_kernel, largest_step(units)),
        grid=(rows // tile,),
        in_specs=[pl.BlockSpec((tile, upstream.shape[1]), lambda i: (i, 0)), inside] + whole,
        out_specs=[inside, out_spec],
        out_shape=[jax.ShapeDtypeStruct((rows, units), BF16), out_shape],
        compiler_params=settings(56),
    )(upstream, slope, first, second)


def head_probs(query, keys, mask):
    scores = product(query, keys, 1, 1) * (HEAD_DIM**-0.5)
    scores = jnp.where(mask > 0, scores, -1000000000.0)
    raised = jnp.exp(scores - jnp.max(scores, -1, keepdims=True))
    return raised * (1.0 / jnp.sum(raised, -1, keepdims=True))


def lane_pairs(width):
    for pair in range(width // LANES):
        yield [slice(at + pair * LANES, at + (pair + 1) * LANES) for at in (0, width, 2 * width)]


def heads_of(pair):
    return [pair[:, at : at + HEAD_DIM] for at in range(0, LANES, HEAD_DIM)]


def attend_kernel(project_ref, mask_ref, out_ref):
    mask = mask_ref[0]
    for places in lane_pairs(out_ref.shape[2]):
        query, keys, values = (heads_of(project_ref[0, :, at]) for at in places)
        parts = [
            product(head_probs(q, k, mask).astype(BF16), u, 1, 0).astype(BF16)
            for q, k, u in zip(query, keys, values)
        ]
        out_ref[0, :, places[0]] = jnp.concatenate(parts, 1)


def attend(project, mask):
    images, tokens, wide = project.shape
    width = wide // 3
    return pl.pallas_call(
        attend_kernel,
        grid=(images,),
        in_specs=[
            pl.BlockSpec((1, tokens, wide), lambda i: (i, 0, 0)),
            pl.BlockSpec((1, 1, tokens), lambda i: (i, 0, 0)),
        ],
        out_specs=pl.BlockSpec((1, tokens, width), lambda i: (i, 0, 0)),
        out_shape=jax.ShapeDtypeStruct((images, tokens, width), BF16),
        compiler_params=settings(48),
    )(project, mask[:, None, :])


def attend_back_kernel(project_ref, mask_ref, upstream_ref, out_ref):
    mask = mask_ref[0]
    scale = HEAD_DIM**-0.5
    for places in lane_pairs(upstream_ref.shape[2]):
        query, keys, values = (heads_of(project_ref[0, :, at]) for at in places)
        upstream = heads_of(upstream_ref[0, :, places[0]])
        grads = ([], [], [])
        for q, k, u, d in zip(query, keys, values, upstream):
            exact = head_probs(q, k, mask)
            grad_probs = product(d, u, 1, 1)
            held = jnp.sum(grad_probs * exact, -1, keepdims=True)
            grad_scores = (exact * (grad_probs - held)).astype(BF16)
            grads[0].append((product(grad_scores, k, 1, 0) * scale).astype(BF16))
            grads[1].append((product(grad_scores, q, 0, 0) * scale).astype(BF16))
            grads[2].append(product(exact.astype(BF16), d, 0, 0).astype(BF16))
        for at, parts in zip(places, grads):
            out_ref[0, :, at] = jnp.concatenate(parts, 1)


def attend_back(project, mask, upstream):
    images, tokens, wide = project.shape
    width = wide // 3
    whole = pl.BlockSpec((1, tokens, wide), lambda i: (i, 0, 0))
    return pl.pallas_call(
        attend_back_kernel,
        grid=(images,),
        in_specs=[
            whole,
            pl.BlockSpec((1, 1, tokens), lambda i: (i, 0, 0)),
            pl.BlockSpec((1, tokens, width), lambda i: (i, 0, 0)),
        ],
        out_specs=whole,
        out_shape=jax.ShapeDtypeStruct(project.shape, BF16),
        compiler_params=settings(48),
    )(project, mask[:, None, :], upstream)


def traded(array, axis, bit):
    return lax.ppermute(array, axis, [(i, i ^ bit) for i in range(lax.axis_size(axis))])


def bits_of(axis):
    return [1 << k for k in range((lax.axis_size(axis) - 1).bit_length())]


def total_over(values, axis):
    for bit in bits_of(axis):
        values = values + traded(values, axis, bit)
    return values


def first_section():
    return lax.axis_index("pipe") == 0


def select(former, latter):
    return jnp.where(first_section(), former, latter)


def layer_pair(own):
    flat = own.reshape((2, own.shape[0] // 2) + own.shape[1:])
    odd = lax.axis_index("dp") % 2
    sent = lax.dynamic_index_in_dim(flat, odd, 0, keepdims=False)
    got = traded(sent, "pipe", 1)
    rest = traded(got, "dp", 1)
    first_half = jnp.where(odd == 0, got, rest)
    second_half = jnp.where(odd == 0, rest, got)
    other = jnp.concatenate([first_half, second_half], 0)
    return (select(own, other), select(other, own))


def small_pair(own):
    other = traded(own, "pipe", 1)
    return (select(own, other), select(other, own))


def own_block(values, count, axis):
    return lax.dynamic_slice_in_dim(values, lax.axis_index("tensor") * count, count, axis)


def widen(values, whole, axis):
    shape = list(values.shape)
    shape[axis] = whole
    empty = jnp.zeros(tuple(shape), F32)
    return lax.dynamic_update_slice_in_dim(
        empty, values, lax.axis_index("tensor") * values.shape[axis], axis
    )


def gather(values):
    return lax.all_gather(values, "tensor", axis=1, tiled=True)


def scatter_tokens(values):
    return lax.psum_scatter(values, "tensor", scatter_dimension=1, tiled=True).astype(F32)


def scatter_parts(parts):
    return lax.psum_scatter(parts, "tensor", scatter_dimension=0, tiled=False).astype(F32)


def relative_order(count):
    width = (count - 1).bit_length()
    return sorted(range(count), key=lambda r: format(r, f"0{width}b")[::-1])


def by_relative(values):
    count = lax.axis_size("dp")
    index = lax.axis_index("dp")
    block = values.shape[1] // count
    return jnp.concatenate(
        [
            lax.dynamic_slice_in_dim(values, (index ^ r) * block, block, 1)
            for r in relative_order(count)
        ],
        1,
    )


def inner(left, right, axis):
    if axis == 0:
        left = by_relative(left)
    else:
        right = by_relative(right)
    return product(left, right, 0, 0).astype(BF16)


def halved(partial, axis):
    for bit in bits_of("dp"):
        kept, sent = jnp.split(partial, 2, axis)
        partial = kept.astype(F32) + traded(sent, "dp", bit).astype(F32)
        if bit != bits_of("dp")[-1]:
            partial = partial.astype(BF16)
    return partial


def share_of(partial, axis, layer):
    block = halved(partial, axis)
    arrived = lax.ppermute(block.astype(BF16), "pipe", [(1 - layer, layer)])
    return (block, arrived)


def windows(coarse, fine):
    starts = [row * fine // coarse for row in range(coarse)]
    stops = [-(-(row + 1) * fine // coarse) for row in range(coarse)]
    return (starts, stops)


def pool_axis(grid, axis, coarse):
    starts, stops = windows(coarse, grid.shape[axis])
    slabs = []
    for start, stop in zip(starts, stops):
        slab = lax.slice_in_dim(grid, start, stop, axis=axis)
        slabs.append(jnp.sum(slab, axis=axis, keepdims=True) * (1.0 / (stop - start)))
    return jnp.concatenate(slabs, axis)


def unpool_axis(grid, axis, fine):
    starts, stops = windows(grid.shape[axis], fine)
    slabs = []
    for place in range(fine):
        parts = [
            lax.slice_in_dim(grid, row, row + 1, axis=axis) * (1.0 / (stop - start))
            for row, (start, stop) in enumerate(zip(starts, stops))
            if start <= place < stop
        ]
        slabs.append(sum(parts[1:], parts[0]))
    return jnp.concatenate(slabs, axis)


def norm_rows(values, epsilon):
    centred = values - jnp.mean(values, -1, keepdims=True)
    inverse = lax.rsqrt(jnp.mean(centred * centred, -1, keepdims=True) + epsilon)
    return (centred * inverse, inverse)


def norm_back(upstream, scaled, inverse, gains):
    weighted = upstream * gains
    return inverse * (
        weighted
        - jnp.mean(weighted, -1, keepdims=True)
        - scaled * jnp.mean(weighted * scaled, -1, keepdims=True)
    )


def flat(values):
    return values.reshape(-1, values.shape[-1])


def placing(places):
    cells = jnp.arange(places.shape[1])
    return (places[:, :, None] == cells[None, None, :]).astype(BF16)


def conv_forward(feature, w):
    images, cells, own = feature.shape
    side = math.isqrt(cells)
    count = lax.axis_size("tensor")
    channels = own * count
    grid = feature.reshape(images, side, side, own)
    mixed = flat(depthwise(grid, w["dw"], 7))
    sums = total_over(jnp.stack([jnp.sum(mixed, -1), jnp.sum(mixed * mixed, -1)]), "tensor")
    centre = sums[0] / channels
    inverse = lax.rsqrt(sums[1] / channels - centre * centre + 1e-06)
    scaled = (mixed - centre[:, None]) * inverse[:, None]
    normed = gather((scaled * w["gain"][0] + w["shift"]).astype(BF16))
    hidden, slope, parts = mlp(normed, w["pw_in"], w["pw_out"], cells // 2, count)
    branch = scatter_parts(parts)
    out = flat(feature).astype(F32) + w["gain"][1] * branch
    square = total_over(jnp.sum(out * out, -1), "tensor")
    measure = jnp.sqrt(square / channels).reshape(images, cells)
    kept = dict(
        grid=grid,
        scaled=scaled,
        inverse=inverse,
        normed=normed,
        hidden=hidden,
        slope=slope,
        branch=branch,
    )
    return (out.reshape(images, cells, own), measure, kept)


def vit_forward(stream, feature_out, places, key_mask, w):
    images, own_tokens, width = stream.shape
    count = lax.axis_size("tensor")
    tokens = own_tokens * count
    side = math.isqrt(tokens)
    cells, own = feature_out.shape[1:]
    fine = math.isqrt(cells)
    own_width = w["attn"].shape[0]
    pooled = pool_axis(feature_out.reshape(images, fine, fine, own), 1, side)
    pooled = pool_axis(pooled, 2, side)
    pooled = gather(pooled.reshape(images * tokens, own).astype(BF16))
    adapted = product(pooled, w["proj_cols"], 1, 0).reshape(images, side, side, own_width)
    spread = depthwise(adapted, w["taps"], 3).reshape(images, tokens, own_width)
    gated = (jnp.tanh(w["gate"]) * spread).astype(BF16)
    picked = jnp.einsum("ntc,ncw->ntw", places, gated, preferred_element_type=F32).astype(BF16)
    moved = lax.all_to_all(picked, "tensor", split_axis=1, concat_axis=2, tiled=True)
    stream_in = stream + moved.astype(F32)
    scaled_a, inverse_a = norm_rows(stream_in, 1e-05)
    normed_a = gather((scaled_a * w["vit_gain"][0] + w["vit_shift"][0]).astype(BF16))
    project = product(flat(normed_a), w["qkv"], 1, 0).astype(BF16)
    project = project.reshape(images, tokens, 3 * own_width)
    attended = attend(project, key_mask)
    partial = product(flat(attended), w["attn"], 1, 0).astype(BF16)
    stream_mid = stream_in + scatter_tokens(partial.reshape(images, tokens, width))
    scaled_b, inverse_b = norm_rows(stream_mid, 1e-05)
    normed_b = gather((scaled_b * w["vit_gain"][1] + w["vit_shift"][1]).astype(BF16))
    hidden, slope, partial = mlp(flat(normed_b), w["fc_in"], w["fc_out"], tokens)
    stream_out = stream_mid + scatter_tokens(partial.reshape(images, tokens, width))
    measure = jnp.sqrt(jnp.mean(stream_out * stream_out, -1))
    kept = dict(
        pooled=pooled,
        adapted=adapted,
        spread=spread,
        places=places,
        key_mask=key_mask,
        scaled_a=scaled_a,
        inverse_a=inverse_a,
        normed_a=normed_a,
        project=project,
        attended=attended,
        scaled_b=scaled_b,
        inverse_b=inverse_b,
        normed_b=normed_b,
        hidden=hidden,
        slope=slope,
    )
    return (stream_out, measure, kept)


def vit_backward(grad_stream, cells, kept, w):
    images, own_tokens, width = grad_stream.shape
    count = lax.axis_size("tensor")
    tokens = own_tokens * count
    side = math.isqrt(tokens)
    own_width = w["attn"].shape[0]
    grad_full = flat(gather(grad_stream.astype(BF16)))
    grad_hidden, partial = mlp_back(grad_full, kept["slope"], w["fc_in"], w["fc_out"], tokens)
    fc_out = inner(kept["hidden"], grad_full, 1)
    fc_in = inner(flat(kept["normed_b"]), grad_hidden, 0)
    grad_normed_b = scatter_tokens(partial.reshape(images, tokens, width))
    gain_second = jnp.sum(grad_normed_b * kept["scaled_b"], (0, 1))
    shift_second = jnp.sum(grad_normed_b, (0, 1))
    grad_mid = grad_stream.astype(F32) + norm_back(
        grad_normed_b, kept["scaled_b"], kept["inverse_b"], w["vit_gain"][1]
    )
    grad_mid_full = flat(gather(grad_mid.astype(BF16)))
    grad_attended = product(grad_mid_full, w["attn"], 1, 1).astype(BF16)
    grad_project = flat(
        attend_back(
            kept["project"], kept["key_mask"], grad_attended.reshape(images, tokens, own_width)
        )
    )
    partial = product(grad_project, w["qkv"], 1, 1).astype(BF16)
    attn = inner(flat(kept["attended"]), grad_mid_full, 1)
    qkv = inner(flat(kept["normed_a"]), grad_project, 0)
    grad_normed_a = scatter_tokens(partial.reshape(images, tokens, width))
    gain_first = jnp.sum(grad_normed_a * kept["scaled_a"], (0, 1))
    shift_first = jnp.sum(grad_normed_a, (0, 1))
    grad_in = grad_mid + norm_back(
        grad_normed_a, kept["scaled_a"], kept["inverse_a"], w["vit_gain"][0]
    )
    grad_cols = lax.all_to_all(
        grad_in.astype(BF16), "tensor", split_axis=2, concat_axis=1, tiled=True
    )
    grad_placed = jnp.einsum(
        "ntc,ntw->ncw", kept["places"], grad_cols, preferred_element_type=F32
    )
    gate_value = jnp.tanh(w["gate"])
    gate = jnp.sum(grad_placed * kept["spread"], (0, 1)) * (1.0 - gate_value * gate_value)
    grad_spread = (grad_placed * gate_value).reshape(images, side, side, own_width)
    grad_adapted = flat(depthwise(grad_spread, w["taps"], 3, reverse=True, dtype=BF16))
    taps = depthwise_taps(kept["adapted"], grad_spread, 3)
    grad_pooled = product(gather(grad_adapted), w["proj_rows"], 1, 1)
    proj = inner(kept["pooled"], grad_adapted, 0)
    grads = dict(qkv=qkv, attn=attn, fc_in=fc_in, fc_out=fc_out, proj=proj)
    model_width = w["vit_gain"].shape[1]
    sums = jnp.concatenate(
        [
            widen(taps, model_width, 1),
            widen(gate[None], model_width, 1),
            jnp.stack([gain_first, gain_second, shift_first, shift_second]),
        ],
        0,
    )
    return (grad_in, grad_pooled, grads, sums)


def conv_backward(grad_feature, grad_pooled, kept, w):
    images, cells, own = grad_feature.shape
    count = lax.axis_size("tensor")
    channels = own * count
    side = math.isqrt(cells)
    coarse = math.isqrt(grad_pooled.shape[0] // images)
    unpooled = unpool_axis(grad_pooled.reshape(images, coarse, coarse, own), 2, side)
    unpooled = unpool_axis(unpooled, 1, side)
    grad_rows = flat(grad_feature).astype(F32) + flat(unpooled)
    grad_branch = gather((grad_rows * w["gain"][1]).astype(BF16))
    grad_hidden, parts = mlp_back(
        grad_branch, kept["slope"], w["pw_in"], w["pw_out"], cells // 2, count
    )
    scale = jnp.sum(grad_rows * kept["branch"], 0)
    pw_out = inner(kept["hidden"], grad_branch, 1)
    pw_in = inner(kept["normed"], grad_hidden, 0)
    grad_normed = scatter_parts(parts)
    scaled = kept["scaled"]
    gain = jnp.sum(grad_normed * scaled, 0)
    shift = jnp.sum(grad_normed, 0)
    weighted = grad_normed * w["gain"][0]
    sums = total_over(jnp.stack([jnp.sum(weighted, -1), jnp.sum(weighted * scaled, -1)]), "tensor")
    grad_mixed = kept["inverse"][:, None] * (
        weighted - sums[0][:, None] / channels - scaled * (sums[1][:, None] / channels)
    )
    grad_grid = grad_mixed.reshape(images, side, side, own)
    grad_in = depthwise(
        grad_grid, w["dw"], 7, base=grad_rows.reshape(images, side, side, own), reverse=True
    )
    taps = depthwise_taps(kept["grid"], grad_grid, 7)
    sums = jnp.concatenate([taps, jnp.stack([gain, scale, shift])], 0)
    return (grad_in.reshape(images, cells, own), dict(pw_in=pw_in, pw_out=pw_out), sums)


SPLIT_AXIS = dict(qkv=0, attn=1, fc_in=0, fc_out=1, pw_in=0, pw_out=1, proj=0)


def body(
    x_vit,
    x_conv,
    positions,
    valid,
    qkv_weight,
    attn_weight,
    fc_in,
    fc_out,
    vit_gains,
    vit_shifts,
    pw_in,
    pw_out,
    dw_kernel,
    conv_gains,
    conv_shift,
    proj_weight,
    taps,
    gate,
    dy_vit,
    dy_conv,
):
    sections = lax.axis_size("pipe")
    here = x_vit.shape[0] // sections
    own_width = attn_weight.shape[1]
    own_channels = pw_out.shape[2] // lax.axis_size("tensor")
    model_width = vit_gains.shape[2]
    tap_count = dw_kernel.shape[1]
    side = taps.shape[1]

    def portion(source):
        return lax.dynamic_slice_in_dim(source, lax.axis_index("pipe") * here, here, 0)

    conv_small = small_pair(jnp.concatenate([dw_kernel[0], conv_gains[0], conv_shift], 0))
    pairs = dict(pw_in=layer_pair(pw_in[0]), pw_out=layer_pair(pw_out[0]))
    vit_small = small_pair(jnp.concatenate([taps[0], gate, vit_gains[0], vit_shifts[0]], 0))
    pairs.update(
        proj_cols=layer_pair(own_block(proj_weight[0], own_width, 1)),
        qkv=layer_pair(qkv_weight[0].reshape(model_width, -1)),
        attn=layer_pair(attn_weight[0]),
        fc_in=layer_pair(fc_in[0]),
        fc_out=layer_pair(fc_out[0]),
        proj_rows=layer_pair(own_block(proj_weight[0], own_channels, 0)),
    )

    def weights_of(layer):
        w = {name: pair[layer] for name, pair in pairs.items()}
        conv, vit = (conv_small[layer], vit_small[layer])
        w.update(
            dw=conv[:tap_count],
            gain=conv[tap_count : tap_count + 2],
            shift=conv[tap_count + 2],
            taps=own_block(vit[:side], own_width, 1),
            gate=own_block(vit[side], own_width, 0),
            vit_gain=vit[side + 1 : side + 3],
            vit_shift=vit[side + 3 :],
        )
        return w

    weights = [weights_of(0), weights_of(1)]
    places = placing(portion(positions))
    key_mask = portion(valid)
    stream, feature = (portion(x_vit), portion(x_conv))
    outs = [{}, {}]
    conv_kept, vit_kept = ([None, None], [None, None])
    features = [None, None]
    for layer in range(2):
        features[layer], measure, conv_kept[layer] = conv_forward(feature, weights[layer])
        feature = features[layer].astype(BF16)
        outs[layer].update(conv=feature, rms_conv=measure)
    for layer in range(2):
        stream_out, measure, vit_kept[layer] = vit_forward(
            stream.astype(F32), features[layer], places, key_mask, weights[layer]
        )
        stream = stream_out.astype(BF16)
        outs[layer].update(vit=stream, rms_vit=measure)
    grad_stream, grad_feature = (portion(dy_vit), portion(dy_conv))
    shares = [{}, {}]
    vit_sums, conv_sums = ([None, None], [None, None])
    pooled_grads = [None, None]
    for layer in (1, 0):
        grad_stream, pooled_grads[layer], grads, vit_sums[layer] = vit_backward(
            grad_stream, feature.shape[1], vit_kept[layer], weights[layer]
        )
        outs[layer]["grad_vit"] = grad_stream
        grad_stream = grad_stream.astype(BF16)
        for name, partial in grads.items():
            shares[layer][name] = share_of(partial, SPLIT_AXIS[name], layer)
    for layer in (1, 0):
        grad_feature, grads, conv_sums[layer] = conv_backward(
            grad_feature, pooled_grads[layer], conv_kept[layer], weights[layer]
        )
        outs[layer]["grad_conv"] = grad_feature
        grad_feature = grad_feature.astype(BF16)
        for name, partial in grads.items():
            shares[layer][name] = share_of(partial, SPLIT_AXIS[name], layer)

    def over_images(pair):
        return total_over(select(*pair) + traded(select(*pair[::-1]), "pipe", 1), "dp")

    token_sums = total_over(over_images(vit_sums), "tensor")
    column_sums = over_images(conv_sums)

    def large(name):
        (block, arrived), (other_block, other_arrived) = (shares[0][name], shares[1][name])
        total = select(block, other_block) + arrived.astype(F32) + other_arrived.astype(F32)
        return total.reshape((1,) + total.shape)

    def both_images(name):
        mine, theirs = (
            select(outs[0][name], outs[1][name]),
            select(outs[1][name], outs[0][name]),
        )
        sent = theirs.astype(BF16) if name.startswith("grad") else theirs
        got = traded(sent, "pipe", 1).astype(mine.dtype)
        return jnp.concatenate([select(mine, got), select(got, mine)], 0)[None]

    grad_qkv = large("qkv")
    return (
        both_images("vit"),
        both_images("conv"),
        both_images("grad_vit"),
        both_images("grad_conv"),
        both_images("rms_vit"),
        both_images("rms_conv"),
        grad_qkv.reshape(grad_qkv.shape[:2] + (3, own_width)),
        large("attn"),
        large("fc_in"),
        large("fc_out"),
        token_sums[side + 1 : side + 3][None],
        token_sums[side + 3 :][None],
        large("pw_in"),
        large("pw_out"),
        column_sums[:tap_count][None],
        column_sums[tap_count : tap_count + 2][None],
        column_sums[tap_count + 2 :],
        large("proj"),
        token_sums[:side][None],
        token_sums[side][None],
    )


def solution(mesh):
    return jax.shard_map(
        body,
        mesh=mesh,
        in_specs=(
            P("dp", "tensor", None),
            P("dp", None, "tensor"),
            P("dp", None),
            P("dp", None),
            P("pipe", None, None, "tensor"),
            P("pipe", "tensor", None),
            P("pipe", None, "tensor"),
            P("pipe", "tensor", None),
            P("pipe", None, None),
            P("pipe", None, None),
            P("pipe", None, "tensor"),
            P("pipe", "tensor", None),
            P("pipe", None, "tensor"),
            P("pipe", None, "tensor"),
            P("pipe", "tensor"),
            P("pipe", None, None),
            P("pipe", None, None),
            P("pipe", None),
            P("dp", "tensor", None),
            P("dp", None, "tensor"),
        ),
        out_specs=(
            P("pipe", "dp", "tensor", None),
            P("pipe", "dp", None, "tensor"),
            P("pipe", "dp", "tensor", None),
            P("pipe", "dp", None, "tensor"),
            P("pipe", "dp", "tensor"),
            P("pipe", "dp", None),
            P("pipe", "dp", None, "tensor"),
            P("pipe", "tensor", "dp"),
            P("pipe", "dp", "tensor"),
            P("pipe", "tensor", "dp"),
            P("pipe", None, None),
            P("pipe", None, None),
            P("pipe", "dp", "tensor"),
            P("pipe", "tensor", "dp"),
            P("pipe", None, "tensor"),
            P("pipe", None, "tensor"),
            P("pipe", "tensor"),
            P("pipe", "dp", "tensor"),
            P("pipe", None, None),
            P("pipe", None),
        ),
        check_vma=False,
    )
```

```python
import functools
import math

import jax
import jax.numpy as jnp
from jax import lax
from jax.experimental import pallas as pl
from jax.experimental.pallas import tpu as pltpu
from jax.sharding import PartitionSpec as P

PIPE, DP, TENSOR = ("pipe", "dp", "tensor")
HEAD_DIM = 64
LANES = 128
MARGIN = 8
BAND = 4
F32 = jnp.float32
BF16 = jnp.bfloat16


def product(left, right, left_axis, right_axis):
    return lax.dot_general(
        left, right, (((left_axis,), (right_axis,)), ((), ())), preferred_element_type=F32
    )


ANYWHERE = pl.BlockSpec(memory_space=pl.ANY)


def settings(mebibytes):
    return pltpu.CompilerParams(vmem_limit_bytes=mebibytes << 20)


def run(kernel, args, in_specs, mebibytes, later_than=(), **rest):
    count, extra = (len(args), len(later_than))

    def without_extra(*refs):
        kernel(*refs[:count], *refs[count + extra :])

    return pl.pallas_call(
        without_extra,
        in_specs=list(in_specs) + [ANYWHERE] * extra,
        compiler_params=settings(mebibytes),
        **rest,
    )(*args, *later_than)


def after(array, *earlier):
    def nothing(*refs):
        return None

    return pl.pallas_call(
        nothing,
        in_specs=[ANYWHERE] * (1 + len(earlier)),
        out_specs=ANYWHERE,
        out_shape=jax.ShapeDtypeStruct(array.shape, array.dtype),
        input_output_aliases={0: 0},
    )(array, *earlier)


def fill_padded(padded, values):
    extent = values.shape[0]
    half = (padded.shape[0] - extent) // 2
    padded[...] = jnp.zeros_like(padded)
    padded[half : half + extent, MARGIN : MARGIN + extent, :] = values.astype(F32)


def windows_of(padded, first, side, extent):
    for col in range(side):
        start = MARGIN - side // 2 + col
        yield col, padded[pl.ds(first, BAND + side - 1), pl.ds(start, extent), :]


def mix_kernel(side, reverse, with_base, *refs):
    x_ref, kernel_ref = refs[:2]
    out_ref, padded = refs[-2:]
    extent = x_ref.shape[1]
    fill_padded(padded, x_ref[0])

    def band(step, carry):
        first = step * BAND
        if with_base:
            total = refs[2][0, pl.ds(first, BAND)]
        else:
            total = jnp.zeros((BAND, extent, x_ref.shape[3]), F32)
        for col, window in windows_of(padded, first, side, extent):
            for row in range(side):
                tap = row * side + col
                weight = kernel_ref[side * side - 1 - tap if reverse else tap]
                total = total + window[row : row + BAND] * weight
        out_ref[0, pl.ds(first, BAND)] = total.astype(out_ref.dtype)
        return carry

    lax.fori_loop(0, extent // BAND, band, 0)


def depthwise(grid, kernel, side, base=None, reverse=False, dtype=F32, later_than=()):
    images, extent, _, channels = grid.shape
    block = pl.BlockSpec((1, extent, extent, LANES), lambda n, c: (n, 0, 0, c))
    taps = pl.BlockSpec((side * side, LANES), lambda n, c: (0, c))
    extra = () if base is None else (base,)
    return run(
        functools.partial(mix_kernel, side, reverse, base is not None),
        (grid, kernel) + extra,
        [block, taps] + [block] * len(extra),
        32,
        later_than,
        grid=(images, channels // LANES),
        out_specs=block,
        out_shape=jax.ShapeDtypeStruct(grid.shape, dtype),
        scratch_shapes=[pltpu.VMEM((extent + side - 1, extent + 2 * MARGIN, LANES), F32)],
    )


def taps_kernel(side, x_ref, upstream_ref, out_ref, padded, sums):
    extent = x_ref.shape[1]
    fill_padded(padded, x_ref[0])
    sums[...] = jnp.zeros_like(sums)

    def band(step, carry):
        first = step * BAND
        upstream = upstream_ref[0, pl.ds(first, BAND)]
        for col, window in windows_of(padded, first, side, extent):
            for row in range(side):
                part = window[row : row + BAND] * upstream
                sums[row * side + col] += jnp.sum(part.reshape(-1, 8, LANES), 0)
        return carry

    lax.fori_loop(0, extent // BAND, band, 0)
    out_ref[0] = jnp.sum(sums[...], 1)


def depthwise_taps(grid, upstream, side, later_than=()):
    images, extent, _, channels = grid.shape
    block = pl.BlockSpec((1, extent, extent, LANES), lambda n, c: (n, 0, 0, c))
    sums = run(
        functools.partial(taps_kernel, side),
        (grid, upstream),
        [block, block],
        32,
        later_than,
        grid=(images, channels // LANES),
        out_specs=pl.BlockSpec((1, side * side, LANES), lambda n, c: (n, 0, c)),
        out_shape=jax.ShapeDtypeStruct((images, side * side, channels), F32),
        scratch_shapes=[
            pltpu.VMEM((extent + side - 1, extent + 2 * MARGIN, LANES), F32),
            pltpu.VMEM((side * side, 8, LANES), F32),
        ],
    )
    return jnp.sum(sums, 0)


def gelu_and_slope(values):
    cumulative = 0.5 * (1.0 + lax.erf(values * (1.0 / math.sqrt(2.0))))
    density = jnp.exp(-0.5 * values * values) * (1.0 / math.sqrt(2.0 * math.pi))
    return ((values * cumulative).astype(BF16), (cumulative + values * density).astype(BF16))


def mlp_kernel(step, x_ref, first_ref, second_ref, hidden_ref, slope_ref, out_ref):
    x = x_ref[...]
    total = None
    for at in range(0, first_ref.shape[1], step):
        units = slice(at, at + step)
        hidden, slope = gelu_and_slope(product(x, first_ref[:, units], 1, 0))
        hidden_ref[:, units] = hidden
        slope_ref[:, units] = slope
        part = product(hidden, second_ref[units, :], 1, 0)
        total = part if total is None else total + part
    out_ref[...] = total.astype(BF16)


def mlp_back_kernel(step, upstream_ref, slope_ref, first_ref, second_ref, grad_ref, out_ref):
    upstream = upstream_ref[...]
    total = None
    for at in range(0, first_ref.shape[1], step):
        units = slice(at, at + step)
        grad = product(upstream, second_ref[units, :], 1, 1) * slope_ref[:, units].astype(F32)
        grad = grad.astype(BF16)
        grad_ref[:, units] = grad
        part = product(grad, first_ref[:, units], 1, 1)
        total = part if total is None else total + part
    out_ref[...] = total.astype(BF16)


QUARTERS = 4


def load_weight(meta_ref, sources, held_ref, semaphores):
    own, got, pair, rest = sources
    size = held_ref.shape[0] // QUARTERS
    rows = [pl.ds(k * size, size) for k in range(QUARTERS)]
    traded_quarters = [(got, 0, 0), (pair, 0, 2), (rest, 0, 1), (rest, 1, 3)]

    @pl.when(meta_ref[0] == 1)
    def _():
        for k in range(QUARTERS):
            pltpu.make_async_copy(
                own.at[rows[k]], held_ref.at[rows[k]], semaphores.at[k]
            ).start()

    @pl.when(meta_ref[0] != 1)
    def _():
        for k, (source, at, relative) in enumerate(traded_quarters):
            start = pl.multiple_of(lax.bitwise_xor(meta_ref[1], relative) * size, 16)
            pltpu.make_async_copy(
                source.at[rows[at]], held_ref.at[pl.ds(start, size)], semaphores.at[k]
            ).start()

    return [
        pltpu.make_async_copy(own.at[rows[k]], held_ref.at[rows[k]], semaphores.at[k])
        for k in range(QUARTERS)
    ]


def store_parts(out_ref, total):
    width = out_ref.shape[2]
    for part in range(out_ref.shape[0]):
        out_ref[part] = total[:, part * width : (part + 1) * width].astype(BF16)


def wide_mlp_kernel(back, step, meta_ref, *refs):
    inputs, refs = (refs[: 2 if back else 1], refs[2 if back else 1 :])
    sources, refs = ((refs[:4], refs[4:8]), refs[8:])
    inside, (out_ref, first_ref, second_ref, sems) = (refs[:-4], refs[-4:])

    @pl.when(pl.program_id(0) == 0)
    def _():
        copies = load_weight(meta_ref, sources[0], first_ref, sems.at[0])
        copies += load_weight(meta_ref, sources[1], second_ref, sems.at[1])
        for copy in copies:
            copy.wait()

    x = inputs[0][...]
    total = None
    for at in range(0, first_ref.shape[1], step):
        units = slice(at, at + step)
        if back:
            value = product(x, second_ref[units, :], 1, 1) * inputs[1][:, units].astype(F32)
            value = value.astype(BF16)
            part = product(value, first_ref[:, units], 1, 1)
        else:
            value, slope = gelu_and_slope(product(x, first_ref[:, units], 1, 0))
            inside[1][:, units] = slope
            part = product(value, second_ref[units, :], 1, 0)
        inside[0][:, units] = value
        total = part if total is None else total + part
    store_parts(out_ref, total)


def wide_mlp(layer, x, first, second, tile, slope=None, later_than=()):
    rows, units = (x.shape[0], first[0].shape[1])
    count = lax.axis_size(TENSOR)
    back = slope is not None
    meta = jnp.stack(
        [(lax.axis_index(PIPE) == layer).astype(jnp.int32), lax.axis_index(DP) % QUARTERS]
    )
    x_spec = pl.BlockSpec((tile, x.shape[1]), lambda i, s: (i, 0))
    units_spec = pl.BlockSpec((tile, units), lambda i, s: (i, 0))
    width = first[0].shape[0] // count
    inside = 1 if back else 2
    args = [x] + ([slope] if back else []) + list(first) + list(second)
    taken, extra = (len(args), len(later_than))
    kernel = functools.partial(wide_mlp_kernel, back, largest_step(units))

    def without_extra(meta_ref, *refs):
        kernel(meta_ref, *refs[:taken], *refs[taken + extra :])

    out = pl.pallas_call(
        without_extra,
        grid_spec=pltpu.PrefetchScalarGridSpec(
            num_scalar_prefetch=1,
            grid=(rows // tile,),
            in_specs=[x_spec] + [units_spec] * back + [ANYWHERE] * (8 + extra),
            out_specs=[units_spec] * inside
            + [pl.BlockSpec((count, tile, width), lambda i, s: (0, i, 0))],
            scratch_shapes=[
                pltpu.VMEM(first[0].shape, BF16),
                pltpu.VMEM(second[0].shape, BF16),
                pltpu.SemaphoreType.DMA((2, QUARTERS)),
            ],
        ),
        out_shape=[jax.ShapeDtypeStruct((rows, units), BF16)] * inside
        + [jax.ShapeDtypeStruct((count, rows, width), BF16)],
        compiler_params=settings(56),
    )(meta, *args, *later_than)
    return (out[:-1], out[-1])


def largest_step(units):
    return 512 if units % 512 == 0 else units


def mlp(x, first, second, later_than=()):
    rows, units = (x.shape[0], first.shape[1])
    args = (x, first, second)
    shapes = [(rows, units), (rows, units), (rows, second.shape[1])]
    return run(
        functools.partial(mlp_kernel, largest_step(units)),
        args,
        [pl.BlockSpec(arg.shape, lambda: (0, 0)) for arg in args],
        56,
        later_than,
        out_specs=[pl.BlockSpec(shape, lambda: (0, 0)) for shape in shapes],
        out_shape=[jax.ShapeDtypeStruct(shape, BF16) for shape in shapes],
    )


def mlp_back(upstream, slope, first, second, later_than=()):
    args = (upstream, slope, first, second)
    shapes = [slope.shape, (slope.shape[0], first.shape[0])]
    return run(
        functools.partial(mlp_back_kernel, largest_step(slope.shape[1])),
        args,
        [pl.BlockSpec(arg.shape, lambda: (0, 0)) for arg in args],
        56,
        later_than,
        out_specs=[pl.BlockSpec(shape, lambda: (0, 0)) for shape in shapes],
        out_shape=[jax.ShapeDtypeStruct(shape, BF16) for shape in shapes],
    )


def head_probs(query, keys, mask):
    scores = product(query, keys, 1, 1) * (HEAD_DIM**-0.5)
    scores = jnp.where(mask > 0, scores, -1000000000.0)
    raised = jnp.exp(scores - jnp.max(scores, -1, keepdims=True))
    return raised * (1.0 / jnp.sum(raised, -1, keepdims=True))


def lane_pairs(width):
    for pair in range(width // LANES):
        yield [slice(at + pair * LANES, at + (pair + 1) * LANES) for at in (0, width, 2 * width)]


def heads_of(pair):
    return [pair[:, at : at + HEAD_DIM] for at in range(0, LANES, HEAD_DIM)]


def attend_kernel(project_ref, mask_ref, out_ref):
    mask = mask_ref[0]
    for places in lane_pairs(out_ref.shape[2]):
        query, keys, values = (heads_of(project_ref[0, :, at]) for at in places)
        parts = [
            product(head_probs(q, k, mask).astype(BF16), u, 1, 0).astype(BF16)
            for q, k, u in zip(query, keys, values)
        ]
        out_ref[0, :, places[0]] = jnp.concatenate(parts, 1)


def attend(project, mask, later_than=()):
    images, tokens, wide = project.shape
    width = wide // 3
    return run(
        attend_kernel,
        (project, mask[:, None, :]),
        [
            pl.BlockSpec((1, tokens, wide), lambda i: (i, 0, 0)),
            pl.BlockSpec((1, 1, tokens), lambda i: (i, 0, 0)),
        ],
        48,
        later_than,
        grid=(images,),
        out_specs=pl.BlockSpec((1, tokens, width), lambda i: (i, 0, 0)),
        out_shape=jax.ShapeDtypeStruct((images, tokens, width), BF16),
    )


def attend_back_kernel(project_ref, mask_ref, upstream_ref, out_ref):
    mask = mask_ref[0]
    scale = HEAD_DIM**-0.5
    for places in lane_pairs(upstream_ref.shape[2]):
        query, keys, values = (heads_of(project_ref[0, :, at]) for at in places)
        upstream = heads_of(upstream_ref[0, :, places[0]])
        grads = ([], [], [])
        for q, k, u, d in zip(query, keys, values, upstream):
            exact = head_probs(q, k, mask)
            grad_probs = product(d, u, 1, 1)
            held = jnp.sum(grad_probs * exact, -1, keepdims=True)
            grad_scores = (exact * (grad_probs - held)).astype(BF16)
            grads[0].append((product(grad_scores, k, 1, 0) * scale).astype(BF16))
            grads[1].append((product(grad_scores, q, 0, 0) * scale).astype(BF16))
            grads[2].append(product(exact.astype(BF16), d, 0, 0).astype(BF16))
        for at, parts in zip(places, grads):
            out_ref[0, :, at] = jnp.concatenate(parts, 1)


def attend_back(project, mask, upstream, later_than=()):
    images, tokens, wide = project.shape
    width = wide // 3
    whole = pl.BlockSpec((1, tokens, wide), lambda i: (i, 0, 0))
    return run(
        attend_back_kernel,
        (project, mask[:, None, :], upstream),
        [
            whole,
            pl.BlockSpec((1, 1, tokens), lambda i: (i, 0, 0)),
            pl.BlockSpec((1, tokens, width), lambda i: (i, 0, 0)),
        ],
        48,
        later_than,
        grid=(images,),
        out_specs=whole,
        out_shape=jax.ShapeDtypeStruct(project.shape, BF16),
    )


def residual_kernel(feature_ref, branch_ref, gain_ref, out_ref, pooled_ref, rows):
    total = feature_ref[0].astype(F32) + gain_ref[0] * branch_ref[0].astype(F32)
    out_ref[0] = total.astype(BF16)
    groups = total.shape[0] // 4
    for group in range(groups):
        for part in range(3):
            fine = 4 * group + part
            rows[3 * group + part] = 0.5 * (total[fine] + total[fine + 1])
    columns = [rows[:, pl.ds(part, groups, stride=4), :] for part in range(4)]
    for part in range(3):
        pooled_ref[0, :, pl.ds(part, groups, stride=3), :] = 0.5 * (columns[part] + columns[part + 1])


def residual_and_pool(feature, branch, gain, later_than=()):
    images, fine, _, channels = feature.shape
    coarse = fine // 4 * 3
    block = pl.BlockSpec((1, fine, fine, LANES), lambda n, c: (n, 0, 0, c))
    out, pooled = run(
        residual_kernel,
        (feature, branch, gain[None]),
        [block, block, pl.BlockSpec((1, LANES), lambda n, c: (0, c))],
        32,
        later_than,
        grid=(images, channels // LANES),
        out_specs=[block, pl.BlockSpec((1, coarse, coarse, LANES), lambda n, c: (n, 0, 0, c))],
        out_shape=[
            jax.ShapeDtypeStruct(feature.shape, BF16),
            jax.ShapeDtypeStruct((images, coarse, coarse, channels), F32),
        ],
        scratch_shapes=[pltpu.VMEM((coarse, fine, LANES), F32)],
    )
    return (out, pooled.astype(BF16))


def spread_back_kernel(pooled_ref, upstream_ref, gain_ref, out_ref, scaled_ref, rows):
    groups = upstream_ref.shape[1] // 4
    columns = [pooled_ref[0, :, pl.ds(part, groups, stride=3), :] for part in range(3)]
    for part in range(4):
        near = [columns[at] for at in (part - 1, part) if 0 <= at < 3]
        rows[:, pl.ds(part, groups, stride=4), :] = 0.5 * sum(near[1:], near[0])
    for group in range(groups):
        for part in range(4):
            near = [rows[3 * group + at] for at in (part - 1, part) if 0 <= at < 3]
            total = upstream_ref[0, 4 * group + part].astype(F32) + 0.5 * sum(near[1:], near[0])
            out_ref[0, 4 * group + part] = total
            scaled_ref[0, 4 * group + part] = (gain_ref[0] * total).astype(BF16)


def spread_back(pooled, upstream, gain, later_than=()):
    images, fine, _, channels = upstream.shape
    coarse = pooled.shape[1]
    block = pl.BlockSpec((1, fine, fine, LANES), lambda n, c: (n, 0, 0, c))
    return run(
        spread_back_kernel,
        (pooled, upstream, gain[None]),
        [
            pl.BlockSpec((1, coarse, coarse, LANES), lambda n, c: (n, 0, 0, c)),
            block,
            pl.BlockSpec((1, LANES), lambda n, c: (0, c)),
        ],
        32,
        later_than,
        grid=(images, channels // LANES),
        out_specs=[block, block],
        out_shape=[
            jax.ShapeDtypeStruct(upstream.shape, F32),
            jax.ShapeDtypeStruct(upstream.shape, BF16),
        ],
        scratch_shapes=[pltpu.VMEM((coarse, fine, LANES), F32)],
    )


def add_kernel(kept_ref, got_ref, out_ref):
    out_ref[...] = (kept_ref[...].astype(F32) + got_ref[...].astype(F32)).astype(BF16)


def add_to_first_half(partial, got, later_than=()):
    rows, width = got.shape
    tile = math.gcd(rows, 256)
    if tile % 16:
        return (partial[:rows].astype(F32) + got.astype(F32)).astype(BF16)
    block = pl.BlockSpec((tile, width), lambda i: (i, 0))
    return run(
        add_kernel,
        (partial, got),
        [block, block],
        32,
        later_than,
        grid=(rows // tile,),
        out_specs=block,
        out_shape=jax.ShapeDtypeStruct(got.shape, BF16),
    )


class Held:
    def __init__(self, **arrays):
        self.add(**arrays)

    def add(self, **arrays):
        vars(self).update(arrays)


def traded(array, axis, bit):
    return lax.ppermute(array, axis, [(i, i ^ bit) for i in range(lax.axis_size(axis))])


def bits_of(axis):
    return [1 << k for k in range((lax.axis_size(axis) - 1).bit_length())]


def total_over(values, axis):
    for bit in bits_of(axis):
        values = values + traded(values, axis, bit)
    return values


def first_section():
    return lax.axis_index(PIPE) == 0


def select(former, latter):
    return jnp.where(first_section(), former, latter)


def halves_of(own, axis):
    half = own.shape[axis] // 2
    odd = lax.axis_index(DP) % 2
    return lax.dynamic_slice_in_dim(own, odd * half, half, axis)


def joined(mine, theirs, axis):
    even = lax.axis_index(DP) % 2 == 0
    return jnp.concatenate([jnp.where(even, mine, theirs), jnp.where(even, theirs, mine)], axis)


class Trade:
    def __init__(self, own, *earlier):
        self.own = own
        self.got = traded(after(halves_of(own, 0), *earlier), PIPE, 1)

    def share(self, *earlier):
        self.got = after(self.got, *earlier)
        self.rest = traded(self.got, DP, 1)

    def layers(self, *earlier):
        rest = after(self.rest, *earlier) if earlier else self.rest
        other = joined(self.got, rest, 0)
        return (select(self.own, other), select(other, self.own))


class QuarterTrade:
    def __init__(self, own, *earlier):
        size = own.shape[0] // QUARTERS
        sent = lax.dynamic_slice_in_dim(own, lax.axis_index(DP) % QUARTERS * size, size, 0)
        self.own = own
        self.got = traded(after(sent, *earlier), PIPE, 1)

    def share(self, *earlier):
        self.got = after(self.got, *earlier)
        self.pair = traded(self.got, DP, 2)

    def share_again(self, *earlier):
        self.pair = after(self.pair, *earlier)
        self.rest = traded(jnp.concatenate([self.got, self.pair], 0), DP, 1)

    def pieces(self):
        return (self.own, self.got, self.pair, self.rest)


def small_pair(own):
    other = traded(own, PIPE, 1)
    return (select(own, other), select(other, own))


def own_block(values, count, axis):
    return lax.dynamic_slice_in_dim(values, lax.axis_index(TENSOR) * count, count, axis)


def widen(values, whole, axis):
    shape = list(values.shape)
    shape[axis] = whole
    empty = jnp.zeros(tuple(shape), F32)
    return lax.dynamic_update_slice_in_dim(
        empty, values, lax.axis_index(TENSOR) * values.shape[axis], axis
    )


def gather(values):
    return lax.all_gather(values, TENSOR, axis=1, tiled=True)


def turned(values, by):
    count = lax.axis_size(TENSOR)
    return lax.ppermute(values, TENSOR, [(i, (i + by) % count) for i in range(count)])


def ring_total(values):
    count = lax.axis_size(TENSOR)
    return sum([turned(values, k) for k in range(1, count)], values)


def in_order(blocks, axis):
    count = len(blocks)
    size = blocks[0].shape[axis]
    start = (count - 1 - lax.axis_index(TENSOR)) * size
    joined = jnp.concatenate(blocks[::-1] + blocks[:0:-1], axis)
    return lax.dynamic_slice_in_dim(joined, start, count * size, axis)


def exchanged(values, split_axis, concat_axis):
    count = lax.axis_size(TENSOR)
    index = lax.axis_index(TENSOR)
    size = values.shape[split_axis] // count
    blocks = []
    for k in range(count):
        start = (index + k) % count * size
        block = lax.dynamic_slice_in_dim(values, start, size, split_axis)
        blocks.append(turned(block, k) if k else block)
    return in_order(blocks, concat_axis)


def ring_gather(values):
    blocks = [turned(values, k) if k else values for k in range(lax.axis_size(TENSOR))]
    return in_order(blocks, 1)


def tokens_to_holders(values):
    return exchanged(values, 1, 2)


def features_to_holders(values):
    return exchanged(values, 2, 1)


def scatter_tokens(values):
    return lax.psum_scatter(values, TENSOR, scatter_dimension=1, tiled=True).astype(F32)


def scatter_parts(parts):
    return lax.psum_scatter(parts, TENSOR, scatter_dimension=0, tiled=False).astype(F32)


def relative_order(count):
    width = (count - 1).bit_length()
    return sorted(range(count), key=lambda r: format(r, f"0{width}b")[::-1])


def by_relative(values, axis=DP):
    count = lax.axis_size(axis)
    index = lax.axis_index(axis)
    block = values.shape[1] // count
    return jnp.concatenate(
        [
            lax.dynamic_slice_in_dim(values, (index ^ r) * block, block, 1)
            for r in relative_order(count)
        ],
        1,
    )


def inner(left, right, *earlier):
    left = by_relative(left)
    if earlier:
        left = after(left, *earlier)
    return product(left, right, 0, 0).astype(BF16)


class Reduction:
    def __init__(self, partial, also_tensor=False):
        self.partial = partial
        self.steps_left = 4 if also_tensor else 2
        self.moves = [(DP, bit, 0) for bit in bits_of(DP)]
        if also_tensor:
            self.moves += [(TENSOR, bit, 1) for bit in bits_of(TENSOR)]
        self.send()

    def send(self):
        name, bit, axis = self.moves.pop(0)
        size = self.partial.shape[axis] // 2
        self.got = traded(lax.slice_in_dim(self.partial, size, 2 * size, axis=axis), name, bit)

    def step(self, *earlier):
        halvings = -(-(len(self.moves) + 1) // self.steps_left)
        self.steps_left -= 1
        for _ in range(halvings):
            self.partial = add_to_first_half(self.partial, self.got, earlier)
            if self.moves:
                self.send()
        return self.partial


def over_sections(former, latter):
    kept, sent = (select(former, latter), select(latter, former))
    return kept.astype(F32) + traded(sent, PIPE, 1).astype(F32)


def norm_rows(values, epsilon):
    centred = values - jnp.mean(values, -1, keepdims=True)
    inverse = lax.rsqrt(jnp.mean(centred * centred, -1, keepdims=True) + epsilon)
    return (centred * inverse, inverse)


def norm_back(upstream, scaled, inverse, gains):
    weighted = upstream * gains
    return inverse * (
        weighted
        - jnp.mean(weighted, -1, keepdims=True)
        - scaled * jnp.mean(weighted * scaled, -1, keepdims=True)
    )


def flat(values):
    return values.reshape(-1, values.shape[-1])


def placing(places):
    cells = jnp.arange(places.shape[1])
    return (places[:, :, None] == cells[None, None, :]).astype(BF16)


def conv_norm(grid, w, later_than=()):
    own = grid.shape[-1]
    channels = own * lax.axis_size(TENSOR)
    mixed = flat(depthwise(grid, w.dw, 7, later_than=later_than))
    sums = ring_total(jnp.stack([jnp.sum(mixed, -1), jnp.sum(mixed * mixed, -1)]))
    centre = sums[0] / channels
    inverse = lax.rsqrt(sums[1] / channels - centre * centre + 1e-06)
    scaled = (mixed - centre[:, None]) * inverse[:, None]
    normed = (scaled * w.gain[0] + w.shift).astype(BF16)
    return (normed, Held(grid=grid, scaled=scaled, inverse=inverse))


def conv_residual(grid, branch, w, *earlier):
    own = grid.shape[-1]
    channels = own * lax.axis_size(TENSOR)
    out, pooled = residual_and_pool(grid, branch.reshape(grid.shape), w.gain[1], earlier)
    exact = grid.astype(F32) + w.gain[1] * branch.reshape(grid.shape).astype(F32)
    square = jnp.sum(exact * exact, -1).reshape(grid.shape[0], -1)
    return (out, flat(pooled), square / channels)


def adapter_forward(stream, pooled, places, w, *earlier):
    images, tokens, _ = places.shape
    side = math.isqrt(tokens)
    pooled_rows = tokens_to_holders(pooled.reshape(images, tokens, -1))
    adapted_rows = product(flat(pooled_rows), w.proj, 1, 0).astype(BF16)
    adapted = features_to_holders(adapted_rows.reshape(pooled_rows.shape[:2] + (-1,)))
    adapted = adapted.reshape(images, side, side, -1)
    spread = depthwise(adapted, w.taps, 3, later_than=earlier).reshape(images, tokens, -1)
    gated = (jnp.tanh(w.gate) * spread).astype(BF16)
    picked = jnp.einsum("ntc,ncw->ntw", places, gated, preferred_element_type=F32).astype(BF16)
    stream_in = stream + tokens_to_holders(picked).astype(F32)
    return (stream_in, Held(pooled=flat(pooled_rows), adapted=adapted, spread=spread))


def vit_norm(stream, w, which):
    scaled, inverse = norm_rows(stream, 1e-05)
    normed = (scaled * w.vit_gain[which] + w.vit_shift[which]).astype(BF16)
    return (normed, scaled, inverse)


def vit_attention(normed, key_mask, w, *earlier):
    images, tokens, width = normed.shape
    project = product(flat(normed), w.qkv, 1, 0).astype(BF16).reshape(images, tokens, -1)
    attended = attend(project, key_mask, earlier)
    held = tokens_to_holders(attended)
    return (project, flat(held), product(flat(held), w.attn, 1, 0).reshape(held.shape))


def vit_attention_back(grad_own, kept, key_mask, w, *earlier):
    images, _, width = grad_own.shape
    grad_attended = product(flat(grad_own), w.attn, 1, 1).astype(BF16)
    grad_attended = features_to_holders(grad_attended.reshape(grad_own.shape))
    grad_project = flat(attend_back(kept.project, key_mask, grad_attended, earlier))
    partial = product(grad_project, w.qkv, 1, 1).astype(BF16)
    return (grad_project, partial.reshape(images, -1, width))


def adapter_backward(grad_cols, kept, places, w, later_than=()):
    images, tokens, _ = places.shape
    side = math.isqrt(tokens)
    grad_placed = jnp.einsum("ntc,ntw->ncw", places, grad_cols, preferred_element_type=F32)
    gate_value = jnp.tanh(w.gate)
    gate = jnp.sum(grad_placed * kept.spread, (0, 1)) * (1.0 - gate_value * gate_value)
    grad_spread = (grad_placed * gate_value).reshape(images, side, side, -1)
    grad_adapted = flat(
        depthwise(
            grad_spread, w.taps, 3, reverse=True, dtype=BF16, later_than=later_than
        )
    )
    grad_rows = tokens_to_holders(grad_adapted.reshape(images, tokens, -1))
    grad_pooled = product(flat(grad_rows), w.proj, 1, 1).astype(BF16)
    grad_pooled = features_to_holders(grad_pooled.reshape(grad_rows.shape[:2] + (-1,)))
    taps = depthwise_taps(kept.adapted, grad_spread, 3, later_than=(grad_adapted,))
    grad_pooled = grad_pooled.astype(F32).reshape(images, side, side, -1)
    return (flat(grad_rows), grad_pooled, taps, gate)


def conv_norm_back(grad_normed, kept, w):
    grid = kept.grid
    channels = grid.shape[-1] * lax.axis_size(TENSOR)
    scaled = kept.scaled
    weighted = grad_normed * w.gain[0]
    sums = ring_total(jnp.stack([jnp.sum(weighted, -1), jnp.sum(weighted * scaled, -1)]))
    grad_mixed = kept.inverse[:, None] * (
        weighted - sums[0][:, None] / channels - scaled * (sums[1][:, None] / channels)
    )
    gain = jnp.sum(grad_normed * scaled, 0)
    shift = jnp.sum(grad_normed, 0)
    return (grad_mixed.reshape(grid.shape), gain, shift)


def body(
    x_vit,
    x_conv,
    positions,
    valid,
    qkv_weight,
    attn_weight,
    fc_in,
    fc_out,
    vit_gains,
    vit_shifts,
    pw_in,
    pw_out,
    dw_kernel,
    conv_gains,
    conv_shift,
    proj_weight,
    taps,
    gate,
    dy_vit,
    dy_conv,
):
    here = x_vit.shape[0] // lax.axis_size(PIPE)
    count = lax.axis_size(TENSOR)
    cells = x_conv.shape[1]
    own_channels = x_conv.shape[2]
    conv_side = math.isqrt(cells)
    own_width = attn_weight.shape[1]
    own_units = fc_out.shape[1]
    conv_units = pw_out.shape[1]
    channels = pw_out.shape[2]
    model_width = vit_gains.shape[2]
    tap_count = dw_kernel.shape[1]
    side = taps.shape[1]
    tile = cells // 2

    def portion(source):
        return lax.dynamic_slice_in_dim(source, lax.axis_index(PIPE) * here, here, 0)

    conv_small = small_pair(jnp.concatenate([dw_kernel[0], conv_gains[0], conv_shift], 0))
    trade_in = QuarterTrade(pw_in[0], conv_small[0])
    vit_small = small_pair(
        after(jnp.concatenate([taps[0], gate, vit_gains[0], vit_shifts[0]], 0), conv_small[0])
    )
    weights = [Held(), Held()]
    for layer in range(2):
        conv, vit = (conv_small[layer], vit_small[layer])
        weights[layer].add(
            dw=conv[:tap_count],
            gain=conv[tap_count : tap_count + 2],
            shift=conv[tap_count + 2],
            taps=own_block(vit[:side], own_width, 1),
            gate=own_block(vit[side], own_width, 0),
            vit_gain=vit[side + 1 : side + 3],
            vit_shift=vit[side + 3 :],
        )
    w0, w1 = weights

    def take(**pairs):
        for name, pair in pairs.items():
            for w, weight in zip(weights, pair):
                w.add(**{name: weight})

    def both_images(former, latter, *earlier):
        mine, theirs = (select(former, latter), select(latter, former))
        sent = theirs.astype(BF16) if theirs.ndim > 3 else theirs
        if earlier:
            sent = after(sent, *earlier)
        got = traded(sent, PIPE, 1).astype(mine.dtype)
        return jnp.concatenate([select(mine, got), select(got, mine)], 0)

    stream = portion(x_vit)
    grid0 = portion(x_conv).reshape(here, conv_side, conv_side, own_channels)
    grad_top = portion(dy_vit)
    grad_top_full = gather(grad_top)
    attn_half = lax.all_gather(halves_of(attn_weight[0], 1), TENSOR, axis=0, tiled=True)
    places = placing(portion(positions))
    key_mask = portion(valid)

    normed0, conv0 = conv_norm(grid0, w0)
    conv0.normed = gather(after(normed0, grad_top_full, attn_half))
    trade_in.share(normed0)
    trade_out = QuarterTrade(pw_out[0], trade_in.got)
    trade_in.share_again()
    first = trade_in.pieces()
    trade_out.share(trade_in.pair)
    trade_proj = Trade(proj_weight[0], trade_out.got)
    trade_out.share_again(trade_proj.got)
    second = trade_out.pieces()
    (conv0.hidden, conv0.slope), parts = wide_mlp(0, conv0.normed, first, second, tile)
    branch = scatter_parts(parts)
    conv0.branch = branch
    trade_proj.share(parts)
    trade_qkv = Trade(qkv_weight[0].reshape(model_width, -1), parts)
    trade_fc_in = Trade(fc_in[0], parts)
    grid1, pooled0, square0 = conv_residual(
        grid0, branch, w0, trade_qkv.got, trade_fc_in.got
    )
    trade_fc_out = Trade(fc_out[0], pooled0)
    take(proj=trade_proj.layers())
    trade_qkv.share(pooled0)

    normed1, conv1 = conv_norm(grid1, w1, (pooled0,))
    conv1.normed = gather(normed1)
    take(qkv=trade_qkv.layers(normed1))
    stream_in0, vit0 = adapter_forward(stream.astype(F32), pooled0, places, w0, normed1, w0.qkv)
    normed_a0, vit0.scaled_a, vit0.inverse_a = vit_norm(stream_in0, w0, 0)
    vit0.normed_a = gather(normed_a0)
    trade_fc_in.share(normed_a0)
    trade_fc_out.share(normed_a0)
    (conv1.hidden, conv1.slope), parts = wide_mlp(
        1, conv1.normed, first, second, tile, None, (normed_a0, trade_fc_out.got)
    )
    branch = scatter_parts(parts)
    conv1.branch = branch
    attn_got = traded(after(attn_half, parts), PIPE, 1)
    attn_halves = jnp.stack([attn_half, attn_got])
    attn_rest = traded(attn_halves, DP, 1)
    attn_full = [joined(mine, theirs, 1) for mine, theirs in zip(attn_halves, attn_rest)]
    take(attn=(select(*attn_full), select(*attn_full[::-1])))
    take(fc_in=trade_fc_in.layers(parts))
    take(fc_out=trade_fc_out.layers(parts))
    vit0.project, vit0.attended, moved = vit_attention(
        vit0.normed_a, key_mask, w0, parts
    )
    stream_mid0 = stream_in0 + moved
    normed_b0, vit0.scaled_b, vit0.inverse_b = vit_norm(stream_mid0, w0, 1)
    vit0.normed_b = gather(normed_b0)
    grid2, pooled1, square1 = conv_residual(grid1, branch, w1)
    vit0.hidden, vit0.slope, partial = mlp(
        flat(vit0.normed_b), w0.fc_in, w0.fc_out, (pooled1,)
    )
    stream_out0 = stream_mid0 + scatter_tokens(partial.reshape(stream_shape(vit0)))
    stream1 = stream_out0.astype(BF16)

    stream_in1, vit1 = adapter_forward(stream1.astype(F32), pooled1, places, w1, partial)
    normed_a1, vit1.scaled_a, vit1.inverse_a = vit_norm(stream_in1, w1, 0)
    vit1.normed_a = gather(normed_a1)
    vit1.project, vit1.attended, moved = vit_attention(vit1.normed_a, key_mask, w1)
    stream_mid1 = stream_in1 + moved
    normed_b1, vit1.scaled_b, vit1.inverse_b = vit_norm(stream_mid1, w1, 1)
    vit1.normed_b = gather(normed_b1)
    vit1.hidden, vit1.slope, top_partial = mlp(
        flat(vit1.normed_b), w1.fc_in, w1.fc_out
    )

    norm_sums = [None, None]
    tap_sums = [None, None]

    def back_to_middle(grad_out, grad_full, kept, w, beside, *earlier):
        grad_hidden, partial = mlp_back(
            flat(grad_full), kept.slope, w.fc_in, w.fc_out, earlier
        )
        grad_normed = scatter_tokens(partial.reshape(stream_shape(kept)))
        packed = jnp.concatenate(
            [
                inner(flat(kept.normed_b), grad_hidden, partial),
                inner(flat(grad_full), kept.hidden, partial),
            ],
            1,
        )
        grad_normed = after(grad_normed, packed, *beside(partial))
        sums = [jnp.sum(grad_normed * kept.scaled_b, (0, 1)), jnp.sum(grad_normed, (0, 1))]
        grad_mid = grad_out.astype(F32) + norm_back(
            grad_normed, kept.scaled_b, kept.inverse_b, w.vit_gain[1]
        )
        return (grad_mid, Reduction(packed), sums)

    def back_to_start(grad_mid, grad_own, kept, w, beside, *earlier):
        grad_project, partial = vit_attention_back(grad_own, kept, key_mask, w, *earlier)
        grad_normed = scatter_tokens(partial)
        qkv = inner(flat(kept.normed_a), grad_project, partial)
        grad_normed = after(grad_normed, qkv, *beside(partial))
        sums = [jnp.sum(grad_normed * kept.scaled_a, (0, 1)), jnp.sum(grad_normed, (0, 1))]
        grad_in = grad_mid + norm_back(
            grad_normed, kept.scaled_a, kept.inverse_a, w.vit_gain[0]
        )
        return (grad_in, qkv, sums)

    def row_grads(kept, grad_rows, grad_own, *earlier):
        sides = lax.axis_size(DP)
        pairs = [
            product(by_relative(left), by_relative(after(right, *earlier), TENSOR), 0, 0)
            for left, right in ((kept.pooled, grad_rows), (flat(grad_own), kept.attended))
        ]
        blocks = [pair.astype(BF16).reshape(sides, -1, model_width) for pair in pairs]
        return jnp.concatenate(blocks, 1).reshape(-1, model_width)

    def step_all(reductions, *earlier):
        return [reduction.step(*earlier) for reduction in reductions]

    grad_mid1, mlp1, sums_b1 = back_to_middle(
        grad_top, grad_top_full, vit1, w1, lambda partial: (), top_partial
    )
    grad_mid1_own = grad_mid1.astype(BF16)

    def beside_start1(partial):
        mlp1.step(partial)
        return [mlp1.step(partial)]

    grad_in1, qkv1, sums_a1 = back_to_start(grad_mid1, grad_mid1_own, vit1, w1, beside_start1)
    norm_sums[1] = jnp.stack([sums_a1[0], sums_b1[0], sums_a1[1], sums_b1[1]])
    grad_stream = grad_in1.astype(BF16)
    grad_stream_full = gather(grad_stream)
    grad_rows1, grad_pooled1, tap_sum, gate_sum = adapter_backward(
        features_to_holders(grad_stream), vit1, places, w1
    )
    tap_sums[1] = jnp.concatenate([tap_sum, gate_sum[None]], 0)

    grad_map1, scaled1 = spread_back(
        grad_pooled1, portion(dy_conv).reshape(grid0.shape), w1.gain[1]
    )
    grad_branch1 = gather(flat(scaled1))
    grad_mid0, mlp0, sums_b0 = back_to_middle(
        grad_stream, grad_stream_full, vit0, w0, lambda partial: (), scaled1
    )
    rows1 = Reduction(row_grads(vit1, grad_rows1, grad_mid1_own, scaled1), True)
    grad_mid0_own = grad_mid0.astype(BF16)
    rows1.step(grad_mid0_own)
    grad_in0, qkv0, sums_a0 = back_to_start(
        grad_mid0, grad_mid0_own, vit0, w0, lambda partial: ()
    )
    (grad_hidden1,), parts = wide_mlp(
        1, grad_branch1, first, second, tile, conv1.slope, (grad_mid0_own, rows1.partial)
    )
    grad_normed1 = scatter_parts(parts)
    conv_in1 = Reduction(inner(conv1.normed, grad_hidden1, parts))
    conv_out1 = Reduction(inner(grad_branch1, conv1.hidden, parts))
    norm_sums[0] = jnp.stack([sums_a0[0], sums_b0[0], sums_a0[1], sums_b0[1]])
    grad_last = grad_in0.astype(BF16)
    qkv = Reduction(jnp.concatenate([qkv0, qkv1], 1))
    grad_mixed1, gain1, shift1 = conv_norm_back(grad_normed1, conv1, w1)
    mlp0.step(grad_last)
    rows1.step(grad_last)
    qkv.step(grad_last)
    grad_rows0, grad_pooled0, tap_sum, gate_sum = adapter_backward(
        features_to_holders(grad_last), vit0, places, w0, (conv_in1.partial, conv_out1.partial)
    )
    tap_sums[0] = jnp.concatenate([tap_sum, gate_sum[None]], 0)
    grad_grid1 = depthwise(grad_mixed1, w1.dw, 7, grad_map1, True)
    grad_next = grad_grid1.astype(BF16)

    ready = step_all([mlp0, qkv], grad_grid1)
    grad_map0, scaled0 = spread_back(grad_pooled0, grad_next, w0.gain[1], ready)
    grad_branch0 = gather(flat(scaled0))
    step_all([conv_out1, conv_in1], scaled0)
    grad_fc = over_sections(after(mlp0.partial, scaled0), mlp1.partial)
    half = qkv.partial.shape[1] // 2
    grad_qkv = over_sections(after(qkv.partial[:, :half], scaled0), qkv.partial[:, half:])
    rows0 = Reduction(row_grads(vit0, grad_rows0, grad_mid0_own), True)
    taps1 = depthwise_taps(conv1.grid, grad_mixed1, 7, later_than=(scaled0,))
    ready = step_all([conv_out1, conv_in1], taps1)
    rows0.step(*ready)
    (grad_hidden0,), parts = wide_mlp(
        0,
        grad_branch0,
        first,
        second,
        tile,
        conv0.slope,
        ready + [rows0.partial, grad_fc, grad_qkv],
    )
    grad_normed0 = scatter_parts(parts)
    rows0.step(parts)
    conv_out0 = Reduction(inner(grad_branch0, conv0.hidden, rows0.partial))
    conv_in0 = Reduction(inner(conv0.normed, grad_hidden0, conv_out0.partial))
    conv_out0.step(conv_in0.partial)
    conv_in0.step(conv_out0.partial)
    conv_out0.step(conv_in0.partial)
    rows1.step(conv_in0.partial)
    grad_normed0 = after(grad_normed0, conv_in0.partial, conv_out0.partial)
    grad_mixed0, gain0, shift0 = conv_norm_back(grad_normed0, conv0, w0)
    grad_grid0 = depthwise(grad_mixed0, w0.dw, 7, grad_map0, True)
    grad_conv_out = over_sections(conv_out0.partial, conv_out1.partial)
    grad_conv = both_images(grad_grid0, grad_grid1)
    taps0 = depthwise_taps(conv0.grid, grad_mixed0, 7, later_than=(grad_grid0,))
    conv_in0.step(grad_grid0)
    grad_conv_in = over_sections(conv_in0.partial, conv_in1.partial)
    step_all([rows0, rows1], grad_grid0)
    stream_out1 = stream_mid1 + scatter_tokens(
        after(top_partial, grad_normed0).reshape(stream_shape(vit1))
    )
    rows0.step(taps0)
    grad_proj_attn = over_sections(rows0.partial, rows1.partial)
    proj_rows = channels // lax.axis_size(DP)
    scale1 = jnp.sum(flat(grad_map1) * conv1.branch, 0)
    scale0 = jnp.sum(flat(grad_map0) * conv0.branch, 0)

    def over_images(pair):
        return total_over(select(*pair) + traded(select(*pair[::-1]), PIPE, 1), DP)

    token_terms = [
        jnp.concatenate([widen(tap_sums[layer], model_width, 1), norm_sums[layer]], 0)
        for layer in range(2)
    ]
    token_sums = total_over(over_images(token_terms), TENSOR)
    column_sums = over_images(
        [
            jnp.concatenate([taps0, jnp.stack([gain0, scale0, shift0])], 0),
            jnp.concatenate([taps1, jnp.stack([gain1, scale1, shift1])], 0),
        ]
    )

    out_conv = both_images(grid1, grid2, grad_mid1_own).reshape(1, -1, cells, own_channels)
    out_vit = both_images(stream1, stream_out1.astype(BF16))[None]
    squares = total_over(both_images(square0, square1, grad_mid1_own), TENSOR)
    rms_conv = jnp.sqrt(squares)[None]
    mean_squares = [jnp.mean(out * out, -1) for out in (stream_out0, stream_out1)]
    rms_vit = jnp.sqrt(both_images(*mean_squares))[None]
    grad_vit = both_images(grad_in0[None], grad_in1[None], grad_last)
    grad_vit = grad_vit.reshape((1, -1) + grad_in0.shape[1:])
    return (
        out_vit,
        out_conv,
        grad_vit,
        grad_conv.reshape(1, -1, cells, own_channels),
        rms_vit,
        rms_conv,
        grad_qkv.reshape(1, -1, 3, own_width),
        grad_proj_attn[proj_rows:].T[None],
        grad_fc[:, :own_units][None],
        grad_fc[:, own_units:].T[None],
        token_sums[side + 1 : side + 3][None],
        token_sums[side + 3 :][None],
        grad_conv_in[None],
        grad_conv_out.T[None],
        column_sums[:tap_count][None],
        column_sums[tap_count : tap_count + 2][None],
        column_sums[tap_count + 2 :],
        grad_proj_attn[:proj_rows][None],
        token_sums[:side][None],
        token_sums[side][None],
    )


def stream_shape(kept):
    return kept.normed_b.shape


def solution(mesh):
    return jax.shard_map(
        body,
        mesh=mesh,
        in_specs=(
            P(DP, TENSOR, None),
            P(DP, None, TENSOR),
            P(DP, None),
            P(DP, None),
            P(PIPE, None, None, TENSOR),
            P(PIPE, TENSOR, None),
            P(PIPE, None, TENSOR),
            P(PIPE, TENSOR, None),
            P(PIPE, None, None),
            P(PIPE, None, None),
            P(PIPE, None, TENSOR),
            P(PIPE, TENSOR, None),
            P(PIPE, None, TENSOR),
            P(PIPE, None, TENSOR),
            P(PIPE, TENSOR),
            P(PIPE, None, None),
            P(PIPE, None, None),
            P(PIPE, None),
            P(DP, TENSOR, None),
            P(DP, None, TENSOR),
        ),
        out_specs=(
            P(PIPE, DP, TENSOR, None),
            P(PIPE, DP, None, TENSOR),
            P(PIPE, DP, TENSOR, None),
            P(PIPE, DP, None, TENSOR),
            P(PIPE, DP, TENSOR),
            P(PIPE, DP, None),
            P(PIPE, DP, None, TENSOR),
            P(PIPE, TENSOR, DP),
            P(PIPE, DP, TENSOR),
            P(PIPE, TENSOR, DP),
            P(PIPE, None, None),
            P(PIPE, None, None),
            P(PIPE, DP, TENSOR),
            P(PIPE, TENSOR, DP),
            P(PIPE, None, TENSOR),
            P(PIPE, None, TENSOR),
            P(PIPE, TENSOR),
            P(PIPE, DP, TENSOR),
            P(PIPE, None, None),
            P(PIPE, None),
        ),
        check_vma=False,
    )
```

```python
import functools
import math

import jax
import jax.numpy as jnp
from jax import lax
from jax.experimental import pallas as pl
from jax.experimental.pallas import tpu as pltpu
from jax.sharding import PartitionSpec as P

PIPE, DP, TENSOR = ("pipe", "dp", "tensor")
HEAD_DIM = 64
LANES = 128
MARGIN = 8
BAND = 4
F32 = jnp.float32
BF16 = jnp.bfloat16


def product(left, right, left_axis, right_axis):
    return lax.dot_general(
        left, right, (((left_axis,), (right_axis,)), ((), ())), preferred_element_type=F32
    )


ANYWHERE = pl.BlockSpec(memory_space=pl.ANY)


def settings(mebibytes):
    return pltpu.CompilerParams(vmem_limit_bytes=mebibytes << 20)


def run(kernel, args, in_specs, mebibytes, later_than=(), **rest):
    count, extra = (len(args), len(later_than))

    def without_extra(*refs):
        kernel(*refs[:count], *refs[count + extra :])

    return pl.pallas_call(
        without_extra,
        in_specs=list(in_specs) + [ANYWHERE] * extra,
        compiler_params=settings(mebibytes),
        **rest,
    )(*args, *later_than)


def after(array, *earlier):
    def nothing(*refs):
        return None

    return pl.pallas_call(
        nothing,
        in_specs=[ANYWHERE] * (1 + len(earlier)),
        out_specs=ANYWHERE,
        out_shape=jax.ShapeDtypeStruct(array.shape, array.dtype),
        input_output_aliases={0: 0},
    )(array, *earlier)


def fill_padded(padded, values):
    extent = values.shape[0]
    half = (padded.shape[0] - extent) // 2
    padded[...] = jnp.zeros_like(padded)
    padded[half : half + extent, MARGIN : MARGIN + extent, :] = values.astype(F32)


def windows_of(padded, first, side, extent):
    for col in range(side):
        start = MARGIN - side // 2 + col
        yield col, padded[pl.ds(first, BAND + side - 1), pl.ds(start, extent), :]


def mix_kernel(side, reverse, with_base, *refs):
    x_ref, kernel_ref = refs[:2]
    out_ref, padded = refs[-2:]
    extent = x_ref.shape[1]
    fill_padded(padded, x_ref[0])

    def band(step, carry):
        first = step * BAND
        if with_base:
            total = refs[2][0, pl.ds(first, BAND)]
        else:
            total = jnp.zeros((BAND, extent, x_ref.shape[3]), F32)
        for col, window in windows_of(padded, first, side, extent):
            for row in range(side):
                tap = row * side + col
                weight = kernel_ref[side * side - 1 - tap if reverse else tap]
                total = total + window[row : row + BAND] * weight
        out_ref[0, pl.ds(first, BAND)] = total.astype(out_ref.dtype)
        return carry

    lax.fori_loop(0, extent // BAND, band, 0)


def depthwise(grid, kernel, side, base=None, reverse=False, dtype=F32, later_than=()):
    images, extent, _, channels = grid.shape
    block = pl.BlockSpec((1, extent, extent, LANES), lambda n, c: (n, 0, 0, c))
    taps = pl.BlockSpec((side * side, LANES), lambda n, c: (0, c))
    extra = () if base is None else (base,)
    return run(
        functools.partial(mix_kernel, side, reverse, base is not None),
        (grid, kernel) + extra,
        [block, taps] + [block] * len(extra),
        32,
        later_than,
        grid=(images, channels // LANES),
        out_specs=block,
        out_shape=jax.ShapeDtypeStruct(grid.shape, dtype),
        scratch_shapes=[pltpu.VMEM((extent + side - 1, extent + 2 * MARGIN, LANES), F32)],
    )


def taps_kernel(side, x_ref, upstream_ref, out_ref, padded, sums):
    extent = x_ref.shape[1]
    fill_padded(padded, x_ref[0])
    sums[...] = jnp.zeros_like(sums)

    def band(step, carry):
        first = step * BAND
        upstream = upstream_ref[0, pl.ds(first, BAND)]
        for col, window in windows_of(padded, first, side, extent):
            for row in range(side):
                part = window[row : row + BAND] * upstream
                sums[row * side + col] += jnp.sum(part.reshape(-1, 8, LANES), 0)
        return carry

    lax.fori_loop(0, extent // BAND, band, 0)
    out_ref[0] = jnp.sum(sums[...], 1)


def depthwise_taps(grid, upstream, side, later_than=()):
    images, extent, _, channels = grid.shape
    block = pl.BlockSpec((1, extent, extent, LANES), lambda n, c: (n, 0, 0, c))
    sums = run(
        functools.partial(taps_kernel, side),
        (grid, upstream),
        [block, block],
        32,
        later_than,
        grid=(images, channels // LANES),
        out_specs=pl.BlockSpec((1, side * side, LANES), lambda n, c: (n, 0, c)),
        out_shape=jax.ShapeDtypeStruct((images, side * side, channels), F32),
        scratch_shapes=[
            pltpu.VMEM((extent + side - 1, extent + 2 * MARGIN, LANES), F32),
            pltpu.VMEM((side * side, 8, LANES), F32),
        ],
    )
    return jnp.sum(sums, 0)


def gelu_and_slope(values):
    cumulative = 0.5 * (1.0 + lax.erf(values * (1.0 / math.sqrt(2.0))))
    density = jnp.exp(-0.5 * values * values) * (1.0 / math.sqrt(2.0 * math.pi))
    return ((values * cumulative).astype(BF16), (cumulative + values * density).astype(BF16))


def mlp_kernel(step, x_ref, first_ref, second_ref, hidden_ref, slope_ref, out_ref):
    x = x_ref[...]
    total = None
    for at in range(0, first_ref.shape[1], step):
        units = slice(at, at + step)
        hidden, slope = gelu_and_slope(product(x, first_ref[:, units], 1, 0))
        hidden_ref[:, units] = hidden
        slope_ref[:, units] = slope
        part = product(hidden, second_ref[units, :], 1, 0)
        total = part if total is None else total + part
    out_ref[...] = total.astype(BF16)


def mlp_back_kernel(step, upstream_ref, slope_ref, first_ref, second_ref, grad_ref, out_ref):
    upstream = upstream_ref[...]
    total = None
    for at in range(0, first_ref.shape[1], step):
        units = slice(at, at + step)
        grad = product(upstream, second_ref[units, :], 1, 1) * slope_ref[:, units].astype(F32)
        grad = grad.astype(BF16)
        grad_ref[:, units] = grad
        part = product(grad, first_ref[:, units], 1, 1)
        total = part if total is None else total + part
    out_ref[...] = total.astype(BF16)


QUARTERS = 4


def load_weight(meta_ref, sources, held_ref, semaphores):
    own, got, pair, rest = sources
    size = held_ref.shape[0] // QUARTERS
    rows = [pl.ds(k * size, size) for k in range(QUARTERS)]
    traded_quarters = [(got, 0, 0), (pair, 0, 2), (rest, 0, 1), (rest, 1, 3)]

    @pl.when(meta_ref[0] == 1)
    def _():
        for k in range(QUARTERS):
            pltpu.make_async_copy(
                own.at[rows[k]], held_ref.at[rows[k]], semaphores.at[k]
            ).start()

    @pl.when(meta_ref[0] != 1)
    def _():
        for k, (source, at, relative) in enumerate(traded_quarters):
            start = pl.multiple_of(lax.bitwise_xor(meta_ref[1], relative) * size, 16)
            pltpu.make_async_copy(
                source.at[rows[at]], held_ref.at[pl.ds(start, size)], semaphores.at[k]
            ).start()

    return [
        pltpu.make_async_copy(own.at[rows[k]], held_ref.at[rows[k]], semaphores.at[k])
        for k in range(QUARTERS)
    ]


def store_parts(out_ref, total):
    width = out_ref.shape[2]
    for part in range(out_ref.shape[0]):
        out_ref[part] = total[:, part * width : (part + 1) * width].astype(BF16)


def wide_mlp_kernel(back, step, meta_ref, *refs):
    inputs, refs = (refs[: 2 if back else 1], refs[2 if back else 1 :])
    sources, refs = ((refs[:4], refs[4:8]), refs[8:])
    inside, (out_ref, first_ref, second_ref, sems) = (refs[:-4], refs[-4:])

    @pl.when(pl.program_id(0) == 0)
    def _():
        copies = load_weight(meta_ref, sources[0], first_ref, sems.at[0])
        copies += load_weight(meta_ref, sources[1], second_ref, sems.at[1])
        for copy in copies:
            copy.wait()

    x = inputs[0][...]
    total = None
    for at in range(0, first_ref.shape[1], step):
        units = slice(at, at + step)
        if back:
            value = product(x, second_ref[units, :], 1, 1) * inputs[1][:, units].astype(F32)
            value = value.astype(BF16)
            part = product(value, first_ref[:, units], 1, 1)
        else:
            value, slope = gelu_and_slope(product(x, first_ref[:, units], 1, 0))
            inside[1][:, units] = slope
            part = product(value, second_ref[units, :], 1, 0)
        inside[0][:, units] = value
        total = part if total is None else total + part
    store_parts(out_ref, total)


def wide_mlp(layer, x, first, second, tile, slope=None, later_than=()):
    rows, units = (x.shape[0], first[0].shape[1])
    count = lax.axis_size(TENSOR)
    back = slope is not None
    meta = jnp.stack(
        [(lax.axis_index(PIPE) == layer).astype(jnp.int32), lax.axis_index(DP) % QUARTERS]
    )
    x_spec = pl.BlockSpec((tile, x.shape[1]), lambda i, s: (i, 0))
    units_spec = pl.BlockSpec((tile, units), lambda i, s: (i, 0))
    width = first[0].shape[0] // count
    inside = 1 if back else 2
    args = [x] + ([slope] if back else []) + list(first) + list(second)
    taken, extra = (len(args), len(later_than))
    kernel = functools.partial(wide_mlp_kernel, back, largest_step(units))

    def without_extra(meta_ref, *refs):
        kernel(meta_ref, *refs[:taken], *refs[taken + extra :])

    out = pl.pallas_call(
        without_extra,
        grid_spec=pltpu.PrefetchScalarGridSpec(
            num_scalar_prefetch=1,
            grid=(rows // tile,),
            in_specs=[x_spec] + [units_spec] * back + [ANYWHERE] * (8 + extra),
            out_specs=[units_spec] * inside
            + [pl.BlockSpec((count, tile, width), lambda i, s: (0, i, 0))],
            scratch_shapes=[
                pltpu.VMEM(first[0].shape, BF16),
                pltpu.VMEM(second[0].shape, BF16),
                pltpu.SemaphoreType.DMA((2, QUARTERS)),
            ],
        ),
        out_shape=[jax.ShapeDtypeStruct((rows, units), BF16)] * inside
        + [jax.ShapeDtypeStruct((count, rows, width), BF16)],
        compiler_params=settings(56),
    )(meta, *args, *later_than)
    return (out[:-1], out[-1])


def largest_step(units):
    return 512 if units % 512 == 0 else units


def mlp(x, first, second, later_than=()):
    rows, units = (x.shape[0], first.shape[1])
    args = (x, first, second)
    shapes = [(rows, units), (rows, units), (rows, second.shape[1])]
    return run(
        functools.partial(mlp_kernel, largest_step(units)),
        args,
        [pl.BlockSpec(arg.shape, lambda: (0, 0)) for arg in args],
        56,
        later_than,
        out_specs=[pl.BlockSpec(shape, lambda: (0, 0)) for shape in shapes],
        out_shape=[jax.ShapeDtypeStruct(shape, BF16) for shape in shapes],
    )


def mlp_back(upstream, slope, first, second, later_than=()):
    args = (upstream, slope, first, second)
    shapes = [slope.shape, (slope.shape[0], first.shape[0])]
    return run(
        functools.partial(mlp_back_kernel, largest_step(slope.shape[1])),
        args,
        [pl.BlockSpec(arg.shape, lambda: (0, 0)) for arg in args],
        56,
        later_than,
        out_specs=[pl.BlockSpec(shape, lambda: (0, 0)) for shape in shapes],
        out_shape=[jax.ShapeDtypeStruct(shape, BF16) for shape in shapes],
    )


def head_probs(query, keys, mask):
    scores = product(query, keys, 1, 1) * (HEAD_DIM**-0.5)
    scores = jnp.where(mask > 0, scores, -1000000000.0)
    raised = jnp.exp(scores - jnp.max(scores, -1, keepdims=True))
    return raised * (1.0 / jnp.sum(raised, -1, keepdims=True))


def lane_pairs(width):
    for pair in range(width // LANES):
        yield [slice(at + pair * LANES, at + (pair + 1) * LANES) for at in (0, width, 2 * width)]


def heads_of(pair):
    return [pair[:, at : at + HEAD_DIM] for at in range(0, LANES, HEAD_DIM)]


def attend_kernel(project_ref, mask_ref, out_ref):
    mask = mask_ref[0]
    for places in lane_pairs(out_ref.shape[2]):
        query, keys, values = (heads_of(project_ref[0, :, at]) for at in places)
        parts = [
            product(head_probs(q, k, mask).astype(BF16), u, 1, 0).astype(BF16)
            for q, k, u in zip(query, keys, values)
        ]
        out_ref[0, :, places[0]] = jnp.concatenate(parts, 1)


def attend(project, mask, later_than=()):
    images, tokens, wide = project.shape
    width = wide // 3
    return run(
        attend_kernel,
        (project, mask[:, None, :]),
        [
            pl.BlockSpec((1, tokens, wide), lambda i: (i, 0, 0)),
            pl.BlockSpec((1, 1, tokens), lambda i: (i, 0, 0)),
        ],
        48,
        later_than,
        grid=(images,),
        out_specs=pl.BlockSpec((1, tokens, width), lambda i: (i, 0, 0)),
        out_shape=jax.ShapeDtypeStruct((images, tokens, width), BF16),
    )


def attend_back_kernel(project_ref, mask_ref, upstream_ref, out_ref):
    mask = mask_ref[0]
    scale = HEAD_DIM**-0.5
    for places in lane_pairs(upstream_ref.shape[2]):
        query, keys, values = (heads_of(project_ref[0, :, at]) for at in places)
        upstream = heads_of(upstream_ref[0, :, places[0]])
        grads = ([], [], [])
        for q, k, u, d in zip(query, keys, values, upstream):
            exact = head_probs(q, k, mask)
            grad_probs = product(d, u, 1, 1)
            held = jnp.sum(grad_probs * exact, -1, keepdims=True)
            grad_scores = (exact * (grad_probs - held)).astype(BF16)
            grads[0].append((product(grad_scores, k, 1, 0) * scale).astype(BF16))
            grads[1].append((product(grad_scores, q, 0, 0) * scale).astype(BF16))
            grads[2].append(product(exact.astype(BF16), d, 0, 0).astype(BF16))
        for at, parts in zip(places, grads):
            out_ref[0, :, at] = jnp.concatenate(parts, 1)


def attend_back(project, mask, upstream, later_than=()):
    images, tokens, wide = project.shape
    width = wide // 3
    whole = pl.BlockSpec((1, tokens, wide), lambda i: (i, 0, 0))
    return run(
        attend_back_kernel,
        (project, mask[:, None, :], upstream),
        [
            whole,
            pl.BlockSpec((1, 1, tokens), lambda i: (i, 0, 0)),
            pl.BlockSpec((1, tokens, width), lambda i: (i, 0, 0)),
        ],
        48,
        later_than,
        grid=(images,),
        out_specs=whole,
        out_shape=jax.ShapeDtypeStruct(project.shape, BF16),
    )


def residual_kernel(feature_ref, branch_ref, gain_ref, out_ref, pooled_ref, rows):
    total = feature_ref[0].astype(F32) + gain_ref[0] * branch_ref[0].astype(F32)
    out_ref[0] = total.astype(BF16)
    groups = total.shape[0] // 4
    for group in range(groups):
        for part in range(3):
            fine = 4 * group + part
            rows[3 * group + part] = 0.5 * (total[fine] + total[fine + 1])
    columns = [rows[:, pl.ds(part, groups, stride=4), :] for part in range(4)]
    for part in range(3):
        pooled_ref[0, :, pl.ds(part, groups, stride=3), :] = 0.5 * (columns[part] + columns[part + 1])


def residual_and_pool(feature, branch, gain, later_than=()):
    images, fine, _, channels = feature.shape
    coarse = fine // 4 * 3
    block = pl.BlockSpec((1, fine, fine, LANES), lambda n, c: (n, 0, 0, c))
    out, pooled = run(
        residual_kernel,
        (feature, branch, gain[None]),
        [block, block, pl.BlockSpec((1, LANES), lambda n, c: (0, c))],
        32,
        later_than,
        grid=(images, channels // LANES),
        out_specs=[block, pl.BlockSpec((1, coarse, coarse, LANES), lambda n, c: (n, 0, 0, c))],
        out_shape=[
            jax.ShapeDtypeStruct(feature.shape, BF16),
            jax.ShapeDtypeStruct((images, coarse, coarse, channels), F32),
        ],
        scratch_shapes=[pltpu.VMEM((coarse, fine, LANES), F32)],
    )
    return (out, pooled.astype(BF16))


def spread_back_kernel(pooled_ref, upstream_ref, gain_ref, out_ref, scaled_ref, rows):
    groups = upstream_ref.shape[1] // 4
    columns = [pooled_ref[0, :, pl.ds(part, groups, stride=3), :] for part in range(3)]
    for part in range(4):
        near = [columns[at] for at in (part - 1, part) if 0 <= at < 3]
        rows[:, pl.ds(part, groups, stride=4), :] = 0.5 * sum(near[1:], near[0])
    for group in range(groups):
        for part in range(4):
            near = [rows[3 * group + at] for at in (part - 1, part) if 0 <= at < 3]
            total = upstream_ref[0, 4 * group + part].astype(F32) + 0.5 * sum(near[1:], near[0])
            out_ref[0, 4 * group + part] = total
            scaled_ref[0, 4 * group + part] = (gain_ref[0] * total).astype(BF16)


def spread_back(pooled, upstream, gain, later_than=()):
    images, fine, _, channels = upstream.shape
    coarse = pooled.shape[1]
    block = pl.BlockSpec((1, fine, fine, LANES), lambda n, c: (n, 0, 0, c))
    return run(
        spread_back_kernel,
        (pooled, upstream, gain[None]),
        [
            pl.BlockSpec((1, coarse, coarse, LANES), lambda n, c: (n, 0, 0, c)),
            block,
            pl.BlockSpec((1, LANES), lambda n, c: (0, c)),
        ],
        32,
        later_than,
        grid=(images, channels // LANES),
        out_specs=[block, block],
        out_shape=[
            jax.ShapeDtypeStruct(upstream.shape, F32),
            jax.ShapeDtypeStruct(upstream.shape, BF16),
        ],
        scratch_shapes=[pltpu.VMEM((coarse, fine, LANES), F32)],
    )


def add_kernel(kept_ref, got_ref, out_ref):
    out_ref[...] = (kept_ref[...].astype(F32) + got_ref[...].astype(F32)).astype(BF16)


def add_to_first_half(partial, got, later_than=()):
    rows, width = got.shape
    tile = math.gcd(rows, 256)
    if tile % 16:
        return (partial[:rows].astype(F32) + got.astype(F32)).astype(BF16)
    block = pl.BlockSpec((tile, width), lambda i: (i, 0))
    return run(
        add_kernel,
        (partial, got),
        [block, block],
        32,
        later_than,
        grid=(rows // tile,),
        out_specs=block,
        out_shape=jax.ShapeDtypeStruct(got.shape, BF16),
    )


class Held:
    def __init__(self, **arrays):
        self.add(**arrays)

    def add(self, **arrays):
        vars(self).update(arrays)


def traded(array, axis, bit):
    return lax.ppermute(array, axis, [(i, i ^ bit) for i in range(lax.axis_size(axis))])


def bits_of(axis):
    return [1 << k for k in range((lax.axis_size(axis) - 1).bit_length())]


def total_over(values, axis):
    for bit in bits_of(axis):
        values = values + traded(values, axis, bit)
    return values


def first_section():
    return lax.axis_index(PIPE) == 0


def select(former, latter):
    return jnp.where(first_section(), former, latter)


def halves_of(own, axis):
    half = own.shape[axis] // 2
    odd = lax.axis_index(DP) % 2
    return lax.dynamic_slice_in_dim(own, odd * half, half, axis)


def joined(mine, theirs, axis):
    even = lax.axis_index(DP) % 2 == 0
    return jnp.concatenate([jnp.where(even, mine, theirs), jnp.where(even, theirs, mine)], axis)


class Trade:
    def __init__(self, own, *earlier):
        self.own = own
        self.got = traded(after(halves_of(own, 0), *earlier), PIPE, 1)

    def share(self, *earlier):
        self.got = after(self.got, *earlier)
        self.rest = traded(self.got, DP, 1)

    def layers(self, *earlier):
        rest = after(self.rest, *earlier) if earlier else self.rest
        other = joined(self.got, rest, 0)
        return (select(self.own, other), select(other, self.own))


class QuarterTrade:
    def __init__(self, own, *earlier):
        size = own.shape[0] // QUARTERS
        sent = lax.dynamic_slice_in_dim(own, lax.axis_index(DP) % QUARTERS * size, size, 0)
        self.own = own
        self.got = traded(after(sent, *earlier), PIPE, 1)

    def share(self, *earlier):
        self.got = after(self.got, *earlier)
        self.pair = traded(self.got, DP, 2)

    def share_again(self, *earlier):
        self.pair = after(self.pair, *earlier)
        self.rest = traded(jnp.concatenate([self.got, self.pair], 0), DP, 1)

    def pieces(self):
        return (self.own, self.got, self.pair, self.rest)


def small_pair(own):
    other = traded(own, PIPE, 1)
    return (select(own, other), select(other, own))


def own_block(values, count, axis):
    return lax.dynamic_slice_in_dim(values, lax.axis_index(TENSOR) * count, count, axis)


def widen(values, whole, axis):
    shape = list(values.shape)
    shape[axis] = whole
    empty = jnp.zeros(tuple(shape), F32)
    return lax.dynamic_update_slice_in_dim(
        empty, values, lax.axis_index(TENSOR) * values.shape[axis], axis
    )


def gather(values):
    return lax.all_gather(values, TENSOR, axis=1, tiled=True)


def turned(values, by):
    count = lax.axis_size(TENSOR)
    return lax.ppermute(values, TENSOR, [(i, (i + by) % count) for i in range(count)])


def ring_total(values):
    count = lax.axis_size(TENSOR)
    return sum([turned(values, k) for k in range(1, count)], values)


def in_order(blocks, axis):
    count = len(blocks)
    size = blocks[0].shape[axis]
    start = (count - 1 - lax.axis_index(TENSOR)) * size
    joined = jnp.concatenate(blocks[::-1] + blocks[:0:-1], axis)
    return lax.dynamic_slice_in_dim(joined, start, count * size, axis)


def exchanged(values, split_axis, concat_axis):
    count = lax.axis_size(TENSOR)
    index = lax.axis_index(TENSOR)
    size = values.shape[split_axis] // count
    blocks = []
    for k in range(count):
        start = (index + k) % count * size
        block = lax.dynamic_slice_in_dim(values, start, size, split_axis)
        blocks.append(turned(block, k) if k else block)
    return in_order(blocks, concat_axis)


def ring_gather(values):
    blocks = [turned(values, k) if k else values for k in range(lax.axis_size(TENSOR))]
    return in_order(blocks, 1)


def tokens_to_holders(values):
    return exchanged(values, 1, 2)


def features_to_holders(values):
    return exchanged(values, 2, 1)


def scatter_tokens(values):
    return lax.psum_scatter(values, TENSOR, scatter_dimension=1, tiled=True).astype(F32)


def scatter_parts(parts):
    return lax.psum_scatter(parts, TENSOR, scatter_dimension=0, tiled=False).astype(F32)


def relative_order(count):
    width = (count - 1).bit_length()
    return sorted(range(count), key=lambda r: format(r, f"0{width}b")[::-1])


def by_relative(values, axis=DP):
    count = lax.axis_size(axis)
    index = lax.axis_index(axis)
    block = values.shape[1] // count
    return jnp.concatenate(
        [
            lax.dynamic_slice_in_dim(values, (index ^ r) * block, block, 1)
            for r in relative_order(count)
        ],
        1,
    )


def inner(left, right, *earlier):
    left = by_relative(left)
    if earlier:
        left = after(left, *earlier)
    return product(left, right, 0, 0).astype(BF16)


class Reduction:
    def __init__(self, partial, also_tensor=False):
        self.partial = partial
        self.steps_left = 4 if also_tensor else 2
        self.moves = [(DP, bit, 0) for bit in bits_of(DP)]
        if also_tensor:
            self.moves += [(TENSOR, bit, 1) for bit in bits_of(TENSOR)]
        self.send()

    def send(self):
        name, bit, axis = self.moves.pop(0)
        size = self.partial.shape[axis] // 2
        self.got = traded(lax.slice_in_dim(self.partial, size, 2 * size, axis=axis), name, bit)

    def step(self, *earlier):
        halvings = -(-(len(self.moves) + 1) // self.steps_left)
        self.steps_left -= 1
        for _ in range(halvings):
            self.partial = add_to_first_half(self.partial, self.got, earlier)
            if self.moves:
                self.send()
        return self.partial


class Sections:
    def __init__(self, former, latter):
        self.kept = select(former, latter)
        self.got = traded(select(latter, former), PIPE, 1)

    def total(self, *earlier):
        got = after(self.got, *earlier) if earlier else self.got
        return self.kept.astype(F32) + got.astype(F32)


def over_sections(former, latter):
    kept, sent = (select(former, latter), select(latter, former))
    return kept.astype(F32) + traded(sent, PIPE, 1).astype(F32)


def norm_rows(values, epsilon):
    centred = values - jnp.mean(values, -1, keepdims=True)
    inverse = lax.rsqrt(jnp.mean(centred * centred, -1, keepdims=True) + epsilon)
    return (centred * inverse, inverse)


def norm_back(upstream, scaled, inverse, gains):
    weighted = upstream * gains
    return inverse * (
        weighted
        - jnp.mean(weighted, -1, keepdims=True)
        - scaled * jnp.mean(weighted * scaled, -1, keepdims=True)
    )


def flat(values):
    return values.reshape(-1, values.shape[-1])


def placing(places):
    cells = jnp.arange(places.shape[1])
    return (places[:, :, None] == cells[None, None, :]).astype(BF16)


def conv_norm(grid, w, later_than=()):
    own = grid.shape[-1]
    channels = own * lax.axis_size(TENSOR)
    mixed = flat(depthwise(grid, w.dw, 7, later_than=later_than))
    sums = ring_total(jnp.stack([jnp.sum(mixed, -1), jnp.sum(mixed * mixed, -1)]))
    centre = sums[0] / channels
    inverse = lax.rsqrt(sums[1] / channels - centre * centre + 1e-06)
    scaled = (mixed - centre[:, None]) * inverse[:, None]
    normed = (scaled * w.gain[0] + w.shift).astype(BF16)
    return (normed, Held(grid=grid, scaled=scaled, inverse=inverse))


def conv_residual(grid, branch, w, *earlier):
    own = grid.shape[-1]
    channels = own * lax.axis_size(TENSOR)
    out, pooled = residual_and_pool(grid, branch.reshape(grid.shape), w.gain[1], earlier)
    exact = grid.astype(F32) + w.gain[1] * branch.reshape(grid.shape).astype(F32)
    square = jnp.sum(exact * exact, -1).reshape(grid.shape[0], -1)
    return (out, flat(pooled), square / channels)


def adapter_forward(stream, pooled, places, w, *earlier):
    images, tokens, _ = places.shape
    side = math.isqrt(tokens)
    pooled_rows = tokens_to_holders(pooled.reshape(images, tokens, -1))
    adapted_rows = product(flat(pooled_rows), w.proj, 1, 0).astype(BF16)
    adapted = features_to_holders(adapted_rows.reshape(pooled_rows.shape[:2] + (-1,)))
    adapted = adapted.reshape(images, side, side, -1)
    spread = depthwise(adapted, w.taps, 3, later_than=earlier).reshape(images, tokens, -1)
    gated = (jnp.tanh(w.gate) * spread).astype(BF16)
    picked = jnp.einsum("ntc,ncw->ntw", places, gated, preferred_element_type=F32).astype(BF16)
    stream_in = stream + tokens_to_holders(picked).astype(F32)
    return (stream_in, Held(pooled=flat(pooled_rows), adapted=adapted, spread=spread))


def vit_norm(stream, w, which):
    scaled, inverse = norm_rows(stream, 1e-05)
    normed = (scaled * w.vit_gain[which] + w.vit_shift[which]).astype(BF16)
    return (normed, scaled, inverse)


def vit_attention(normed, key_mask, w, *earlier):
    images, tokens, width = normed.shape
    project = product(flat(normed), w.qkv, 1, 0).astype(BF16).reshape(images, tokens, -1)
    attended = attend(project, key_mask, earlier)
    held = tokens_to_holders(attended)
    return (project, flat(held), product(flat(held), w.attn, 1, 0).reshape(held.shape))


def vit_attention_back(grad_own, kept, key_mask, w, *earlier):
    images, _, width = grad_own.shape
    grad_attended = product(flat(grad_own), w.attn, 1, 1).astype(BF16)
    grad_attended = features_to_holders(grad_attended.reshape(grad_own.shape))
    grad_project = flat(attend_back(kept.project, key_mask, grad_attended, earlier))
    partial = product(grad_project, w.qkv, 1, 1).astype(BF16)
    return (grad_project, partial.reshape(images, -1, width))


def adapter_backward(grad_cols, kept, places, w, later_than=()):
    images, tokens, _ = places.shape
    side = math.isqrt(tokens)
    grad_placed = jnp.einsum("ntc,ntw->ncw", places, grad_cols, preferred_element_type=F32)
    gate_value = jnp.tanh(w.gate)
    gate = jnp.sum(grad_placed * kept.spread, (0, 1)) * (1.0 - gate_value * gate_value)
    grad_spread = (grad_placed * gate_value).reshape(images, side, side, -1)
    grad_adapted = flat(
        depthwise(
            grad_spread, w.taps, 3, reverse=True, dtype=BF16, later_than=later_than
        )
    )
    grad_rows = tokens_to_holders(grad_adapted.reshape(images, tokens, -1))
    grad_pooled = product(flat(grad_rows), w.proj, 1, 1).astype(BF16)
    grad_pooled = features_to_holders(grad_pooled.reshape(grad_rows.shape[:2] + (-1,)))
    taps = depthwise_taps(kept.adapted, grad_spread, 3, later_than=(grad_adapted,))
    grad_pooled = grad_pooled.astype(F32).reshape(images, side, side, -1)
    return (flat(grad_rows), grad_pooled, taps, gate)


def conv_norm_back(grad_normed, kept, w):
    grid = kept.grid
    channels = grid.shape[-1] * lax.axis_size(TENSOR)
    scaled = kept.scaled
    weighted = grad_normed * w.gain[0]
    sums = ring_total(jnp.stack([jnp.sum(weighted, -1), jnp.sum(weighted * scaled, -1)]))
    grad_mixed = kept.inverse[:, None] * (
        weighted - sums[0][:, None] / channels - scaled * (sums[1][:, None] / channels)
    )
    gain = jnp.sum(grad_normed * scaled, 0)
    shift = jnp.sum(grad_normed, 0)
    return (grad_mixed.reshape(grid.shape), gain, shift)


def body(
    x_vit,
    x_conv,
    positions,
    valid,
    qkv_weight,
    attn_weight,
    fc_in,
    fc_out,
    vit_gains,
    vit_shifts,
    pw_in,
    pw_out,
    dw_kernel,
    conv_gains,
    conv_shift,
    proj_weight,
    taps,
    gate,
    dy_vit,
    dy_conv,
):
    here = x_vit.shape[0] // lax.axis_size(PIPE)
    count = lax.axis_size(TENSOR)
    cells = x_conv.shape[1]
    own_channels = x_conv.shape[2]
    conv_side = math.isqrt(cells)
    own_width = attn_weight.shape[1]
    own_units = fc_out.shape[1]
    conv_units = pw_out.shape[1]
    channels = pw_out.shape[2]
    model_width = vit_gains.shape[2]
    tap_count = dw_kernel.shape[1]
    side = taps.shape[1]
    tile = cells // 2

    def portion(source):
        return lax.dynamic_slice_in_dim(source, lax.axis_index(PIPE) * here, here, 0)

    conv_small = small_pair(jnp.concatenate([dw_kernel[0], conv_gains[0], conv_shift], 0))
    trade_in = QuarterTrade(pw_in[0], conv_small[0])
    vit_small = small_pair(
        after(jnp.concatenate([taps[0], gate, vit_gains[0], vit_shifts[0]], 0), conv_small[0])
    )
    weights = [Held(), Held()]
    for layer in range(2):
        conv, vit = (conv_small[layer], vit_small[layer])
        weights[layer].add(
            dw=conv[:tap_count],
            gain=conv[tap_count : tap_count + 2],
            shift=conv[tap_count + 2],
            taps=own_block(vit[:side], own_width, 1),
            gate=own_block(vit[side], own_width, 0),
            vit_gain=vit[side + 1 : side + 3],
            vit_shift=vit[side + 3 :],
        )
    w0, w1 = weights

    def take(**pairs):
        for name, pair in pairs.items():
            for w, weight in zip(weights, pair):
                w.add(**{name: weight})

    def both_images(former, latter, *earlier):
        mine, theirs = (select(former, latter), select(latter, former))
        sent = theirs.astype(BF16) if theirs.ndim > 3 else theirs
        if earlier:
            sent = after(sent, *earlier)
        got = traded(sent, PIPE, 1).astype(mine.dtype)
        return jnp.concatenate([select(mine, got), select(got, mine)], 0)

    stream = portion(x_vit)
    grid0 = portion(x_conv).reshape(here, conv_side, conv_side, own_channels)
    grad_top = portion(dy_vit)
    grad_top_full = gather(grad_top)
    attn_half = lax.all_gather(halves_of(attn_weight[0], 1), TENSOR, axis=0, tiled=True)
    places = placing(portion(positions))
    key_mask = portion(valid)

    normed0, conv0 = conv_norm(grid0, w0)
    conv0.normed = gather(after(normed0, grad_top_full, attn_half))
    trade_in.share(normed0)
    trade_out = QuarterTrade(pw_out[0], trade_in.got)
    trade_in.share_again()
    first = trade_in.pieces()
    trade_out.share(trade_in.pair)
    trade_proj = Trade(proj_weight[0], trade_out.got)
    trade_out.share_again(trade_proj.got)
    second = trade_out.pieces()
    (conv0.hidden, conv0.slope), parts = wide_mlp(0, conv0.normed, first, second, tile)
    branch = scatter_parts(parts)
    conv0.branch = branch
    trade_proj.share(parts)
    trade_qkv = Trade(qkv_weight[0].reshape(model_width, -1), parts)
    trade_fc_in = Trade(fc_in[0], parts)
    grid1, pooled0, square0 = conv_residual(
        grid0, branch, w0, trade_qkv.got, trade_fc_in.got
    )
    trade_fc_out = Trade(fc_out[0], pooled0)
    take(proj=trade_proj.layers())
    trade_qkv.share(pooled0)

    normed1, conv1 = conv_norm(grid1, w1, (pooled0,))
    conv1.normed = gather(normed1)
    take(qkv=trade_qkv.layers(normed1))
    stream_in0, vit0 = adapter_forward(stream.astype(F32), pooled0, places, w0, normed1, w0.qkv)
    normed_a0, vit0.scaled_a, vit0.inverse_a = vit_norm(stream_in0, w0, 0)
    vit0.normed_a = gather(normed_a0)
    trade_fc_in.share(normed_a0)
    trade_fc_out.share(normed_a0)
    (conv1.hidden, conv1.slope), parts = wide_mlp(
        1, conv1.normed, first, second, tile, None, (normed_a0, trade_fc_out.got)
    )
    branch = scatter_parts(parts)
    conv1.branch = branch
    attn_got = traded(after(attn_half, parts), PIPE, 1)
    attn_halves = jnp.stack([attn_half, attn_got])
    attn_rest = traded(attn_halves, DP, 1)
    attn_full = [joined(mine, theirs, 1) for mine, theirs in zip(attn_halves, attn_rest)]
    take(attn=(select(*attn_full), select(*attn_full[::-1])))
    take(fc_in=trade_fc_in.layers(parts))
    take(fc_out=trade_fc_out.layers(parts))
    vit0.project, vit0.attended, moved = vit_attention(
        vit0.normed_a, key_mask, w0, parts
    )
    stream_mid0 = stream_in0 + moved
    normed_b0, vit0.scaled_b, vit0.inverse_b = vit_norm(stream_mid0, w0, 1)
    vit0.normed_b = gather(normed_b0)
    grid2, pooled1, square1 = conv_residual(grid1, branch, w1)
    vit0.hidden, vit0.slope, partial = mlp(
        flat(vit0.normed_b), w0.fc_in, w0.fc_out, (pooled1,)
    )
    stream_out0 = stream_mid0 + scatter_tokens(partial.reshape(stream_shape(vit0)))
    stream1 = stream_out0.astype(BF16)

    stream_in1, vit1 = adapter_forward(stream1.astype(F32), pooled1, places, w1, partial)
    normed_a1, vit1.scaled_a, vit1.inverse_a = vit_norm(stream_in1, w1, 0)
    vit1.normed_a = gather(normed_a1)
    vit1.project, vit1.attended, moved = vit_attention(vit1.normed_a, key_mask, w1)
    stream_mid1 = stream_in1 + moved
    out_conv = both_images(grid1, grid2, normed_a1).reshape(1, -1, cells, own_channels)
    normed_b1, vit1.scaled_b, vit1.inverse_b = vit_norm(stream_mid1, w1, 1)
    vit1.normed_b = gather(normed_b1)
    vit1.hidden, vit1.slope, top_partial = mlp(
        flat(vit1.normed_b), w1.fc_in, w1.fc_out, (out_conv,)
    )

    norm_sums = [None, None]
    tap_sums = [None, None]

    def back_to_middle(grad_out, grad_full, kept, w, beside, *earlier):
        grad_hidden, partial = mlp_back(
            flat(grad_full), kept.slope, w.fc_in, w.fc_out, earlier
        )
        grad_normed = scatter_tokens(partial.reshape(stream_shape(kept)))
        packed = jnp.concatenate(
            [
                inner(flat(kept.normed_b), grad_hidden, partial),
                inner(flat(grad_full), kept.hidden, partial),
            ],
            1,
        )
        grad_normed = after(grad_normed, packed, *beside(partial))
        sums = [jnp.sum(grad_normed * kept.scaled_b, (0, 1)), jnp.sum(grad_normed, (0, 1))]
        grad_mid = grad_out.astype(F32) + norm_back(
            grad_normed, kept.scaled_b, kept.inverse_b, w.vit_gain[1]
        )
        return (grad_mid, Reduction(packed), sums)

    def back_to_start(grad_mid, grad_own, kept, w, beside, *earlier):
        grad_project, partial = vit_attention_back(grad_own, kept, key_mask, w, *earlier)
        grad_normed = scatter_tokens(partial)
        qkv = inner(flat(kept.normed_a), grad_project, partial)
        grad_normed = after(grad_normed, qkv, *beside(partial))
        sums = [jnp.sum(grad_normed * kept.scaled_a, (0, 1)), jnp.sum(grad_normed, (0, 1))]
        grad_in = grad_mid + norm_back(
            grad_normed, kept.scaled_a, kept.inverse_a, w.vit_gain[0]
        )
        return (grad_in, qkv, sums)

    def row_grads(kept, grad_rows, grad_own, *earlier):
        sides = lax.axis_size(DP)
        pairs = [
            product(by_relative(left), after(right, *earlier), 0, 0)
            for left, right in ((kept.pooled, grad_rows), (flat(grad_own), kept.attended))
        ]
        blocks = [pair.astype(BF16).reshape(sides, -1, model_width) for pair in pairs]
        return jnp.concatenate(blocks, 1).reshape(-1, model_width)

    def step_all(reductions, *earlier):
        return [reduction.step(*earlier) for reduction in reductions]

    grad_mid1, mlp1, sums_b1 = back_to_middle(
        grad_top, grad_top_full, vit1, w1, lambda partial: (), top_partial
    )
    grad_mid1_own = grad_mid1.astype(BF16)

    def beside_start1(partial):
        mlp1.step(partial)
        return [mlp1.step(partial)]

    grad_in1, qkv1, sums_a1 = back_to_start(grad_mid1, grad_mid1_own, vit1, w1, beside_start1)
    norm_sums[1] = jnp.stack([sums_a1[0], sums_b1[0], sums_a1[1], sums_b1[1]])
    grad_stream = grad_in1.astype(BF16)
    grad_stream_full = gather(grad_stream)
    grad_rows1, grad_pooled1, tap_sum, gate_sum = adapter_backward(
        features_to_holders(grad_stream), vit1, places, w1
    )
    tap_sums[1] = jnp.concatenate([tap_sum, gate_sum[None]], 0)

    squares = total_over(both_images(square0, square1, grad_mid1_own), TENSOR)
    rms_conv = jnp.sqrt(squares)[None]
    grad_map1, scaled1 = spread_back(
        grad_pooled1, portion(dy_conv).reshape(grid0.shape), w1.gain[1], (rms_conv,)
    )
    grad_branch1 = gather(flat(scaled1))
    grad_mid0, mlp0, sums_b0 = back_to_middle(
        grad_stream, grad_stream_full, vit0, w0, lambda partial: (), scaled1
    )
    rows1 = Reduction(row_grads(vit1, grad_rows1, grad_mid1_own, scaled1))
    grad_mid0_own = grad_mid0.astype(BF16)
    rows1.step(grad_mid0_own)
    grad_in0, qkv0, sums_a0 = back_to_start(
        grad_mid0, grad_mid0_own, vit0, w0, lambda partial: ()
    )
    (grad_hidden1,), parts = wide_mlp(
        1, grad_branch1, first, second, tile, conv1.slope, (grad_mid0_own, rows1.partial)
    )
    grad_normed1 = scatter_parts(parts)
    conv_in1 = Reduction(inner(conv1.normed, grad_hidden1, parts))
    conv_out1 = Reduction(inner(grad_branch1, conv1.hidden, parts))
    norm_sums[0] = jnp.stack([sums_a0[0], sums_b0[0], sums_a0[1], sums_b0[1]])
    grad_last = grad_in0.astype(BF16)
    qkv = Reduction(jnp.concatenate([qkv0, qkv1], 1))
    grad_mixed1, gain1, shift1 = conv_norm_back(grad_normed1, conv1, w1)
    mlp0.step(grad_last)
    rows1.step(grad_last)
    qkv.step(grad_last)
    grad_rows0, grad_pooled0, tap_sum, gate_sum = adapter_backward(
        features_to_holders(grad_last), vit0, places, w0, (conv_in1.partial, conv_out1.partial)
    )
    tap_sums[0] = jnp.concatenate([tap_sum, gate_sum[None]], 0)
    ready = step_all([conv_out1, conv_in1], conv_in1.partial, conv_out1.partial)
    grad_grid1 = depthwise(
        grad_mixed1, w1.dw, 7, grad_map1, True, F32, ready + [rows1.partial]
    )
    grad_next = grad_grid1.astype(BF16)

    ready = step_all([mlp0, qkv, conv_out1], grad_grid1)
    grad_map0, scaled0 = spread_back(grad_pooled0, grad_next, w0.gain[1], ready)
    grad_branch0 = gather(flat(scaled0))
    fc = Sections(after(mlp0.partial, scaled0), mlp1.partial)
    half = qkv.partial.shape[1] // 2
    sections_qkv = Sections(after(qkv.partial[:, :half], scaled0), qkv.partial[:, half:])
    rows0 = Reduction(row_grads(vit0, grad_rows0, grad_mid0_own, scaled0))
    grad_vit = both_images(grad_in0[None], grad_in1[None], scaled0)
    grad_vit = grad_vit.reshape((1, -1) + grad_in0.shape[1:])
    taps1 = depthwise_taps(conv1.grid, grad_mixed1, 7, later_than=(scaled0,))
    ready = step_all([conv_in1], taps1)
    rows0.step(*ready)
    (grad_hidden0,), parts = wide_mlp(
        0,
        grad_branch0,
        first,
        second,
        tile,
        conv0.slope,
        ready + [rows0.partial, fc.got, sections_qkv.got, grad_vit],
    )
    grad_normed0 = scatter_parts(parts)
    rows0.step(parts)
    conv_out0 = Reduction(inner(grad_branch0, conv0.hidden, rows0.partial))
    conv_in0 = Reduction(inner(conv0.normed, grad_hidden0, conv_out0.partial))
    conv_out0.step(conv_in0.partial)
    conv_in0.step(conv_out0.partial)
    conv_out0.step(conv_in0.partial)
    grad_normed0 = after(grad_normed0, conv_out0.partial)
    row_parts = jnp.concatenate([rows0.partial, rows1.partial], 0)
    row_parts = row_parts.reshape(row_parts.shape[0], count, -1).swapaxes(0, 1)
    row_sums = lax.psum_scatter(
        after(row_parts, grad_normed0), TENSOR, scatter_dimension=0, tiled=False
    )
    grad_mixed0, gain0, shift0 = conv_norm_back(grad_normed0, conv0, w0)
    conv_in0.step(conv_out0.partial)
    grad_grid0 = depthwise(
        grad_mixed0, w0.dw, 7, grad_map0, True, F32, (conv_in0.partial,)
    )
    conv_out = Sections(conv_out0.partial, conv_out1.partial)
    grad_conv = both_images(grad_grid0, grad_grid1)
    conv_in = Sections(conv_in0.partial, conv_in1.partial)
    taps0 = depthwise_taps(conv0.grid, grad_mixed0, 7, later_than=(grad_grid0,))
    stream_out1 = stream_mid1 + scatter_tokens(
        after(top_partial, row_sums).reshape(stream_shape(vit1))
    )
    grad_fc = fc.total(taps0)
    grad_qkv = sections_qkv.total(taps0)
    grad_conv_out = conv_out.total(taps0)
    row_blocks = jnp.split(row_sums, 2, 0)
    grad_proj_attn = over_sections(after(row_blocks[0], taps0), row_blocks[1])
    grad_conv_in = conv_in.total(taps0)
    proj_rows = channels // lax.axis_size(DP)
    scale1 = jnp.sum(flat(grad_map1) * conv1.branch, 0)
    scale0 = jnp.sum(flat(grad_map0) * conv0.branch, 0)

    def over_images(pair):
        return total_over(select(*pair) + traded(select(*pair[::-1]), PIPE, 1), DP)

    token_terms = [
        jnp.concatenate(
            [
                widen(after(tap_sums[layer], grad_grid0), model_width, 1),
                after(norm_sums[layer], grad_grid0),
            ],
            0,
        )
        for layer in range(2)
    ]
    token_terms = total_over(jnp.concatenate(token_terms, 0), TENSOR)

    def rows_of_lanes(values):
        return values.reshape(-1, LANES)

    column_terms = [
        jnp.concatenate([taps0, jnp.stack([gain0, scale0, shift0])], 0),
        jnp.concatenate([taps1, jnp.stack([gain1, scale1, shift1])], 0),
    ]
    token_rows = side + 5
    column_sums, token_sums = jnp.split(
        over_images(
            [
                jnp.concatenate(
                    [
                        rows_of_lanes(columns),
                        rows_of_lanes(token_terms[layer * token_rows : (layer + 1) * token_rows]),
                    ],
                    0,
                )
                for layer, columns in enumerate(column_terms)
            ]
        ),
        [column_terms[0].size // LANES],
    )
    column_sums = column_sums.reshape(column_terms[0].shape)
    token_sums = token_sums.reshape(token_rows, model_width)

    out_vit = both_images(stream1, stream_out1.astype(BF16))[None]
    mean_squares = [jnp.mean(out * out, -1) for out in (stream_out0, stream_out1)]
    rms_vit = jnp.sqrt(both_images(*mean_squares))[None]
    return (
        out_vit,
        out_conv,
        grad_vit,
        grad_conv.reshape(1, -1, cells, own_channels),
        rms_vit,
        rms_conv,
        grad_qkv.reshape(1, -1, 3, own_width),
        grad_proj_attn[proj_rows:].T[None],
        grad_fc[:, :own_units][None],
        grad_fc[:, own_units:].T[None],
        token_sums[side + 1 : side + 3][None],
        token_sums[side + 3 :][None],
        grad_conv_in[None],
        grad_conv_out.T[None],
        column_sums[:tap_count][None],
        column_sums[tap_count : tap_count + 2][None],
        column_sums[tap_count + 2 :],
        grad_proj_attn[:proj_rows][None],
        token_sums[:side][None],
        token_sums[side][None],
    )


def stream_shape(kept):
    return kept.normed_b.shape


def solution(mesh):
    return jax.shard_map(
        body,
        mesh=mesh,
        in_specs=(
            P(DP, TENSOR, None),
            P(DP, None, TENSOR),
            P(DP, None),
            P(DP, None),
            P(PIPE, None, None, TENSOR),
            P(PIPE, TENSOR, None),
            P(PIPE, None, TENSOR),
            P(PIPE, TENSOR, None),
            P(PIPE, None, None),
            P(PIPE, None, None),
            P(PIPE, None, TENSOR),
            P(PIPE, TENSOR, None),
            P(PIPE, None, TENSOR),
            P(PIPE, None, TENSOR),
            P(PIPE, TENSOR),
            P(PIPE, None, None),
            P(PIPE, None, None),
            P(PIPE, None),
            P(DP, TENSOR, None),
            P(DP, None, TENSOR),
        ),
        out_specs=(
            P(PIPE, DP, TENSOR, None),
            P(PIPE, DP, None, TENSOR),
            P(PIPE, DP, TENSOR, None),
            P(PIPE, DP, None, TENSOR),
            P(PIPE, DP, TENSOR),
            P(PIPE, DP, None),
            P(PIPE, DP, None, TENSOR),
            P(PIPE, TENSOR, DP),
            P(PIPE, DP, TENSOR),
            P(PIPE, TENSOR, DP),
            P(PIPE, None, None),
            P(PIPE, None, None),
            P(PIPE, DP, TENSOR),
            P(PIPE, TENSOR, DP),
            P(PIPE, None, TENSOR),
            P(PIPE, None, TENSOR),
            P(PIPE, TENSOR),
            P(PIPE, DP, TENSOR),
            P(PIPE, None, None),
            P(PIPE, None),
        ),
        check_vma=False,
    )
```

```python
import functools
import math

import jax
import jax.numpy as jnp
from jax import lax
from jax.experimental import pallas as pl
from jax.experimental.pallas import tpu as pltpu
from jax.sharding import PartitionSpec as P

PIPE, DP, TENSOR = ("pipe", "dp", "tensor")
HEAD_DIM = 64
LANES = 128
MARGIN = 8
BAND = 4
F32 = jnp.float32
BF16 = jnp.bfloat16


def product(left, right, left_axis, right_axis):
    return lax.dot_general(
        left, right, (((left_axis,), (right_axis,)), ((), ())), preferred_element_type=F32
    )


ANYWHERE = pl.BlockSpec(memory_space=pl.ANY)


def settings(mebibytes):
    return pltpu.CompilerParams(vmem_limit_bytes=mebibytes << 20)


def run(kernel, args, in_specs, mebibytes, later_than=(), **rest):
    count, extra = (len(args), len(later_than))

    def without_extra(*refs):
        kernel(*refs[:count], *refs[count + extra :])

    return pl.pallas_call(
        without_extra,
        in_specs=list(in_specs) + [ANYWHERE] * extra,
        compiler_params=settings(mebibytes),
        **rest,
    )(*args, *later_than)


def after(array, *earlier):
    def nothing(*refs):
        return None

    return pl.pallas_call(
        nothing,
        in_specs=[ANYWHERE] * (1 + len(earlier)),
        out_specs=ANYWHERE,
        out_shape=jax.ShapeDtypeStruct(array.shape, array.dtype),
        input_output_aliases={0: 0},
    )(array, *earlier)


def fill_padded(padded, values):
    extent = values.shape[0]
    half = (padded.shape[0] - extent) // 2
    padded[...] = jnp.zeros_like(padded)
    padded[half : half + extent, MARGIN : MARGIN + extent, :] = values.astype(F32)


def windows_of(padded, first, side, extent):
    for col in range(side):
        start = MARGIN - side // 2 + col
        yield col, padded[pl.ds(first, BAND + side - 1), pl.ds(start, extent), :]


def mix_kernel(side, reverse, with_base, *refs):
    x_ref, kernel_ref = refs[:2]
    out_ref, padded = refs[-2:]
    extent = x_ref.shape[1]
    fill_padded(padded, x_ref[0])

    def band(step, carry):
        first = step * BAND
        if with_base:
            total = refs[2][0, pl.ds(first, BAND)]
        else:
            total = jnp.zeros((BAND, extent, x_ref.shape[3]), F32)
        for col, window in windows_of(padded, first, side, extent):
            for row in range(side):
                tap = row * side + col
                weight = kernel_ref[side * side - 1 - tap if reverse else tap]
                total = total + window[row : row + BAND] * weight
        out_ref[0, pl.ds(first, BAND)] = total.astype(out_ref.dtype)
        return carry

    lax.fori_loop(0, extent // BAND, band, 0)


def depthwise(grid, kernel, side, base=None, reverse=False, dtype=F32, later_than=()):
    images, extent, _, channels = grid.shape
    block = pl.BlockSpec((1, extent, extent, LANES), lambda n, c: (n, 0, 0, c))
    taps = pl.BlockSpec((side * side, LANES), lambda n, c: (0, c))
    extra = () if base is None else (base,)
    return run(
        functools.partial(mix_kernel, side, reverse, base is not None),
        (grid, kernel) + extra,
        [block, taps] + [block] * len(extra),
        32,
        later_than,
        grid=(images, channels // LANES),
        out_specs=block,
        out_shape=jax.ShapeDtypeStruct(grid.shape, dtype),
        scratch_shapes=[pltpu.VMEM((extent + side - 1, extent + 2 * MARGIN, LANES), F32)],
    )


def taps_kernel(side, x_ref, upstream_ref, out_ref, padded, sums):
    extent = x_ref.shape[1]
    fill_padded(padded, x_ref[0])
    sums[...] = jnp.zeros_like(sums)

    def band(step, carry):
        first = step * BAND
        upstream = upstream_ref[0, pl.ds(first, BAND)]
        for col, window in windows_of(padded, first, side, extent):
            for row in range(side):
                part = window[row : row + BAND] * upstream
                sums[row * side + col] += jnp.sum(part.reshape(-1, 8, LANES), 0)
        return carry

    lax.fori_loop(0, extent // BAND, band, 0)
    out_ref[0] = jnp.sum(sums[...], 1)


def depthwise_taps(grid, upstream, side, later_than=()):
    images, extent, _, channels = grid.shape
    block = pl.BlockSpec((1, extent, extent, LANES), lambda n, c: (n, 0, 0, c))
    sums = run(
        functools.partial(taps_kernel, side),
        (grid, upstream),
        [block, block],
        32,
        later_than,
        grid=(images, channels // LANES),
        out_specs=pl.BlockSpec((1, side * side, LANES), lambda n, c: (n, 0, c)),
        out_shape=jax.ShapeDtypeStruct((images, side * side, channels), F32),
        scratch_shapes=[
            pltpu.VMEM((extent + side - 1, extent + 2 * MARGIN, LANES), F32),
            pltpu.VMEM((side * side, 8, LANES), F32),
        ],
    )
    return jnp.sum(sums, 0)


def gelu_and_slope(values):
    cumulative = 0.5 * (1.0 + lax.erf(values * (1.0 / math.sqrt(2.0))))
    density = jnp.exp(-0.5 * values * values) * (1.0 / math.sqrt(2.0 * math.pi))
    return ((values * cumulative).astype(BF16), (cumulative + values * density).astype(BF16))


def mlp_kernel(step, x_ref, first_ref, second_ref, hidden_ref, slope_ref, out_ref):
    x = x_ref[...]
    total = None
    for at in range(0, first_ref.shape[1], step):
        units = slice(at, at + step)
        hidden, slope = gelu_and_slope(product(x, first_ref[:, units], 1, 0))
        hidden_ref[:, units] = hidden
        slope_ref[:, units] = slope
        part = product(hidden, second_ref[units, :], 1, 0)
        total = part if total is None else total + part
    out_ref[...] = total.astype(BF16)


def mlp_back_kernel(step, upstream_ref, slope_ref, first_ref, second_ref, grad_ref, out_ref):
    upstream = upstream_ref[...]
    total = None
    for at in range(0, first_ref.shape[1], step):
        units = slice(at, at + step)
        grad = product(upstream, second_ref[units, :], 1, 1) * slope_ref[:, units].astype(F32)
        grad = grad.astype(BF16)
        grad_ref[:, units] = grad
        part = product(grad, first_ref[:, units], 1, 1)
        total = part if total is None else total + part
    out_ref[...] = total.astype(BF16)


QUARTERS = 4


def load_weight(meta_ref, sources, held_ref, semaphores):
    own, got, pair, rest = sources
    size = held_ref.shape[0] // QUARTERS
    rows = [pl.ds(k * size, size) for k in range(QUARTERS)]
    traded_quarters = [(got, 0, 0), (pair, 0, 2), (rest, 0, 1), (rest, 1, 3)]

    @pl.when(meta_ref[0] == 1)
    def _():
        for k in range(QUARTERS):
            pltpu.make_async_copy(
                own.at[rows[k]], held_ref.at[rows[k]], semaphores.at[k]
            ).start()

    @pl.when(meta_ref[0] != 1)
    def _():
        for k, (source, at, relative) in enumerate(traded_quarters):
            start = pl.multiple_of(lax.bitwise_xor(meta_ref[1], relative) * size, 16)
            pltpu.make_async_copy(
                source.at[rows[at]], held_ref.at[pl.ds(start, size)], semaphores.at[k]
            ).start()

    return [
        pltpu.make_async_copy(own.at[rows[k]], held_ref.at[rows[k]], semaphores.at[k])
        for k in range(QUARTERS)
    ]


def store_parts(out_ref, total):
    width = out_ref.shape[2]
    for part in range(out_ref.shape[0]):
        out_ref[part] = total[:, part * width : (part + 1) * width].astype(BF16)


def wide_mlp_kernel(back, step, meta_ref, *refs):
    inputs, refs = (refs[: 2 if back else 1], refs[2 if back else 1 :])
    sources, refs = ((refs[:4], refs[4:8]), refs[8:])
    inside, (out_ref, first_ref, second_ref, sems) = (refs[:-4], refs[-4:])

    @pl.when(pl.program_id(0) == 0)
    def _():
        copies = load_weight(meta_ref, sources[0], first_ref, sems.at[0])
        copies += load_weight(meta_ref, sources[1], second_ref, sems.at[1])
        for copy in copies:
            copy.wait()

    x = inputs[0][...]
    total = None
    for at in range(0, first_ref.shape[1], step):
        units = slice(at, at + step)
        if back:
            value = product(x, second_ref[units, :], 1, 1) * inputs[1][:, units].astype(F32)
            value = value.astype(BF16)
            part = product(value, first_ref[:, units], 1, 1)
        else:
            value, slope = gelu_and_slope(product(x, first_ref[:, units], 1, 0))
            inside[1][:, units] = slope
            part = product(value, second_ref[units, :], 1, 0)
        inside[0][:, units] = value
        total = part if total is None else total + part
    store_parts(out_ref, total)


def wide_mlp(layer, x, first, second, tile, slope=None, later_than=()):
    rows, units = (x.shape[0], first[0].shape[1])
    count = lax.axis_size(TENSOR)
    back = slope is not None
    meta = jnp.stack(
        [(lax.axis_index(PIPE) == layer).astype(jnp.int32), lax.axis_index(DP) % QUARTERS]
    )
    x_spec = pl.BlockSpec((tile, x.shape[1]), lambda i, s: (i, 0))
    units_spec = pl.BlockSpec((tile, units), lambda i, s: (i, 0))
    width = first[0].shape[0] // count
    inside = 1 if back else 2
    args = [x] + ([slope] if back else []) + list(first) + list(second)
    taken, extra = (len(args), len(later_than))
    kernel = functools.partial(wide_mlp_kernel, back, largest_step(units))

    def without_extra(meta_ref, *refs):
        kernel(meta_ref, *refs[:taken], *refs[taken + extra :])

    out = pl.pallas_call(
        without_extra,
        grid_spec=pltpu.PrefetchScalarGridSpec(
            num_scalar_prefetch=1,
            grid=(rows // tile,),
            in_specs=[x_spec] + [units_spec] * back + [ANYWHERE] * (8 + extra),
            out_specs=[units_spec] * inside
            + [pl.BlockSpec((count, tile, width), lambda i, s: (0, i, 0))],
            scratch_shapes=[
                pltpu.VMEM(first[0].shape, BF16),
                pltpu.VMEM(second[0].shape, BF16),
                pltpu.SemaphoreType.DMA((2, QUARTERS)),
            ],
        ),
        out_shape=[jax.ShapeDtypeStruct((rows, units), BF16)] * inside
        + [jax.ShapeDtypeStruct((count, rows, width), BF16)],
        compiler_params=settings(56),
    )(meta, *args, *later_than)
    return (out[:-1], out[-1])


def largest_step(units):
    return 512 if units % 512 == 0 else units


def mlp(x, first, second, later_than=()):
    rows, units = (x.shape[0], first.shape[1])
    args = (x, first, second)
    shapes = [(rows, units), (rows, units), (rows, second.shape[1])]
    return run(
        functools.partial(mlp_kernel, largest_step(units)),
        args,
        [pl.BlockSpec(arg.shape, lambda: (0, 0)) for arg in args],
        56,
        later_than,
        out_specs=[pl.BlockSpec(shape, lambda: (0, 0)) for shape in shapes],
        out_shape=[jax.ShapeDtypeStruct(shape, BF16) for shape in shapes],
    )


def mlp_back(upstream, slope, first, second, later_than=()):
    args = (upstream, slope, first, second)
    shapes = [slope.shape, (slope.shape[0], first.shape[0])]
    return run(
        functools.partial(mlp_back_kernel, largest_step(slope.shape[1])),
        args,
        [pl.BlockSpec(arg.shape, lambda: (0, 0)) for arg in args],
        56,
        later_than,
        out_specs=[pl.BlockSpec(shape, lambda: (0, 0)) for shape in shapes],
        out_shape=[jax.ShapeDtypeStruct(shape, BF16) for shape in shapes],
    )


def head_probs(query, keys, mask):
    scores = product(query, keys, 1, 1) * (HEAD_DIM**-0.5)
    scores = jnp.where(mask > 0, scores, -1000000000.0)
    raised = jnp.exp(scores - jnp.max(scores, -1, keepdims=True))
    return raised * (1.0 / jnp.sum(raised, -1, keepdims=True))


def lane_pairs(width):
    for pair in range(width // LANES):
        yield [slice(at + pair * LANES, at + (pair + 1) * LANES) for at in (0, width, 2 * width)]


def heads_of(pair):
    return [pair[:, at : at + HEAD_DIM] for at in range(0, LANES, HEAD_DIM)]


def attend_kernel(project_ref, mask_ref, out_ref):
    mask = mask_ref[0]
    for places in lane_pairs(out_ref.shape[2]):
        query, keys, values = (heads_of(project_ref[0, :, at]) for at in places)
        parts = [
            product(head_probs(q, k, mask).astype(BF16), u, 1, 0).astype(BF16)
            for q, k, u in zip(query, keys, values)
        ]
        out_ref[0, :, places[0]] = jnp.concatenate(parts, 1)


def attend(project, mask, later_than=()):
    images, tokens, wide = project.shape
    width = wide // 3
    return run(
        attend_kernel,
        (project, mask[:, None, :]),
        [
            pl.BlockSpec((1, tokens, wide), lambda i: (i, 0, 0)),
            pl.BlockSpec((1, 1, tokens), lambda i: (i, 0, 0)),
        ],
        48,
        later_than,
        grid=(images,),
        out_specs=pl.BlockSpec((1, tokens, width), lambda i: (i, 0, 0)),
        out_shape=jax.ShapeDtypeStruct((images, tokens, width), BF16),
    )


def attend_back_kernel(project_ref, mask_ref, upstream_ref, out_ref):
    mask = mask_ref[0]
    scale = HEAD_DIM**-0.5
    for places in lane_pairs(upstream_ref.shape[2]):
        query, keys, values = (heads_of(project_ref[0, :, at]) for at in places)
        upstream = heads_of(upstream_ref[0, :, places[0]])
        grads = ([], [], [])
        for q, k, u, d in zip(query, keys, values, upstream):
            exact = head_probs(q, k, mask)
            grad_probs = product(d, u, 1, 1)
            held = jnp.sum(grad_probs * exact, -1, keepdims=True)
            grad_scores = (exact * (grad_probs - held)).astype(BF16)
            grads[0].append((product(grad_scores, k, 1, 0) * scale).astype(BF16))
            grads[1].append((product(grad_scores, q, 0, 0) * scale).astype(BF16))
            grads[2].append(product(exact.astype(BF16), d, 0, 0).astype(BF16))
        for at, parts in zip(places, grads):
            out_ref[0, :, at] = jnp.concatenate(parts, 1)


def attend_back(project, mask, upstream, later_than=()):
    images, tokens, wide = project.shape
    width = wide // 3
    whole = pl.BlockSpec((1, tokens, wide), lambda i: (i, 0, 0))
    return run(
        attend_back_kernel,
        (project, mask[:, None, :], upstream),
        [
            whole,
            pl.BlockSpec((1, 1, tokens), lambda i: (i, 0, 0)),
            pl.BlockSpec((1, tokens, width), lambda i: (i, 0, 0)),
        ],
        48,
        later_than,
        grid=(images,),
        out_specs=whole,
        out_shape=jax.ShapeDtypeStruct(project.shape, BF16),
    )


def residual_kernel(feature_ref, branch_ref, gain_ref, out_ref, pooled_ref, rows):
    total = feature_ref[0].astype(F32) + gain_ref[0] * branch_ref[0].astype(F32)
    out_ref[0] = total.astype(BF16)
    groups = total.shape[0] // 4
    for group in range(groups):
        for part in range(3):
            fine = 4 * group + part
            rows[3 * group + part] = 0.5 * (total[fine] + total[fine + 1])
    columns = [rows[:, pl.ds(part, groups, stride=4), :] for part in range(4)]
    for part in range(3):
        pooled_ref[0, :, pl.ds(part, groups, stride=3), :] = 0.5 * (columns[part] + columns[part + 1])


def residual_and_pool(feature, branch, gain, later_than=()):
    images, fine, _, channels = feature.shape
    coarse = fine // 4 * 3
    block = pl.BlockSpec((1, fine, fine, LANES), lambda n, c: (n, 0, 0, c))
    out, pooled = run(
        residual_kernel,
        (feature, branch, gain[None]),
        [block, block, pl.BlockSpec((1, LANES), lambda n, c: (0, c))],
        32,
        later_than,
        grid=(images, channels // LANES),
        out_specs=[block, pl.BlockSpec((1, coarse, coarse, LANES), lambda n, c: (n, 0, 0, c))],
        out_shape=[
            jax.ShapeDtypeStruct(feature.shape, BF16),
            jax.ShapeDtypeStruct((images, coarse, coarse, channels), F32),
        ],
        scratch_shapes=[pltpu.VMEM((coarse, fine, LANES), F32)],
    )
    return (out, pooled.astype(BF16))


def spread_back_kernel(pooled_ref, upstream_ref, gain_ref, out_ref, scaled_ref, rows):
    groups = upstream_ref.shape[1] // 4
    columns = [pooled_ref[0, :, pl.ds(part, groups, stride=3), :] for part in range(3)]
    for part in range(4):
        near = [columns[at] for at in (part - 1, part) if 0 <= at < 3]
        rows[:, pl.ds(part, groups, stride=4), :] = 0.5 * sum(near[1:], near[0])
    for group in range(groups):
        for part in range(4):
            near = [rows[3 * group + at] for at in (part - 1, part) if 0 <= at < 3]
            total = upstream_ref[0, 4 * group + part].astype(F32) + 0.5 * sum(near[1:], near[0])
            out_ref[0, 4 * group + part] = total
            scaled_ref[0, 4 * group + part] = (gain_ref[0] * total).astype(BF16)


def spread_back(pooled, upstream, gain, later_than=()):
    images, fine, _, channels = upstream.shape
    coarse = pooled.shape[1]
    block = pl.BlockSpec((1, fine, fine, LANES), lambda n, c: (n, 0, 0, c))
    return run(
        spread_back_kernel,
        (pooled, upstream, gain[None]),
        [
            pl.BlockSpec((1, coarse, coarse, LANES), lambda n, c: (n, 0, 0, c)),
            block,
            pl.BlockSpec((1, LANES), lambda n, c: (0, c)),
        ],
        32,
        later_than,
        grid=(images, channels // LANES),
        out_specs=[block, block],
        out_shape=[
            jax.ShapeDtypeStruct(upstream.shape, F32),
            jax.ShapeDtypeStruct(upstream.shape, BF16),
        ],
        scratch_shapes=[pltpu.VMEM((coarse, fine, LANES), F32)],
    )


def add_kernel(kept_ref, got_ref, out_ref):
    out_ref[...] = (kept_ref[...].astype(F32) + got_ref[...].astype(F32)).astype(BF16)


def add_to_first_half(partial, got, later_than=()):
    rows, width = got.shape
    tile = math.gcd(rows, 256)
    if tile % 16:
        return (partial[:rows].astype(F32) + got.astype(F32)).astype(BF16)
    block = pl.BlockSpec((tile, width), lambda i: (i, 0))
    return run(
        add_kernel,
        (partial, got),
        [block, block],
        32,
        later_than,
        grid=(rows // tile,),
        out_specs=block,
        out_shape=jax.ShapeDtypeStruct(got.shape, BF16),
    )


class Held:
    def __init__(self, **arrays):
        self.add(**arrays)

    def add(self, **arrays):
        vars(self).update(arrays)


def traded(array, axis, bit):
    return lax.ppermute(array, axis, [(i, i ^ bit) for i in range(lax.axis_size(axis))])


def bits_of(axis):
    return [1 << k for k in range((lax.axis_size(axis) - 1).bit_length())]


def total_over(values, axis):
    for bit in bits_of(axis):
        values = values + traded(values, axis, bit)
    return values


def first_section():
    return lax.axis_index(PIPE) == 0


def select(former, latter):
    return jnp.where(first_section(), former, latter)


def halves_of(own, axis):
    half = own.shape[axis] // 2
    odd = lax.axis_index(DP) % 2
    return lax.dynamic_slice_in_dim(own, odd * half, half, axis)


def joined(mine, theirs, axis):
    even = lax.axis_index(DP) % 2 == 0
    return jnp.concatenate([jnp.where(even, mine, theirs), jnp.where(even, theirs, mine)], axis)


class Trade:
    def __init__(self, own, *earlier):
        self.own = own
        self.got = traded(after(halves_of(own, 0), *earlier), PIPE, 1)

    def share(self, *earlier):
        self.got = after(self.got, *earlier)
        self.rest = traded(self.got, DP, 1)

    def layers(self, *earlier):
        rest = after(self.rest, *earlier) if earlier else self.rest
        other = joined(self.got, rest, 0)
        return (select(self.own, other), select(other, self.own))


class QuarterTrade:
    def __init__(self, own, *earlier):
        size = own.shape[0] // QUARTERS
        sent = lax.dynamic_slice_in_dim(own, lax.axis_index(DP) % QUARTERS * size, size, 0)
        self.own = own
        self.got = traded(after(sent, *earlier), PIPE, 1)

    def share(self, *earlier):
        self.got = after(self.got, *earlier)
        self.pair = traded(self.got, DP, 2)

    def share_again(self, *earlier):
        self.pair = after(self.pair, *earlier)
        self.rest = traded(jnp.concatenate([self.got, self.pair], 0), DP, 1)

    def pieces(self):
        return (self.own, self.got, self.pair, self.rest)


def small_pair(own):
    other = traded(own, PIPE, 1)
    return (select(own, other), select(other, own))


def own_block(values, count, axis):
    return lax.dynamic_slice_in_dim(values, lax.axis_index(TENSOR) * count, count, axis)


def widen(values, whole, axis):
    shape = list(values.shape)
    shape[axis] = whole
    empty = jnp.zeros(tuple(shape), F32)
    return lax.dynamic_update_slice_in_dim(
        empty, values, lax.axis_index(TENSOR) * values.shape[axis], axis
    )


def gather(values):
    return lax.all_gather(values, TENSOR, axis=1, tiled=True)


def turned(values, by):
    count = lax.axis_size(TENSOR)
    return lax.ppermute(values, TENSOR, [(i, (i + by) % count) for i in range(count)])


def ring_total(values):
    count = lax.axis_size(TENSOR)
    return sum([turned(values, k) for k in range(1, count)], values)


def in_order(blocks, axis):
    count = len(blocks)
    size = blocks[0].shape[axis]
    start = (count - 1 - lax.axis_index(TENSOR)) * size
    joined = jnp.concatenate(blocks[::-1] + blocks[:0:-1], axis)
    return lax.dynamic_slice_in_dim(joined, start, count * size, axis)


def exchanged(values, split_axis, concat_axis):
    count = lax.axis_size(TENSOR)
    index = lax.axis_index(TENSOR)
    size = values.shape[split_axis] // count
    blocks = []
    for k in range(count):
        start = (index + k) % count * size
        block = lax.dynamic_slice_in_dim(values, start, size, split_axis)
        blocks.append(turned(block, k) if k else block)
    return in_order(blocks, concat_axis)


def ring_gather(values):
    blocks = [turned(values, k) if k else values for k in range(lax.axis_size(TENSOR))]
    return in_order(blocks, 1)


def tokens_to_holders(values):
    return exchanged(values, 1, 2)


def features_to_holders(values):
    return exchanged(values, 2, 1)


def scatter_tokens(values):
    return lax.psum_scatter(values, TENSOR, scatter_dimension=1, tiled=True).astype(F32)


def scatter_parts(parts):
    return lax.psum_scatter(parts, TENSOR, scatter_dimension=0, tiled=False).astype(F32)


def relative_order(count):
    width = (count - 1).bit_length()
    return sorted(range(count), key=lambda r: format(r, f"0{width}b")[::-1])


def by_relative(values, axis=DP):
    count = lax.axis_size(axis)
    index = lax.axis_index(axis)
    block = values.shape[1] // count
    return jnp.concatenate(
        [
            lax.dynamic_slice_in_dim(values, (index ^ r) * block, block, 1)
            for r in relative_order(count)
        ],
        1,
    )


def inner(left, right, *earlier):
    left = by_relative(left)
    if earlier:
        left = after(left, *earlier)
    return product(left, right, 0, 0).astype(BF16)


class Reduction:
    def __init__(self, partial, also_tensor=False):
        self.partial = partial
        self.steps_left = 4 if also_tensor else 2
        self.moves = [(DP, bit, 0) for bit in bits_of(DP)]
        if also_tensor:
            self.moves += [(TENSOR, bit, 1) for bit in bits_of(TENSOR)]
        self.send()

    def send(self):
        name, bit, axis = self.moves.pop(0)
        size = self.partial.shape[axis] // 2
        self.got = traded(lax.slice_in_dim(self.partial, size, 2 * size, axis=axis), name, bit)

    def step(self, *earlier):
        halvings = -(-(len(self.moves) + 1) // self.steps_left)
        self.steps_left -= 1
        for _ in range(halvings):
            self.partial = add_to_first_half(self.partial, self.got, earlier)
            if self.moves:
                self.send()
        return self.partial


class Sections:
    def __init__(self, former, latter):
        self.kept = select(former, latter)
        self.got = traded(select(latter, former), PIPE, 1)

    def total(self, *earlier):
        got = after(self.got, *earlier) if earlier else self.got
        return self.kept.astype(F32) + got.astype(F32)


def over_sections(former, latter):
    kept, sent = (select(former, latter), select(latter, former))
    return kept.astype(F32) + traded(sent, PIPE, 1).astype(F32)


def norm_rows(values, epsilon):
    centred = values - jnp.mean(values, -1, keepdims=True)
    inverse = lax.rsqrt(jnp.mean(centred * centred, -1, keepdims=True) + epsilon)
    return (centred * inverse, inverse)


def norm_back(upstream, scaled, inverse, gains):
    weighted = upstream * gains
    return inverse * (
        weighted
        - jnp.mean(weighted, -1, keepdims=True)
        - scaled * jnp.mean(weighted * scaled, -1, keepdims=True)
    )


def flat(values):
    return values.reshape(-1, values.shape[-1])


def placing(places):
    cells = jnp.arange(places.shape[1])
    return (places[:, :, None] == cells[None, None, :]).astype(BF16)


def conv_norm(grid, w, later_than=()):
    own = grid.shape[-1]
    channels = own * lax.axis_size(TENSOR)
    mixed = flat(depthwise(grid, w.dw, 7, later_than=later_than))
    sums = ring_total(jnp.stack([jnp.sum(mixed, -1), jnp.sum(mixed * mixed, -1)]))
    centre = sums[0] / channels
    inverse = lax.rsqrt(sums[1] / channels - centre * centre + 1e-06)
    scaled = (mixed - centre[:, None]) * inverse[:, None]
    normed = (scaled * w.gain[0] + w.shift).astype(BF16)
    return (normed, Held(grid=grid, scaled=scaled, inverse=inverse))


def conv_residual(grid, branch, w, *earlier):
    own = grid.shape[-1]
    channels = own * lax.axis_size(TENSOR)
    out, pooled = residual_and_pool(grid, branch.reshape(grid.shape), w.gain[1], earlier)
    exact = grid.astype(F32) + w.gain[1] * branch.reshape(grid.shape).astype(F32)
    square = jnp.sum(exact * exact, -1).reshape(grid.shape[0], -1)
    return (out, flat(pooled), square / channels)


def adapter_forward(stream, pooled, places, w, *earlier):
    images, tokens, _ = places.shape
    side = math.isqrt(tokens)
    pooled_rows = tokens_to_holders(pooled.reshape(images, tokens, -1))
    adapted_rows = product(flat(pooled_rows), w.proj, 1, 0).astype(BF16)
    adapted = features_to_holders(adapted_rows.reshape(pooled_rows.shape[:2] + (-1,)))
    adapted = adapted.reshape(images, side, side, -1)
    spread = depthwise(adapted, w.taps, 3, later_than=earlier).reshape(images, tokens, -1)
    gated = (jnp.tanh(w.gate) * spread).astype(BF16)
    picked = jnp.einsum("ntc,ncw->ntw", places, gated, preferred_element_type=F32).astype(BF16)
    stream_in = stream + tokens_to_holders(picked).astype(F32)
    return (stream_in, Held(pooled=flat(pooled_rows), adapted=adapted, spread=spread))


def vit_norm(stream, w, which):
    scaled, inverse = norm_rows(stream, 1e-05)
    normed = (scaled * w.vit_gain[which] + w.vit_shift[which]).astype(BF16)
    return (normed, scaled, inverse)


def vit_attention(normed, key_mask, w, *earlier):
    images, tokens, width = normed.shape
    project = product(flat(normed), w.qkv, 1, 0).astype(BF16).reshape(images, tokens, -1)
    attended = attend(project, key_mask, earlier)
    held = tokens_to_holders(attended)
    return (project, flat(held), product(flat(held), w.attn, 1, 0).reshape(held.shape))


def vit_attention_back(grad_own, kept, key_mask, w, *earlier):
    images, _, width = grad_own.shape
    grad_attended = product(flat(grad_own), w.attn, 1, 1).astype(BF16)
    grad_attended = features_to_holders(grad_attended.reshape(grad_own.shape))
    grad_project = flat(attend_back(kept.project, key_mask, grad_attended, earlier))
    partial = product(grad_project, w.qkv, 1, 1).astype(BF16)
    return (grad_project, partial.reshape(images, -1, width))


def adapter_backward(grad_cols, kept, places, w, later_than=()):
    images, tokens, _ = places.shape
    side = math.isqrt(tokens)
    grad_placed = jnp.einsum("ntc,ntw->ncw", places, grad_cols, preferred_element_type=F32)
    gate_value = jnp.tanh(w.gate)
    gate = jnp.sum(grad_placed * kept.spread, (0, 1)) * (1.0 - gate_value * gate_value)
    grad_spread = (grad_placed * gate_value).reshape(images, side, side, -1)
    grad_adapted = flat(
        depthwise(
            grad_spread, w.taps, 3, reverse=True, dtype=BF16, later_than=later_than
        )
    )
    grad_rows = tokens_to_holders(grad_adapted.reshape(images, tokens, -1))
    grad_pooled = product(flat(grad_rows), w.proj, 1, 1).astype(BF16)
    grad_pooled = features_to_holders(grad_pooled.reshape(grad_rows.shape[:2] + (-1,)))
    taps = depthwise_taps(kept.adapted, grad_spread, 3, later_than=(grad_adapted,))
    grad_pooled = grad_pooled.astype(F32).reshape(images, side, side, -1)
    return (flat(grad_rows), grad_pooled, taps, gate)


def conv_norm_back(grad_normed, kept, w):
    grid = kept.grid
    channels = grid.shape[-1] * lax.axis_size(TENSOR)
    scaled = kept.scaled
    weighted = grad_normed * w.gain[0]
    sums = ring_total(jnp.stack([jnp.sum(weighted, -1), jnp.sum(weighted * scaled, -1)]))
    grad_mixed = kept.inverse[:, None] * (
        weighted - sums[0][:, None] / channels - scaled * (sums[1][:, None] / channels)
    )
    gain = jnp.sum(grad_normed * scaled, 0)
    shift = jnp.sum(grad_normed, 0)
    return (grad_mixed.reshape(grid.shape), gain, shift)


def body(
    x_vit,
    x_conv,
    positions,
    valid,
    qkv_weight,
    attn_weight,
    fc_in,
    fc_out,
    vit_gains,
    vit_shifts,
    pw_in,
    pw_out,
    dw_kernel,
    conv_gains,
    conv_shift,
    proj_weight,
    taps,
    gate,
    dy_vit,
    dy_conv,
):
    here = x_vit.shape[0] // lax.axis_size(PIPE)
    count = lax.axis_size(TENSOR)
    cells = x_conv.shape[1]
    own_channels = x_conv.shape[2]
    conv_side = math.isqrt(cells)
    own_width = attn_weight.shape[1]
    own_units = fc_out.shape[1]
    conv_units = pw_out.shape[1]
    channels = pw_out.shape[2]
    model_width = vit_gains.shape[2]
    tap_count = dw_kernel.shape[1]
    side = taps.shape[1]
    tile = cells // 2

    def portion(source):
        return lax.dynamic_slice_in_dim(source, lax.axis_index(PIPE) * here, here, 0)

    conv_small = small_pair(jnp.concatenate([dw_kernel[0], conv_gains[0], conv_shift], 0))
    trade_in = QuarterTrade(pw_in[0], conv_small[0])
    vit_small = small_pair(
        after(jnp.concatenate([taps[0], gate, vit_gains[0], vit_shifts[0]], 0), conv_small[0])
    )
    weights = [Held(), Held()]
    for layer in range(2):
        conv, vit = (conv_small[layer], vit_small[layer])
        weights[layer].add(
            dw=conv[:tap_count],
            gain=conv[tap_count : tap_count + 2],
            shift=conv[tap_count + 2],
            taps=own_block(vit[:side], own_width, 1),
            gate=own_block(vit[side], own_width, 0),
            vit_gain=vit[side + 1 : side + 3],
            vit_shift=vit[side + 3 :],
        )
    w0, w1 = weights

    def take(**pairs):
        for name, pair in pairs.items():
            for w, weight in zip(weights, pair):
                w.add(**{name: weight})

    def both_images(former, latter, *earlier):
        mine, theirs = (select(former, latter), select(latter, former))
        sent = theirs.astype(BF16) if theirs.ndim > 3 else theirs
        if earlier:
            sent = after(sent, *earlier)
        got = traded(sent, PIPE, 1).astype(mine.dtype)
        return jnp.concatenate([select(mine, got), select(got, mine)], 0)

    stream = portion(x_vit)
    grid0 = portion(x_conv).reshape(here, conv_side, conv_side, own_channels)
    grad_top = portion(dy_vit)
    grad_top_full = gather(grad_top)
    attn_half = lax.all_gather(halves_of(attn_weight[0], 1), TENSOR, axis=0, tiled=True)
    places = placing(portion(positions))
    key_mask = portion(valid)

    normed0, conv0 = conv_norm(grid0, w0)
    conv0.normed = gather(after(normed0, grad_top_full, attn_half))
    trade_in.share(normed0)
    trade_out = QuarterTrade(pw_out[0], trade_in.got)
    trade_in.share_again()
    first = trade_in.pieces()
    trade_out.share(trade_in.pair)
    trade_proj = Trade(proj_weight[0], trade_out.got)
    trade_out.share_again(trade_proj.got)
    second = trade_out.pieces()
    (conv0.hidden, conv0.slope), parts = wide_mlp(0, conv0.normed, first, second, tile)
    branch = scatter_parts(parts)
    conv0.branch = branch
    trade_proj.share(parts)
    trade_qkv = Trade(qkv_weight[0].reshape(model_width, -1), parts)
    trade_fc_in = Trade(fc_in[0], parts)
    grid1, pooled0, square0 = conv_residual(
        grid0, branch, w0, trade_qkv.got, trade_fc_in.got
    )
    trade_fc_out = Trade(fc_out[0], pooled0)
    take(proj=trade_proj.layers())
    trade_qkv.share(pooled0)

    normed1, conv1 = conv_norm(grid1, w1, (pooled0,))
    conv1.normed = gather(normed1)
    take(qkv=trade_qkv.layers(normed1))
    stream_in0, vit0 = adapter_forward(stream.astype(F32), pooled0, places, w0, normed1, w0.qkv)
    normed_a0, vit0.scaled_a, vit0.inverse_a = vit_norm(stream_in0, w0, 0)
    vit0.normed_a = gather(normed_a0)
    trade_fc_in.share(normed_a0)
    trade_fc_out.share(normed_a0)
    (conv1.hidden, conv1.slope), parts = wide_mlp(
        1, conv1.normed, first, second, tile, None, (normed_a0, trade_fc_out.got)
    )
    branch = scatter_parts(parts)
    conv1.branch = branch
    attn_got = traded(after(attn_half, parts), PIPE, 1)
    attn_halves = jnp.stack([attn_half, attn_got])
    attn_rest = traded(attn_halves, DP, 1)
    attn_full = [joined(mine, theirs, 1) for mine, theirs in zip(attn_halves, attn_rest)]
    take(attn=(select(*attn_full), select(*attn_full[::-1])))
    take(fc_in=trade_fc_in.layers(parts))
    take(fc_out=trade_fc_out.layers(parts))
    vit0.project, vit0.attended, moved = vit_attention(
        vit0.normed_a, key_mask, w0, parts
    )
    stream_mid0 = stream_in0 + moved
    normed_b0, vit0.scaled_b, vit0.inverse_b = vit_norm(stream_mid0, w0, 1)
    vit0.normed_b = gather(normed_b0)
    grid2, pooled1, square1 = conv_residual(grid1, branch, w1)
    vit0.hidden, vit0.slope, partial = mlp(
        flat(vit0.normed_b), w0.fc_in, w0.fc_out, (pooled1,)
    )
    stream_out0 = stream_mid0 + scatter_tokens(partial.reshape(stream_shape(vit0)))
    stream1 = stream_out0.astype(BF16)

    stream_in1, vit1 = adapter_forward(stream1.astype(F32), pooled1, places, w1, partial)
    normed_a1, vit1.scaled_a, vit1.inverse_a = vit_norm(stream_in1, w1, 0)
    vit1.normed_a = gather(normed_a1)
    vit1.project, vit1.attended, moved = vit_attention(vit1.normed_a, key_mask, w1)
    stream_mid1 = stream_in1 + moved
    out_conv = both_images(grid1, grid2, normed_a1).reshape(1, -1, cells, own_channels)
    normed_b1, vit1.scaled_b, vit1.inverse_b = vit_norm(stream_mid1, w1, 1)
    vit1.normed_b = gather(normed_b1)
    vit1.hidden, vit1.slope, top_partial = mlp(
        flat(vit1.normed_b), w1.fc_in, w1.fc_out, (out_conv,)
    )

    norm_sums = [None, None]
    tap_sums = [None, None]

    def back_to_middle(grad_out, grad_full, kept, w, beside, *earlier):
        grad_hidden, partial = mlp_back(
            flat(grad_full), kept.slope, w.fc_in, w.fc_out, earlier
        )
        grad_normed = scatter_tokens(partial.reshape(stream_shape(kept)))
        packed = jnp.concatenate(
            [
                inner(flat(kept.normed_b), grad_hidden, partial),
                inner(flat(grad_full), kept.hidden, partial),
            ],
            1,
        )
        grad_normed = after(grad_normed, packed, *beside(partial))
        sums = [jnp.sum(grad_normed * kept.scaled_b, (0, 1)), jnp.sum(grad_normed, (0, 1))]
        grad_mid = grad_out.astype(F32) + norm_back(
            grad_normed, kept.scaled_b, kept.inverse_b, w.vit_gain[1]
        )
        return (grad_mid, Reduction(packed), sums)

    def back_to_start(grad_mid, grad_own, kept, w, beside, *earlier):
        grad_project, partial = vit_attention_back(grad_own, kept, key_mask, w, *earlier)
        grad_normed = scatter_tokens(partial)
        qkv = inner(flat(kept.normed_a), grad_project, partial)
        grad_normed = after(grad_normed, qkv, *beside(partial))
        sums = [jnp.sum(grad_normed * kept.scaled_a, (0, 1)), jnp.sum(grad_normed, (0, 1))]
        grad_in = grad_mid + norm_back(
            grad_normed, kept.scaled_a, kept.inverse_a, w.vit_gain[0]
        )
        return (grad_in, qkv, sums)

    def row_grads(kept, grad_rows, grad_own, *earlier):
        sides = lax.axis_size(DP)
        pairs = [
            product(by_relative(left), after(right, *earlier), 0, 0)
            for left, right in ((kept.pooled, grad_rows), (flat(grad_own), kept.attended))
        ]
        blocks = [pair.astype(BF16).reshape(sides, -1, model_width) for pair in pairs]
        return jnp.concatenate(blocks, 1).reshape(-1, model_width)

    def step_all(reductions, *earlier):
        return [reduction.step(*earlier) for reduction in reductions]

    grad_mid1, mlp1, sums_b1 = back_to_middle(
        grad_top, grad_top_full, vit1, w1, lambda partial: (), top_partial
    )
    grad_mid1_own = grad_mid1.astype(BF16)

    def beside_start1(partial):
        mlp1.step(partial)
        return [mlp1.step(partial)]

    grad_in1, qkv1, sums_a1 = back_to_start(grad_mid1, grad_mid1_own, vit1, w1, beside_start1)
    norm_sums[1] = jnp.stack([sums_a1[0], sums_b1[0], sums_a1[1], sums_b1[1]])
    grad_stream = grad_in1.astype(BF16)
    grad_stream_full = gather(grad_stream)
    grad_rows1, grad_pooled1, tap_sum, gate_sum = adapter_backward(
        features_to_holders(grad_stream), vit1, places, w1
    )
    tap_sums[1] = jnp.concatenate([tap_sum, gate_sum[None]], 0)

    squares = total_over(both_images(square0, square1, grad_mid1_own), TENSOR)
    rms_conv = jnp.sqrt(squares)[None]
    grad_map1, scaled1 = spread_back(
        grad_pooled1, portion(dy_conv).reshape(grid0.shape), w1.gain[1], (rms_conv,)
    )
    grad_branch1 = gather(flat(scaled1))
    grad_mid0, mlp0, sums_b0 = back_to_middle(
        grad_stream, grad_stream_full, vit0, w0, lambda partial: (), scaled1
    )
    rows1 = Reduction(row_grads(vit1, grad_rows1, grad_mid1_own, scaled1))
    grad_mid0_own = grad_mid0.astype(BF16)
    rows1.step(grad_mid0_own)
    grad_in0, qkv0, sums_a0 = back_to_start(
        grad_mid0, grad_mid0_own, vit0, w0, lambda partial: ()
    )
    (grad_hidden1,), parts = wide_mlp(
        1, grad_branch1, first, second, tile, conv1.slope, (grad_mid0_own, rows1.partial)
    )
    grad_normed1 = scatter_parts(parts)
    conv_in1 = Reduction(inner(conv1.normed, grad_hidden1, parts))
    conv_out1 = Reduction(inner(grad_branch1, conv1.hidden, parts))
    norm_sums[0] = jnp.stack([sums_a0[0], sums_b0[0], sums_a0[1], sums_b0[1]])
    grad_last = grad_in0.astype(BF16)
    qkv = Reduction(jnp.concatenate([qkv0, qkv1], 1))
    grad_mixed1, gain1, shift1 = conv_norm_back(grad_normed1, conv1, w1)
    mlp0.step(grad_last)
    rows1.step(grad_last)
    qkv.step(grad_last)
    grad_rows0, grad_pooled0, tap_sum, gate_sum = adapter_backward(
        features_to_holders(grad_last), vit0, places, w0, (conv_in1.partial, conv_out1.partial)
    )
    tap_sums[0] = jnp.concatenate([tap_sum, gate_sum[None]], 0)
    ready = step_all([conv_out1, conv_in1], conv_in1.partial, conv_out1.partial)
    grad_grid1 = depthwise(
        grad_mixed1, w1.dw, 7, grad_map1, True, F32, ready + [rows1.partial]
    )
    grad_next = grad_grid1.astype(BF16)

    ready = step_all([mlp0, qkv, conv_out1], grad_grid1)
    grad_map0, scaled0 = spread_back(grad_pooled0, grad_next, w0.gain[1], ready)
    grad_branch0 = gather(flat(scaled0))
    fc = Sections(after(mlp0.partial, scaled0), mlp1.partial)
    half = qkv.partial.shape[1] // 2
    sections_qkv = Sections(after(qkv.partial[:, :half], scaled0), qkv.partial[:, half:])
    rows0 = Reduction(row_grads(vit0, grad_rows0, grad_mid0_own, scaled0))
    grad_vit = both_images(grad_in0[None], grad_in1[None], scaled0)
    grad_vit = grad_vit.reshape((1, -1) + grad_in0.shape[1:])
    taps1 = depthwise_taps(conv1.grid, grad_mixed1, 7, later_than=(scaled0,))
    ready = step_all([conv_in1], taps1)
    rows0.step(*ready)
    (grad_hidden0,), parts = wide_mlp(
        0,
        grad_branch0,
        first,
        second,
        tile,
        conv0.slope,
        ready + [rows0.partial, fc.got, sections_qkv.got, grad_vit],
    )
    grad_normed0 = scatter_parts(parts)
    rows0.step(parts)
    conv_out0 = Reduction(inner(grad_branch0, conv0.hidden, rows0.partial))
    conv_in0 = Reduction(inner(conv0.normed, grad_hidden0, conv_out0.partial))
    conv_out0.step(conv_in0.partial)
    conv_in0.step(conv_out0.partial)
    conv_out0.step(conv_in0.partial)
    grad_normed0 = after(grad_normed0, conv_out0.partial)
    row_parts = jnp.concatenate([rows0.partial, rows1.partial], 0)
    row_parts = row_parts.reshape(row_parts.shape[0], count, -1).swapaxes(0, 1)
    row_sums = lax.psum_scatter(
        after(row_parts, grad_normed0), TENSOR, scatter_dimension=0, tiled=False
    )
    grad_mixed0, gain0, shift0 = conv_norm_back(grad_normed0, conv0, w0)
    conv_in0.step(conv_out0.partial)
    grad_grid0 = depthwise(
        grad_mixed0, w0.dw, 7, grad_map0, True, F32, (conv_in0.partial,)
    )
    conv_out = Sections(conv_out0.partial, conv_out1.partial)
    grad_conv = both_images(grad_grid0, grad_grid1)
    conv_in = Sections(conv_in0.partial, conv_in1.partial)
    taps0 = depthwise_taps(conv0.grid, grad_mixed0, 7, later_than=(grad_grid0,))
    stream_out1 = stream_mid1 + scatter_tokens(
        after(top_partial, row_sums).reshape(stream_shape(vit1))
    )
    grad_fc = fc.total(taps0)
    grad_qkv = sections_qkv.total(taps0)
    grad_conv_out = conv_out.total(taps0)
    row_blocks = jnp.split(row_sums, 2, 0)
    grad_proj_attn = over_sections(after(row_blocks[0], taps0), row_blocks[1])
    grad_conv_in = conv_in.total(taps0)
    proj_rows = channels // lax.axis_size(DP)
    scale1 = jnp.sum(flat(grad_map1) * conv1.branch, 0)
    scale0 = jnp.sum(flat(grad_map0) * conv0.branch, 0)

    def over_images(pair):
        return total_over(select(*pair) + traded(select(*pair[::-1]), PIPE, 1), DP)

    token_terms = [
        jnp.concatenate(
            [
                widen(after(tap_sums[layer], scaled0), model_width, 1),
                after(norm_sums[layer], scaled0),
            ],
            0,
        )
        for layer in range(2)
    ]
    token_terms = total_over(jnp.concatenate(token_terms, 0), TENSOR)

    def rows_of_lanes(values):
        return values.reshape(-1, LANES)

    column_terms = [
        jnp.concatenate([taps0, jnp.stack([gain0, scale0, shift0])], 0),
        jnp.concatenate([taps1, jnp.stack([gain1, scale1, shift1])], 0),
    ]
    token_rows = side + 5
    column_sums, token_sums = jnp.split(
        over_images(
            [
                jnp.concatenate(
                    [
                        rows_of_lanes(columns),
                        rows_of_lanes(token_terms[layer * token_rows : (layer + 1) * token_rows]),
                    ],
                    0,
                )
                for layer, columns in enumerate(column_terms)
            ]
        ),
        [column_terms[0].size // LANES],
    )
    column_sums = column_sums.reshape(column_terms[0].shape)
    token_sums = token_sums.reshape(token_rows, model_width)

    out_vit = both_images(stream1, stream_out1.astype(BF16))[None]
    mean_squares = [jnp.mean(out * out, -1) for out in (stream_out0, stream_out1)]
    rms_vit = jnp.sqrt(both_images(*mean_squares))[None]
    return (
        out_vit,
        out_conv,
        grad_vit,
        grad_conv.reshape(1, -1, cells, own_channels),
        rms_vit,
        rms_conv,
        grad_qkv.reshape(1, -1, 3, own_width),
        grad_proj_attn[proj_rows:].T[None],
        grad_fc[:, :own_units][None],
        grad_fc[:, own_units:].T[None],
        token_sums[side + 1 : side + 3][None],
        token_sums[side + 3 :][None],
        grad_conv_in[None],
        grad_conv_out.T[None],
        column_sums[:tap_count][None],
        column_sums[tap_count : tap_count + 2][None],
        column_sums[tap_count + 2 :],
        grad_proj_attn[:proj_rows][None],
        token_sums[:side][None],
        token_sums[side][None],
    )


def stream_shape(kept):
    return kept.normed_b.shape


def solution(mesh):
    return jax.shard_map(
        body,
        mesh=mesh,
        in_specs=(
            P(DP, TENSOR, None),
            P(DP, None, TENSOR),
            P(DP, None),
            P(DP, None),
            P(PIPE, None, None, TENSOR),
            P(PIPE, TENSOR, None),
            P(PIPE, None, TENSOR),
            P(PIPE, TENSOR, None),
            P(PIPE, None, None),
            P(PIPE, None, None),
            P(PIPE, None, TENSOR),
            P(PIPE, TENSOR, None),
            P(PIPE, None, TENSOR),
            P(PIPE, None, TENSOR),
            P(PIPE, TENSOR),
            P(PIPE, None, None),
            P(PIPE, None, None),
            P(PIPE, None),
            P(DP, TENSOR, None),
            P(DP, None, TENSOR),
        ),
        out_specs=(
            P(PIPE, DP, TENSOR, None),
            P(PIPE, DP, None, TENSOR),
            P(PIPE, DP, TENSOR, None),
            P(PIPE, DP, None, TENSOR),
            P(PIPE, DP, TENSOR),
            P(PIPE, DP, None),
            P(PIPE, DP, None, TENSOR),
            P(PIPE, TENSOR, DP),
            P(PIPE, DP, TENSOR),
            P(PIPE, TENSOR, DP),
            P(PIPE, None, None),
            P(PIPE, None, None),
            P(PIPE, DP, TENSOR),
            P(PIPE, TENSOR, DP),
            P(PIPE, None, TENSOR),
            P(PIPE, None, TENSOR),
            P(PIPE, TENSOR),
            P(PIPE, DP, TENSOR),
            P(PIPE, None, None),
            P(PIPE, None),
        ),
        check_vma=False,
    )
```
